128 devices in a mesh: px: 8 (over y, z_hi), py: 16 (over z_lo, x, core).
Axes of the slice: x: 4, y: 4, z: 4 (z_hi: 2, z_lo: 2; z = z_hi * 2 + z_lo), core: 2. Of those that a mesh axis runs over, the one named last changes fastest.
Arguments:
- flow_field: bfloat16 [640, 1280, 128], P('px', 'py'), may hold values from -6 to 6
- cotangent: bfloat16 [640, 1280, 128], P('px', 'py'), may hold values from -6 to 6
- spec_weight: float32 [2, 64, 64, 128, 128], P(None, 'px', 'py'), may hold values from -0.375 to 0.375
- skip_weight: bfloat16 [128, 128], replicated, may hold values from -0.5 to 0.5
- ctx_weight: bfloat16 [8, 128, 128], replicated, may hold values from -0.1875 to 0.1875
- up_weight: bfloat16 [128, 512], replicated, may hold values from -0.5 to 0.5
- down_weight: bfloat16 [512, 128], replicated, may hold values from -0.25 to 0.25
- ctx_level: int32 [128, 8], replicated, may hold values from 0 to 2
- ctx_offset: int32 [128, 8, 2], replicated, may hold values from 0 to 60
Outputs:
- layer_output: bfloat16 [640, 1280, 128], P('px', 'py')
- grad_field: bfloat16 [640, 1280, 128], P('px', 'py')
- grad_spec: float32 [2, 64, 64, 128, 128], P(None, 'px', 'py')
- grad_skip: float32 [128, 128], replicated
- grad_ctx: float32 [8, 128, 128], replicated
- grad_up: float32 [128, 512], replicated
- grad_down: float32 [512, 128], replicated
The draws below stay inside these ranges and needn't reach their ends.
Inputs may be any that keep to these rules, and one draw needn't show every extreme that they name: `ctx_level`: levels name 0, 1 or 2.
All inputs are finite; a program needn't handle non-finite values.
Results may differ from the reference program's by a relative error of at most 0.0075.
Values may be sent and summed in bfloat16 or wider, within the bound.
A program may use at most 256 MiB of HBM per device.

```python
import math
import jax
import jax.numpy as jnp
from jax import lax

P_SIZE = 80
C = 128
H = 512
MX = 64
MY = 64
BLK = 20
PATCH_ROWS = 8
PATCH_COLS = 16
NPATCH = 128
NX = 640
NY = 1280


def place_ends(entries, rng, low, high):
    longest = entries.shape.index(max(entries.shape))
    spots = []
    for shift in (0, 1):
        where = [jax.random.randint(jax.random.fold_in(rng, axis), (), 0, length) for axis, length in enumerate(entries.shape)]
        where[longest] = (where[longest] + shift) % entries.shape[longest]
        spots.append(tuple(where))
    return entries.at[spots[0]].set(low).at[spots[1]].set(high)


def block_scale(own_key, dims, cuts, low, largest):
    loudness, own = 1.0, jax.random.fold_in(own_key, 6)
    for position, blocks in cuts:
        draws = jnp.exp(jax.random.uniform(jax.random.fold_in(own, position), (blocks,), jnp.float32, low / len(cuts), largest / len(cuts)))
        loudness = loudness * jnp.repeat(draws, dims[position] // blocks).reshape([-1 if axis == position else 1 for axis in range(len(dims))])
    return loudness


def bell_draw(own_key, extent, deviation, most, cuts=(), kind=jnp.bfloat16):
    values = jax.random.normal(own_key, extent, jnp.float32) * deviation
    if len(cuts) > 0:
        values = block_scale(own_key, extent, cuts, -0.22, 0.18) * values
    return jnp.clip(values, min=-most, max=most).astype(kind)


def setup_inputs(seed: int = 0) -> dict:
    streams_of = jax.random.split(jax.random.key(seed), 10)
    return {
        "flow_field": bell_draw(streams_of[0], (NX, NY, C), 1.0, 6.0, ((0, 8), (1, 16))),
        "cotangent": bell_draw(streams_of[1], (NX, NY, C), 1.0, 6.0, ((0, 8), (1, 16))),
        "spec_weight": bell_draw(streams_of[2], (2, MX, MY, C, C), (2 * C) ** -0.5, 0.375, ((1, 8), (2, 16)), jnp.float32),
        "skip_weight": bell_draw(streams_of[3], (C, C), C ** -0.5, 0.5),
        "ctx_weight": bell_draw(streams_of[4], (8, C, C), (8 * C) ** -0.5, 0.1875),
        "up_weight": bell_draw(streams_of[5], (C, H), C ** -0.5, 0.5),
        "down_weight": bell_draw(streams_of[6], (H, C), H ** -0.5, 0.25),
        "ctx_level": place_ends(jax.random.randint(streams_of[7], (NPATCH, 8), 0, 3), jax.random.fold_in(streams_of[7], 1), 0, 2).astype(jnp.int32),
        "ctx_offset": place_ends(jax.random.randint(streams_of[8], (NPATCH, 8, 2), 0, P_SIZE - BLK + 1), jax.random.fold_in(streams_of[8], 1), 0, P_SIZE - BLK).astype(jnp.int32),
    }


TANH_SCALE = 0.7978845608028654
CUBIC_TERM = 0.044715
HIGHEST = lax.Precision.HIGHEST
STEP_ROWS = (-1, -1, -1, 0, 0, 1, 1, 1)
STEP_COLS = (-1, 0, 1, -1, 1, -1, 0, 1)

def gelu_value(values):
    return 0.5 * values * (1.0 + jnp.tanh(TANH_SCALE * (values + CUBIC_TERM * values * values * values)))

def gelu_slope(values):
    tanh_part = jnp.tanh(TANH_SCALE * (values + CUBIC_TERM * values * values * values))
    return 0.5 * (1.0 + tanh_part) + 0.5 * values * (1.0 - tanh_part * tanh_part) * TANH_SCALE * (1.0 + 3.0 * CUBIC_TERM * values * values)

def angles(positions, wave_list, length):
    turn_count = jnp.mod(positions[:, None] * wave_list[None, :], length)
    phase_angle = turn_count.astype(jnp.float32) * (2.0 * math.pi / length)
    return (jnp.cos(phase_angle), jnp.sin(phase_angle))

def wave_numbers(number):
    return jnp.arange(number, dtype=jnp.int32) - number // 2

def cell_numbers(number):
    return jnp.arange(number, dtype=jnp.int32)

def forward_y(values, factor):
    cosine, sine_part = angles(cell_numbers(NY), wave_numbers(MY), NY)
    cos_table = lax.optimization_barrier((cosine / math.sqrt(NY)).astype(jnp.bfloat16)).astype(jnp.float32)
    sin_table = lax.optimization_barrier((-sine_part / math.sqrt(NY)).astype(jnp.bfloat16)).astype(jnp.float32)
    wide_values = values.astype(jnp.float32)
    real_part = jnp.einsum('xyc,yk->kxc', wide_values, cos_table, precision=HIGHEST)
    imag_part = jnp.einsum('xyc,yk->kxc', wide_values, sin_table, precision=HIGHEST)
    return jnp.stack([real_part, imag_part]) * factor

def forward_x(spectrum, factor):
    cosine, sine_part = angles(cell_numbers(NX), wave_numbers(MX), NX)
    cos_table = cosine / math.sqrt(NX)
    sin_table = -sine_part / math.sqrt(NX)
    first_part, second = (spectrum[0], spectrum[1])
    real_part = jnp.einsum('kxc,xm->mkc', first_part, cos_table, precision=HIGHEST) - jnp.einsum('kxc,xm->mkc', second, sin_table, precision=HIGHEST)
    imag_part = jnp.einsum('kxc,xm->mkc', first_part, sin_table, precision=HIGHEST) + jnp.einsum('kxc,xm->mkc', second, cos_table, precision=HIGHEST)
    return jnp.stack([real_part, imag_part]) * factor

def mix_modes(spectrum_modes, weights):
    real_part = jnp.einsum('mkc,mkco->mko', spectrum_modes[0], weights[0], precision=HIGHEST) - jnp.einsum('mkc,mkco->mko', spectrum_modes[1], weights[1], precision=HIGHEST)
    imag_part = jnp.einsum('mkc,mkco->mko', spectrum_modes[0], weights[1], precision=HIGHEST) + jnp.einsum('mkc,mkco->mko', spectrum_modes[1], weights[0], precision=HIGHEST)
    return jnp.stack([real_part, imag_part])

def inverse_x(spectrum_modes, factor):
    cosine, sine_part = angles(cell_numbers(NX), wave_numbers(MX), NX)
    cos_table = cosine / math.sqrt(MX)
    sin_table = sine_part / math.sqrt(MX)
    real_part = jnp.einsum('mkc,xm->kxc', spectrum_modes[0], cos_table, precision=HIGHEST) - jnp.einsum('mkc,xm->kxc', spectrum_modes[1], sin_table, precision=HIGHEST)
    imag_part = jnp.einsum('mkc,xm->kxc', spectrum_modes[0], sin_table, precision=HIGHEST) + jnp.einsum('mkc,xm->kxc', spectrum_modes[1], cos_table, precision=HIGHEST)
    return jnp.stack([real_part, imag_part]) * factor

def inverse_y(spectrum, factor):
    cosine, sine_part = angles(cell_numbers(NY), wave_numbers(MY), NY)
    cos_table = cosine / math.sqrt(MY)
    sin_table = sine_part / math.sqrt(MY)
    result = jnp.einsum('kxc,yk->xyc', spectrum[0], cos_table, precision=HIGHEST) - jnp.einsum('kxc,yk->xyc', spectrum[1], sin_table, precision=HIGHEST)
    return result * factor

def coarsen(values, factor):
    leading = values.shape[:-3]
    edge_cells = values.shape[-3]
    channels = values.shape[-1]
    grouped = values.astype(jnp.float32).reshape(leading + (edge_cells // factor, factor, edge_cells // factor, factor, channels))
    return lax.optimization_barrier(jnp.mean(grouped, axis=(-4, -2))).astype(jnp.bfloat16)

def pick_block(pooled, level_value, offset, block_side):
    edge_cells = pooled[0].shape[0]
    channels = pooled[0].shape[2]
    candidates = []
    for depth_level in range(3):
        limit_start = edge_cells // 2 ** depth_level - block_side
        start_row = jnp.minimum(offset[0] // 2 ** depth_level, limit_start)
        start_col = jnp.minimum(offset[1] // 2 ** depth_level, limit_start)
        candidates.append(lax.dynamic_slice(pooled[depth_level], (start_row, start_col, jnp.int32(0)), (block_side, block_side, channels)))
    return jnp.where(level_value == 0, candidates[0], jnp.where(level_value == 1, candidates[1], candidates[2]))

def place_block(gradient, level_value, offset, edge_cells):
    block_side = gradient.shape[0]
    channels = gradient.shape[2]
    candidates = []
    for depth_level in range(3):
        factor = 2 ** depth_level
        coarse_side = edge_cells // factor
        limit_start = coarse_side - block_side
        start_row = jnp.minimum(offset[0] // factor, limit_start)
        start_col = jnp.minimum(offset[1] // factor, limit_start)
        canvas = lax.dynamic_update_slice(jnp.zeros((coarse_side, coarse_side, channels), jnp.float32), gradient, (start_row, start_col, jnp.int32(0)))
        spread = jnp.broadcast_to(canvas[:, None, :, None, :], (coarse_side, factor, coarse_side, factor, channels))
        candidates.append(spread.reshape(edge_cells, edge_cells, channels) / float(factor * factor))
    return jnp.where(level_value == 0, candidates[0], jnp.where(level_value == 1, candidates[1], candidates[2]))

def pick_three(fine_grid, half_grid, quarter_grid, level_value, offset):
    return pick_block((fine_grid, half_grid, quarter_grid), level_value, offset, BLK)

def place_one(items):
    gradient, level_value, offset = items
    return place_block(gradient, level_value, offset, P_SIZE)

def to_patches(values):
    return values.reshape(PATCH_ROWS, P_SIZE, PATCH_COLS, P_SIZE, C).transpose(0, 2, 1, 3, 4).reshape(NPATCH, P_SIZE, P_SIZE, C)

def to_field(values):
    return values.reshape(PATCH_ROWS, PATCH_COLS, P_SIZE, P_SIZE, C).transpose(0, 2, 1, 3, 4).reshape(NX, NY, C)

def spread_cells(coarse):
    leading = coarse.shape[:-3]
    wide_values = jnp.broadcast_to(coarse[..., :, None, :, None, :], leading + (BLK, 4, BLK, 4, C))
    return wide_values.reshape(leading + (P_SIZE, P_SIZE, C))

def reference(flow_field, cotangent, spec_weight, skip_weight, ctx_weight, up_weight, down_weight, ctx_level, ctx_offset):
    inv_cells = 1.0 / math.sqrt(NX * NY)
    patches = to_patches(flow_field)
    pooled = (patches, coarsen(patches, 2), coarsen(patches, 4))
    patch_ids = jnp.arange(NPATCH, dtype=jnp.int32)
    row_ids = patch_ids // PATCH_COLS
    col_ids = patch_ids % PATCH_COLS
    sources = []
    arrived = []
    for direction in range(8):
        source = jnp.mod(row_ids + STEP_ROWS[direction], PATCH_ROWS) * PATCH_COLS + jnp.mod(col_ids + STEP_COLS[direction], PATCH_COLS)
        picked = jax.vmap(pick_three)(pooled[0][source], pooled[1][source], pooled[2][source], ctx_level[:, direction], ctx_offset[:, direction])
        sources.append(source)
        arrived.append(picked)
    arrived = jnp.stack(arrived, axis=1)
    wide_arrived = arrived.astype(jnp.float32)
    wide_ctx = ctx_weight.astype(jnp.float32)
    coarse = jnp.einsum('pdabc,dco->pabo', wide_arrived, wide_ctx, precision=HIGHEST)
    spectrum_modes = forward_x(forward_y(flow_field, 1.0), 1.0)
    spectral = inverse_y(inverse_x(mix_modes(spectrum_modes, spec_weight), 1.0), 1.0)
    spectral = lax.optimization_barrier(spectral.astype(jnp.bfloat16))
    flat_field = flow_field.reshape(NX * NY, C)
    skip_term = jnp.dot(flat_field, skip_weight, preferred_element_type=jnp.float32).reshape(NX, NY, C)
    preact = spectral.astype(jnp.float32) + skip_term + to_field(spread_cells(coarse))

    def row_step(totals, row_data):
        field_row, preact_row, grad_row = row_data
        middle = lax.optimization_barrier(gelu_value(preact_row).astype(jnp.bfloat16))
        lifted = jnp.dot(middle, up_weight, preferred_element_type=jnp.float32)
        hidden = gelu_value(lifted).astype(jnp.bfloat16)
        out_row = (middle.astype(jnp.float32) + jnp.dot(hidden, down_weight, preferred_element_type=jnp.float32)).astype(jnp.bfloat16)
        lift_grad = (jnp.dot(grad_row, down_weight.T, preferred_element_type=jnp.float32) * gelu_slope(lifted)).astype(jnp.bfloat16)
        middle_grad = grad_row.astype(jnp.float32) + jnp.dot(lift_grad, up_weight.T, preferred_element_type=jnp.float32)
        pre_grad_row = (middle_grad * gelu_slope(preact_row)).astype(jnp.bfloat16)
        totals = (totals[0] + jnp.dot(field_row.T, pre_grad_row, preferred_element_type=jnp.float32), totals[1] + jnp.dot(middle.T, lift_grad, preferred_element_type=jnp.float32), totals[2] + jnp.dot(hidden.T, grad_row, preferred_element_type=jnp.float32))
        return (totals, (out_row, pre_grad_row))
    initial = (jnp.zeros((C, C), jnp.float32), jnp.zeros((C, H), jnp.float32), jnp.zeros((H, C), jnp.float32))
    totals, (layer_output, pre_grad) = lax.scan(row_step, initial, (flow_field, preact, cotangent))
    cell_grad = to_patches(pre_grad.astype(jnp.float32)).reshape(NPATCH, BLK, 4, BLK, 4, C).sum(axis=(2, 4))
    grad_ctx = jnp.einsum('pdabc,pabo->dco', wide_arrived, cell_grad, precision=HIGHEST) * inv_cells
    block_grad = jnp.einsum('pabo,dco->pdabc', cell_grad, wide_ctx, precision=HIGHEST)
    ctx_back = jnp.zeros((NPATCH, P_SIZE, P_SIZE, C), jnp.float32)
    for direction in range(8):
        placed = lax.map(place_one, (block_grad[:, direction], ctx_level[:, direction], ctx_offset[:, direction]))
        ctx_back = ctx_back.at[sources[direction]].add(placed)
    grad_modes = forward_x(forward_y(pre_grad, math.sqrt(NY / MY)), math.sqrt(NX / MX))
    grad_real = jnp.einsum('mkc,mko->mkco', spectrum_modes[0], grad_modes[0], precision=HIGHEST) + jnp.einsum('mkc,mko->mkco', spectrum_modes[1], grad_modes[1], precision=HIGHEST)
    grad_imag = jnp.einsum('mkc,mko->mkco', spectrum_modes[0], grad_modes[1], precision=HIGHEST) - jnp.einsum('mkc,mko->mkco', spectrum_modes[1], grad_modes[0], precision=HIGHEST)
    grad_spec = jnp.stack([grad_real, grad_imag])
    back_real = jnp.einsum('mko,mkco->mkc', grad_modes[0], spec_weight[0], precision=HIGHEST) + jnp.einsum('mko,mkco->mkc', grad_modes[1], spec_weight[1], precision=HIGHEST)
    back_imag = jnp.einsum('mko,mkco->mkc', grad_modes[1], spec_weight[0], precision=HIGHEST) - jnp.einsum('mko,mkco->mkc', grad_modes[0], spec_weight[1], precision=HIGHEST)
    spec_back = inverse_y(inverse_x(jnp.stack([back_real, back_imag]), math.sqrt(MX / NX)), math.sqrt(MY / NY))
    skip_back = jnp.dot(pre_grad.reshape(NX * NY, C), skip_weight.T, preferred_element_type=jnp.float32).reshape(NX, NY, C)
    grad_field = (spec_back + skip_back + to_field(ctx_back)).astype(jnp.bfloat16)
    return (layer_output, grad_field, grad_spec, totals[0] * inv_cells, grad_ctx, totals[1] * inv_cells, totals[2] * inv_cells)
```

```python
import functools
import math

import jax
import jax.numpy as jnp
import ml_dtypes
import numpy as np
from jax import lax
from jax.experimental import pallas as pl
from jax.experimental.pallas import tpu as pltpu
from jax.sharding import PartitionSpec as P

BF = jnp.bfloat16
F32 = jnp.float32
TANH_SCALE = 0.7978845608028654
CUBIC_TERM = 0.044715
STEP_ROWS = (-1, -1, -1, 0, 0, 1, 1, 1)
STEP_COLS = (-1, 0, 1, -1, 1, -1, 0, 1)
ROWS, COLS = 8, 16
SIDE, C, H, BLK = 80, 128, 512, 20
NX, NY, MX, MY = 640, 1280, 64, 64
TOT = 2304
PIECE = TOT // COLS
VMEM_LIMIT = 56 * 1024 * 1024
MESH = pl.DeviceIdType.MESH
VM = pl.BlockSpec(memory_space=pltpu.VMEM)
SM = pl.BlockSpec(memory_space=pltpu.SMEM)
HB = pl.BlockSpec(memory_space=pl.ANY)


def wave_tables():
    waves = np.arange(64) - 32

    def parts(length, side):
        turns = (np.arange(length)[:, None] * waves[None, :]) % length
        phase = turns * (2.0 * math.pi / length)
        return np.cos(phase).reshape(-1, side, 64), np.sin(phase).reshape(-1, side, 64)

    cos_y, sin_y = parts(NY, SIDE)
    cos_x, sin_x = parts(NX, SIDE)
    to_modes_y = np.stack([cos_y, -sin_y], axis=-1).reshape(COLS, SIDE, 128) / math.sqrt(NY)
    to_modes_y = to_modes_y.transpose(0, 2, 1)
    to_cells_y = np.stack([cos_y, -sin_y], axis=-1).reshape(COLS, SIDE, 128) / math.sqrt(MY)
    cx, sx = cos_x.transpose(0, 2, 1), -sin_x.transpose(0, 2, 1)
    real = np.concatenate([cx, -sx], axis=2)
    imag = np.concatenate([sx, cx], axis=2)
    to_modes_x = np.stack([real, imag], axis=2).reshape(ROWS, 128, 2 * SIDE) / math.sqrt(NX)
    real = np.stack([cos_x, -sin_x], axis=-1).reshape(ROWS, SIDE, 128)
    imag = np.stack([sin_x, cos_x], axis=-1).reshape(ROWS, SIDE, 128)
    to_cells_x = np.concatenate([real, imag], axis=1) / math.sqrt(MX)
    return [
        np.ascontiguousarray(t).astype(ml_dtypes.bfloat16)
        for t in (to_modes_y, to_cells_y, to_modes_x, to_cells_x)
    ]


def iota(shape, axis):
    return lax.broadcasted_iota(jnp.int32, shape, axis)


def dot(a, b):
    return jnp.dot(a, b, preferred_element_type=F32)


def dot_tb(a, b):
    return lax.dot_general(a, b, (((1,), (1,)), ((), ())), preferred_element_type=F32)


def dot_ta(a, b):
    return lax.dot_general(a, b, (((0,), (0,)), ((), ())), preferred_element_type=F32)


def over_80(v):
    return (v * 52429) >> 22


def over_20(v):
    return (v * 52429) >> 20


def build_to_modes(table, big_ref):
    lane = iota((SIDE, 640), 1)
    tile = (lane - 80 * over_80(lane) == iota((SIDE, 640), 0)).astype(F32).astype(BF)
    for part in range(8):
        rep = ((iota((128, 128), 0) >> 3) + 16 * part == iota((128, 128), 1)).astype(F32)
        rows = dot(dot(rep.astype(BF), table).astype(BF), tile)
        mask = (iota((128, 640), 0) & 7) == over_80(iota((128, 640), 1))
        big_ref[pl.ds(128 * part, 128), :] = jnp.where(mask, rows, 0.0).astype(BF)


def build_to_cells(table, big_ref):
    rep = ((iota((128, 1024), 1) >> 3) == iota((128, 1024), 0)).astype(F32)
    wide = dot(table, rep.astype(BF))
    lane = iota((SIDE, 1024), 1) & 7
    for x in range(8):
        big_ref[pl.ds(SIDE * x, SIDE), :] = jnp.where(lane == x, wide, 0.0).astype(BF)


def x_to_modes(table, ay_ref, out_ref):
    def step(pair, carry):
        wide = []
        for ky in (2 * pair, 2 * pair + 1):
            real = ay_ref[:, 2 * ky].reshape(SIDE, C).astype(BF)
            imag = ay_ref[:, 2 * ky + 1].reshape(SIDE, C).astype(BF)
            wide.append(jnp.concatenate([real, imag], axis=0))
        modes = dot(table, jnp.concatenate(wide, axis=1))
        out_ref[2 * pair] = modes[:, :C].astype(BF)
        out_ref[2 * pair + 1] = modes[:, C:].astype(BF)
        return carry

    lax.fori_loop(0, 32, step, 0)


def x_to_cells(table, z_ref, p_ref):
    def step(pair, carry):
        wide = jnp.concatenate([z_ref[2 * pair], z_ref[2 * pair + 1]], axis=1)
        cells = dot(table, wide)
        for h in range(2):
            for r in range(2):
                piece = cells[r * SIDE : (r + 1) * SIDE, h * C : (h + 1) * C]
                p_ref[:, 2 * (2 * pair + h) + r] = piece.reshape(10, 8, C)
        return carry

    lax.fori_loop(0, 32, step, 0)


def y_store(modes, ay_ref, pair):
    ay_ref[2 * pair] = modes[:, :C].reshape(128, 8, C)
    ay_ref[2 * pair + 1] = modes[:, C:].reshape(128, 8, C)


def first_kernel(level, offset, field, ty, tx, s_out, blocks, big_out, ay, p0, p1, p2, tmp):
    row, col = lax.axis_index("px"), lax.axis_index("py")
    build_to_modes(ty[col], big_out)

    def y_step(pair, carry):
        first = field[pl.ds(16 * pair, 8)].reshape(640, C)
        second = field[pl.ds(16 * pair + 8, 8)].reshape(640, C)
        y_store(dot(big_out[...], jnp.concatenate([first, second], axis=1)), ay, pair)
        return carry

    lax.fori_loop(0, 5, y_step, 0)
    x_to_modes(tx[row], ay, s_out)

    def widen(x, carry):
        p0[x, pl.ds(0, SIDE)] = field[x].astype(F32)
        return carry

    lax.fori_loop(0, SIDE, widen, 0)

    def pool1(x, carry):
        total = jnp.zeros((40, C), F32)
        for a in range(2):
            for b in range(2):
                total = total + p0[2 * x + a, pl.ds(b, 40, stride=2)]
        p1[x, pl.ds(0, 40)] = (total * 0.25).astype(BF).astype(F32)
        return carry

    lax.fori_loop(0, 40, pool1, 0)

    def pool2(x, carry):
        total = jnp.zeros((20, C), F32)
        for a in range(4):
            for b in range(4):
                total = total + p0[4 * x + a, pl.ds(b, 20, stride=4)]
        p2[x, pl.ds(0, 20)] = (total * 0.0625).astype(BF).astype(F32)
        return carry

    lax.fori_loop(0, 20, pool2, 0)
    for d in range(8):
        target = lax.rem(row - STEP_ROWS[d] + ROWS, ROWS) * COLS
        target = target + lax.rem(col - STEP_COLS[d] + COLS, COLS)
        depth = level[target, d]
        for l, grid in enumerate((p0, p1, p2)):

            @pl.when(depth == l)
            def _():
                last = SIDE // 2**l - BLK
                sx = jnp.minimum(offset[target, 2 * d] >> l, last)
                sy = jnp.minimum(offset[target, 2 * d + 1] >> l, last)
                for a in range(BLK):
                    tmp[pl.ds(BLK * a, 24)] = grid[sx + a, pl.ds(sy, 24)]

        blocks[d] = tmp[pl.ds(0, 400)].astype(BF)


def first_call(level, offset, field, ty, tx):
    return pl.pallas_call(
        first_kernel,
        out_shape=(
            jax.ShapeDtypeStruct((64, 128, C), BF),
            jax.ShapeDtypeStruct((8, 400, C), BF),
            jax.ShapeDtypeStruct((1024, 640), BF),
        ),
        in_specs=[SM, SM, VM, VM, VM],
        out_specs=(VM, VM, VM),
        scratch_shapes=[
            pltpu.VMEM((10, 128, 8, C), F32),
            pltpu.VMEM((SIDE, 88, C), F32),
            pltpu.VMEM((40, 48, C), F32),
            pltpu.VMEM((20, 32, C), F32),
            pltpu.VMEM((408, C), F32),
        ],
        compiler_params=pltpu.CompilerParams(vmem_limit_bytes=VMEM_LIMIT),
        name="pick_and_forward",
    )(level, offset, field, ty, tx)


def exchange_kernel(back, *refs):
    if back:
        s, t, b, w, z, to, bo, u = refs[:8]
        refs = refs[8:]
    else:
        s, b, w, z, bo, u = refs[:6]
        refs = refs[6:]
    r0, s1, r1, s2, r2, zs, zp, wv, acc = refs[:9]
    send0, recv0, send1, recv1, send2, recv2, send3, recv3 = refs[9:17]
    send4, recv4, send5, recv5, sendc, recvc, local = refs[17:24]
    if back:
        t0, t1, q1, t2, q2, tacc, tout = refs[24:31]
        tsend0, trecv0, tsend1, trecv1, tsend2, trecv2 = refs[31:37]
        tsend4, trecv4, tsend5, trecv5 = refs[37:41]
    i, j = lax.axis_index("px"), lax.axis_index("py")
    c, q = j % 2, j // 2
    sibling = (i, 2 * q + 1 - c)

    def chip(n):
        return (i, 2 * n + c)

    def remote(src, dst, send, recv, device):
        return pltpu.make_async_remote_copy(
            src_ref=src,
            dst_ref=dst,
            send_sem=send,
            recv_sem=recv,
            device_id=device,
            device_id_type=MESH,
        )

    def loop(low, high, body):
        def step(n, carry):
            body(n)
            return carry

        lax.fori_loop(low, high, step, 0)

    def neighbour(d, sign):
        return (
            (i + sign * STEP_ROWS[d] + ROWS) % ROWS,
            (j + sign * STEP_COLS[d] + COLS) % COLS,
        )

    barrier = pltpu.get_barrier_semaphore()

    def greet(device):
        pl.semaphore_signal(barrier, inc=1, device_id=device, device_id_type=MESH)

    greet(sibling)

    def greet_more(r):
        greet(chip((q + r) % 8))
        greet(((i + r) % 8, j))

    loop(1, 8, greet_more)
    for d in range(8):
        greet(neighbour(d, 1))
    pl.semaphore_wait(barrier, 23)

    weights = pltpu.make_async_copy(w, wv, local.at[0])
    weights.start()

    def core_copy(n):
        return remote(s.at[2 * n + 1 - c], r0.at[n], send0.at[n], recv0.at[n], sibling)

    def core_copy_t(n):
        return remote(t.at[2 * n + 1 - c], t0.at[n], tsend0.at[n], trecv0.at[n], sibling)

    loop(1, 9, lambda r: core_copy((q + r) % 8).start())
    if back:
        loop(1, 9, lambda r: core_copy_t((q + r) % 8).start())

    def chip_copy(n, slot, device):
        return remote(s1.at[n], r1.at[slot], send1.at[n], recv1.at[slot], device)

    def chip_copy_t(n, slot, device):
        return remote(q1.at[n], t1.at[slot], tsend1.at[n], trecv1.at[slot], device)

    def pass_on(r):
        n = (q + r) % 8
        core_copy(n).wait_recv()
        s1[n] = (s[2 * n + c].astype(F32) + r0[n].astype(F32)).astype(BF)
        chip_copy(n, q, chip(n)).start()

    loop(1, 8, pass_on)
    core_copy(q).wait_recv()
    acc[...] = s[2 * q + c].astype(F32) + r0[q].astype(F32)

    def block_copy(d):
        sign = 1 if back else -1
        return remote(b.at[d], bo.at[d], sendc.at[d], recvc.at[d], neighbour(d, sign))

    for d in range(8):
        block_copy(d).start()
    if back:

        def pass_on_t(r):
            n = (q + r) % 8
            core_copy_t(n).wait_recv()
            q1[n] = (t[2 * n + c].astype(F32) + t0[n].astype(F32)).astype(BF)
            chip_copy_t(n, q, chip(n)).start()

        loop(1, 8, pass_on_t)
        core_copy_t(q).wait_recv()
        tacc[...] = t[2 * q + c].astype(F32) + t0[q].astype(F32)

    def gather_chip(r):
        n = (q - r + 8) % 8
        chip_copy(n, n, chip(n)).wait_recv()
        acc[...] = acc[...] + r1[n].astype(F32)

    loop(1, 8, gather_chip)
    s2[...] = acc[...].astype(BF).reshape(4, 128, C)

    def rows_of(n):
        return pl.ds(pl.multiple_of(n * 16, 16), 16)

    def row_copy(n, slot, device):
        return remote(s2.at[:, rows_of(n)], r2.at[slot], send2.at[n], recv2.at[slot], device)

    def send_row(r):
        n = (i + r) % 8
        row_copy(n, i, (n, j)).start()

    loop(1, 8, send_row)
    u[...] = s2[:, rows_of(i)].astype(F32)

    def gather_row(r):
        n = (i - r + 8) % 8
        row_copy(n, n, (n, j)).wait_recv()
        u[...] = u[...] + r2[n].astype(F32)

    loop(1, 8, gather_row)
    if back:
        u[...] = u[...] * math.sqrt(NX * NY / (MX * MY))
    weights.wait()
    same = iota((16, 16), 0) ^ 1
    turn = jnp.where(iota((16, 16), 1) == same, 1.0, 0.0)
    odd = (iota((16, 16), 0) & 1) == 1
    flip = odd if back else jnp.logical_not(odd)
    turn = jnp.where(flip, -turn, turn).astype(BF)

    def mix(ky):
        first = u[ky].astype(BF)
        both = jnp.concatenate([first, dot(turn, first).astype(BF)], axis=1)
        total = jnp.zeros((16, C), F32)
        for kx in range(8):
            if back:
                mat = jnp.concatenate([wv[0, kx, ky], wv[1, kx, ky]], axis=1).astype(BF)
                res = dot_tb(both, mat)
            else:
                mat = jnp.concatenate([wv[0, kx, ky], wv[1, kx, ky]], axis=0).astype(BF)
                res = dot(both, mat)
            total = jnp.where((iota((16, C), 0) >> 1) == kx, res, total)
        zs[ky] = total.astype(BF)

    loop(0, 4, mix)
    zp[:, rows_of(i)] = zs[...]

    def mode_copy(slot, sem, device):
        return remote(zs, zp.at[:, rows_of(slot)], send3.at[sem], recv3.at[slot], device)

    def send_mode(r):
        n = (i + r) % 8
        mode_copy(i, n, (n, j)).start()

    loop(1, 8, send_mode)
    if back:

        def gather_chip_t(r):
            n = (q - r + 8) % 8
            chip_copy_t(n, n, chip(n)).wait_recv()
            tacc[...] = tacc[...] + t1[n].astype(F32)

        loop(1, 8, gather_chip_t)
        q2[...] = tacc[...].astype(BF)
        t2[i] = q2[...]

        def row_copy_t(n, slot, device):
            return remote(q2, t2.at[slot], tsend2.at[n], trecv2.at[slot], device)

        def send_row_t(r):
            n = (i + r) % 8
            row_copy_t(n, i, (n, j)).start()

        loop(1, 8, send_row_t)

    def gather_mode(r):
        n = (i - r + 8) % 8
        mode_copy(n, n, (n, j)).wait_recv()

    loop(1, 8, gather_mode)

    own = pltpu.make_async_copy(zp, z.at[j], local.at[1])
    own.start()

    def all_copy(slot, sem, recv, device):
        return remote(zp, z.at[slot], send4.at[sem], recv, device)

    def send_all(r):
        n = (q + r) % 8
        all_copy(j, n, recv4.at[q], chip(n)).start()

    loop(1, 8, send_all)
    all_copy(j, q, recv5.at[q], sibling).start()
    if back:

        def gather_row_t(r):
            n = (i - r + 8) % 8
            row_copy_t(n, n, (n, j)).wait_recv()

        loop(1, 8, gather_row_t)
        total = t2[0].astype(F32)
        for n in range(1, 8):
            total = total + t2[n].astype(F32)
        tout[...] = total.astype(BF)
        own_t = pltpu.make_async_copy(tout, to.at[j], local.at[2])
        own_t.start()

        def all_copy_t(slot, sem, recv, device):
            return remote(tout, to.at[slot], tsend4.at[sem], recv, device)

        def send_all_t(r):
            n = (q + r) % 8
            all_copy_t(j, n, trecv4.at[q], chip(n)).start()

        loop(1, 8, send_all_t)
        all_copy_t(j, q, trecv5.at[q], sibling).start()

    def forward_copy(n):
        piece = z.at[2 * n + c]
        return remote(piece, piece, send5.at[n], recv5.at[n], sibling)

    def forward(r):
        n = (q - r + 8) % 8
        all_copy(2 * n + c, n, recv4.at[n], chip(n)).wait_recv()
        forward_copy(n).start()

    loop(1, 8, forward)
    if back:

        def forward_copy_t(n):
            piece = to.at[2 * n + c]
            return remote(piece, piece, tsend5.at[n], trecv5.at[n], sibling)

        def forward_t(r):
            n = (q - r + 8) % 8
            all_copy_t(2 * n + c, n, trecv4.at[n], chip(n)).wait_recv()
            forward_copy_t(n).start()

        loop(1, 8, forward_t)

    def settle(r):
        n = (q + r) % 8
        all_copy(2 * n + 1 - c, n, recv5.at[n], sibling).wait_recv()
        core_copy(n).wait_send()
        all_copy(j, n, recv4.at[q], chip(n)).wait_send()
        if back:
            all_copy_t(2 * n + 1 - c, n, trecv5.at[n], sibling).wait_recv()
            core_copy_t(n).wait_send()
            all_copy_t(j, n, trecv4.at[q], chip(n)).wait_send()

    loop(1, 9, settle)

    def settle_most(r):
        n = (q + r) % 8
        forward_copy(n).wait_send()
        chip_copy(n, q, chip(n)).wait_send()
        m = (i + r) % 8
        row_copy(m, i, (m, j)).wait_send()
        mode_copy(i, m, (m, j)).wait_send()
        if back:
            forward_copy_t(n).wait_send()
            chip_copy_t(n, q, chip(n)).wait_send()
            row_copy_t(m, i, (m, j)).wait_send()

    loop(1, 8, settle_most)
    own.wait()
    if back:
        own_t.wait()
    for d in range(8):
        block_copy(d).wait()


def exchange(back, s, blocks, weights, totals=None):
    shape = jax.ShapeDtypeStruct
    out_shape = [shape((16, 4, 128, C), BF)]
    out_specs = [HB]
    operands = [s.reshape(16, 512, C)]
    in_specs = [VM]
    if back:
        out_shape.append(shape((16, PIECE, C), BF))
        out_specs.append(HB)
        operands.append(totals)
        in_specs.append(VM)
    out_shape += [shape((8, 400, C), BF), shape((4, 16, C), F32)]
    out_specs += [HB, VM]
    operands += [blocks, weights]
    in_specs += [HB, HB]
    sem = pltpu.SemaphoreType.DMA((8,))
    scratch = [
        pltpu.VMEM((8, 512, C), BF),
        pltpu.VMEM((8, 512, C), BF),
        pltpu.VMEM((8, 512, C), BF),
        pltpu.VMEM((4, 128, C), BF),
        pltpu.VMEM((8, 4, 16, C), BF),
        pltpu.VMEM((4, 16, C), BF),
        pltpu.VMEM((4, 128, C), BF),
        pltpu.VMEM((2, 8, 4, C, C), F32),
        pltpu.VMEM((512, C), F32),
    ] + [sem] * 15
    if back:
        scratch += [
            pltpu.VMEM((8, PIECE, C), BF),
            pltpu.VMEM((8, PIECE, C), BF),
            pltpu.VMEM((8, PIECE, C), BF),
            pltpu.VMEM((8, PIECE, C), BF),
            pltpu.VMEM((PIECE, C), BF),
            pltpu.VMEM((PIECE, C), F32),
            pltpu.VMEM((PIECE, C), BF),
        ] + [sem] * 10
    return pl.pallas_call(
        functools.partial(exchange_kernel, back),
        out_shape=tuple(out_shape),
        in_specs=in_specs,
        out_specs=tuple(out_specs),
        scratch_shapes=scratch,
        compiler_params=pltpu.CompilerParams(
            collective_id=2 if back else 1,
            has_side_effects=True,
            vmem_limit_bytes=VMEM_LIMIT,
        ),
        name="exchange_back" if back else "exchange",
    )(*operands)


def gelu_both(v):
    square = v * v
    t = jnp.tanh(v * (TANH_SCALE + (TANH_SCALE * CUBIC_TERM) * square))
    half = 0.5 + 0.5 * t
    inner = (0.5 * TANH_SCALE) + (1.5 * TANH_SCALE * CUBIC_TERM) * square
    return v * half, half + v * (1.0 - t * t) * inner


def middle_kernel(
    field, cot, z, blk, skip, ctx, up, down, gy, gx, tx, big_in,
    layer, pre_out, s_out, tot, bgrad,
    p, ay, cells_big, spread, gather, coarse, cell, pre, slope, mid, lifted, dh, hid, lg,
    acc_skip, acc_up, acc_down,
):
    step = pl.program_id(0)
    row, col = lax.axis_index("px"), lax.axis_index("py")

    @pl.when(step == 0)
    def _():
        x_to_cells(gx[row], z, p)
        build_to_cells(gy[col], cells_big)
        total = dot(blk[0], ctx[0])
        for d in range(1, 8):
            total = total + dot(blk[d], ctx[d])
        coarse[...] = total
        n, l = iota((1280, 160), 0), iota((1280, 160), 1)
        l = jnp.where(l >= 80, l - 80, l)
        x = over_80(n)
        y = n - 80 * x
        a = over_20(l)
        hit = ((x >> 2) == a) & ((y >> 2) == l - 20 * a)
        spread[...] = jnp.where(hit, 1.0, 0.0).astype(BF)
        l, n = iota((80, 1280), 0), iota((80, 1280), 1)
        x = over_80(n)
        y = n - 80 * x
        a = over_20(l)
        hit = ((x >> 2) == a) & ((y >> 2) == l - 20 * a)
        gather[...] = jnp.where(hit, 1.0, 0.0).astype(BF)
        acc_skip[...] = jnp.zeros_like(acc_skip)
        acc_up[...] = jnp.zeros_like(acc_up)
        acc_down[...] = jnp.zeros_like(acc_down)

    own_rows = pl.ds(pl.multiple_of(80 * step, 8), 80)
    flat = field[...].reshape(1280, C)
    flat_cot = cot[...].reshape(1280, C)
    wide = jnp.concatenate(
        [p[2 * step].reshape(1024, C).astype(BF), p[2 * step + 1].reshape(1024, C).astype(BF)],
        axis=1,
    )
    spectral = dot(cells_big[...], wide)
    own = coarse[own_rows]
    high = own.astype(BF)
    low = (own - high.astype(F32)).astype(BF)
    rest = dot(flat, skip[...]) + dot(spread[...], jnp.concatenate([high, low], axis=0))
    pre[pl.ds(0, 640)] = spectral[:, :C].astype(BF).astype(F32) + rest[:640]
    pre[pl.ds(640, 640)] = spectral[:, C:].astype(BF).astype(F32) + rest[640:]

    def activate(n, carry):
        rows = pl.ds(pl.multiple_of(64 * n, 64), 64)
        value, slant = gelu_both(pre[rows])
        mid[rows] = value.astype(BF)
        slope[rows] = slant
        return carry

    lax.fori_loop(0, 20, activate, 0)
    lifted[...] = dot(mid[...], up[...])
    dh[...] = dot_tb(flat_cot, down[...])

    def activate_wide(n, carry):
        rows = pl.ds(pl.multiple_of(16 * n, 16), 16)
        value, slant = gelu_both(lifted[rows])
        hid[rows] = value.astype(BF)
        lg[rows] = (dh[rows] * slant).astype(BF)
        return carry

    lax.fori_loop(0, 80, activate_wide, 0)
    result = mid[...].astype(F32) + dot(hid[...], down[...])
    layer[...] = result.astype(BF).reshape(16, SIDE, C)
    grad = flat_cot.astype(F32) + dot_tb(lg[...], up[...])
    grad = (grad * slope[...]).astype(BF)
    pre_out[...] = grad.reshape(16, SIDE, C)
    acc_skip[...] += dot_ta(flat, grad)
    acc_up[...] += dot_ta(mid[...], lg[...])
    acc_down[...] += dot_ta(flat_cot, hid[...])
    cell[own_rows] = dot(gather[...], grad)
    y_store(dot(big_in[...], jnp.concatenate([grad[:640], grad[640:]], axis=1)), ay, step)

    @pl.when(step == 4)
    def _():
        x_to_modes(tx[row], ay, s_out)
        narrow = cell[...].astype(BF)
        tot[pl.ds(0, 128)] = acc_skip[...].astype(BF)
        for d in range(8):
            tot[pl.ds(128 + 128 * d, 128)] = dot_ta(blk[d], narrow).astype(BF)
            bgrad[d] = dot_tb(narrow, ctx[d]).astype(BF)
        for part in range(4):
            cut = slice(128 * part, 128 * part + 128)
            tot[pl.ds(1152 + 128 * part, 128)] = acc_up[:, cut].astype(BF)
            tot[pl.ds(1664 + 128 * part, 128)] = acc_down[:, cut].T.astype(BF)
        tot[pl.ds(2176, 128)] = jnp.zeros((128, C), BF)


def whole(*shape):
    zeros = (0,) * len(shape)
    return pl.BlockSpec(shape, lambda n: zeros)


def middle_call(field, cot, z, blk, skip, ctx, up, down, gy, gx, tx, big):
    shape = jax.ShapeDtypeStruct
    tile = pl.BlockSpec((16, SIDE, C), lambda n: (n, 0, 0))
    return pl.pallas_call(
        middle_kernel,
        grid=(5,),
        out_shape=(
            shape((SIDE, SIDE, C), BF),
            shape((SIDE, SIDE, C), BF),
            shape((64, 128, C), BF),
            shape((TOT, C), BF),
            shape((8, 400, C), BF),
        ),
        in_specs=[
            tile, tile, whole(64, 128, C), whole(8, 400, C), whole(C, C), whole(8, C, C),
            whole(C, H), whole(H, C), whole(COLS, SIDE, 128), whole(ROWS, 160, 128),
            whole(ROWS, 128, 160), whole(1024, 640),
        ],
        out_specs=(tile, tile, whole(64, 128, C), whole(TOT, C), whole(8, 400, C)),
        scratch_shapes=[
            pltpu.VMEM((10, 128, 8, C), F32),
            pltpu.VMEM((10, 128, 8, C), F32),
            pltpu.VMEM((640, 1024), BF),
            pltpu.VMEM((1280, 160), BF),
            pltpu.VMEM((80, 1280), BF),
            pltpu.VMEM((400, C), F32),
            pltpu.VMEM((400, C), F32),
            pltpu.VMEM((1280, C), F32),
            pltpu.VMEM((1280, C), F32),
            pltpu.VMEM((1280, C), BF),
            pltpu.VMEM((1280, H), F32),
            pltpu.VMEM((1280, H), F32),
            pltpu.VMEM((1280, H), BF),
            pltpu.VMEM((1280, H), BF),
            pltpu.VMEM((C, C), F32),
            pltpu.VMEM((C, H), F32),
            pltpu.VMEM((C, H), F32),
        ],
        compiler_params=pltpu.CompilerParams(vmem_limit_bytes=VMEM_LIMIT),
        name="cells",
    )(field, cot, z, blk, skip, ctx, up, down, gy, gx, tx, big)


def last_kernel(level, offset, pre, z, back, skip, gy, gx, out, p, cells_big, place, grads, wide):
    step = pl.program_id(0)
    row, col = lax.axis_index("px"), lax.axis_index("py")
    starts = []
    for d in range(8):
        target = lax.rem(row - STEP_ROWS[d] + ROWS, ROWS) * COLS
        target = target + lax.rem(col - STEP_COLS[d] + COLS, COLS)
        depth = level[target, d]
        last = jnp.where(depth == 0, 60, jnp.where(depth == 1, 20, 0))
        sx = jnp.minimum(offset[target, 2 * d] >> depth, last)
        sy = jnp.minimum(offset[target, 2 * d + 1] >> depth, last)
        starts.append((depth, sx, sy))

    @pl.when(step == 0)
    def _():
        x_to_cells(gx[row], z, p)
        build_to_cells(gy[col], cells_big)
        y, lane = iota((SIDE, 192), 0), iota((SIDE, 192), 1)
        total = jnp.zeros((SIDE, 192), F32)
        for d in range(8):
            depth, sx, sy = starts[d]
            share = jnp.where(depth == 0, 1.0, jnp.where(depth == 1, 0.25, 0.0625))
            spot = lane - 24 * d
            line = jnp.where(depth == 0, y, jnp.where(depth == 1, y >> 1, y >> 2))
            hit = (spot >= 0) & (spot < BLK) & (line - sy == spot)
            total = jnp.where(hit, share, total)
        place[...] = total.astype(BF)
        wide[pl.ds(400, 8)] = jnp.zeros((8, C), F32)
        for d in range(8):
            wide[pl.ds(0, 400)] = back[d].astype(F32)
            for a in range(BLK):
                grads[d, a] = wide[pl.ds(BLK * a, 24)]
            grads[d, BLK] = jnp.zeros((24, C), F32)

    both = jnp.concatenate(
        [p[2 * step].reshape(1024, C).astype(BF), p[2 * step + 1].reshape(1024, C).astype(BF)],
        axis=1,
    )
    factor = math.sqrt(MX * MY / (NX * NY))
    spectral = dot(cells_big[...], both) * factor
    straight = dot_tb(pre[...].reshape(1280, C), skip[...])
    for x in range(16):
        pieces = []
        for d in range(8):
            depth, sx, sy = starts[d]
            a = ((16 * step + x) >> depth) - sx
            a = jnp.where((a >= 0) & (a < BLK), a, BLK)
            pieces.append(grads[d, a])
        context = dot(place[...], jnp.concatenate(pieces, axis=0).astype(BF))
        h, k = x // 8, x % 8
        total = spectral[80 * k : 80 * k + 80, C * h : C * h + C]
        total = total + straight[80 * x : 80 * x + 80] + context
        out[x] = total.astype(BF)


def last_call(level, offset, pre, z, back, skip, gy, gx):
    tile = pl.BlockSpec((16, SIDE, C), lambda n: (n, 0, 0))
    return pl.pallas_call(
        last_kernel,
        grid=(5,),
        out_shape=jax.ShapeDtypeStruct((SIDE, SIDE, C), BF),
        in_specs=[
            SM, SM, tile, whole(64, 128, C), whole(8, 400, C), whole(C, C),
            whole(COLS, SIDE, 128), whole(ROWS, 160, 128),
        ],
        out_specs=tile,
        scratch_shapes=[
            pltpu.VMEM((10, 128, 8, C), F32),
            pltpu.VMEM((640, 1024), BF),
            pltpu.VMEM((SIDE, 192), BF),
            pltpu.VMEM((8, BLK + 1, 24, C), F32),
            pltpu.VMEM((408, C), F32),
        ],
        compiler_params=pltpu.CompilerParams(vmem_limit_bytes=VMEM_LIMIT),
        name="field_gradient",
    )(level, offset, pre, z, back, skip, gy, gx)


def outer_kernel(u, g, tot, spec, skip, ctx, up, down):
    kx = pl.program_id(0)
    mask = (iota((16, C), 0) >> 1) == kx
    turn = jnp.where(iota((16, 16), 1) == (iota((16, 16), 0) ^ 1), 1.0, 0.0)
    turn = jnp.where((iota((16, 16), 0) & 1) == 1, -turn, turn)
    for ky in range(4):
        left = jnp.where(mask, u[ky], 0.0)
        left_high = left.astype(BF)
        left_low = (left - left_high.astype(F32)).astype(BF)
        right = g[ky]
        right_high = right.astype(BF)
        right_low = (right - right_high.astype(F32)).astype(BF)
        narrow = turn.astype(BF)
        high = jnp.concatenate([right_high, dot(narrow, right_high).astype(BF)], axis=1)
        low = jnp.concatenate([right_low, dot(narrow, right_low).astype(BF)], axis=1)
        lefts = jnp.concatenate([left_high, left_high, left_low], axis=0)
        rights = jnp.concatenate([high, low, high], axis=0)
        res = dot_ta(lefts, rights)
        spec[0, 0, ky] = res[:, :C]
        spec[1, 0, ky] = res[:, C:]

    @pl.when(kx == 0)
    def _():
        inv = 1.0 / math.sqrt(NX * NY)
        skip[...] = tot[pl.ds(0, 128)].astype(F32) * inv
        for d in range(8):
            ctx[d] = tot[pl.ds(128 + 128 * d, 128)].astype(F32) * inv
        for part in range(4):
            cut = slice(128 * part, 128 * part + 128)
            up[:, cut] = tot[pl.ds(1152 + 128 * part, 128)].astype(F32) * inv
        down[...] = tot[pl.ds(1664, 512)].astype(F32) * inv


def outer_call(u, g, tot):
    shape = jax.ShapeDtypeStruct
    return pl.pallas_call(
        outer_kernel,
        grid=(8,),
        out_shape=(
            shape((2, 8, 4, C, C), F32),
            shape((C, C), F32),
            shape((8, C, C), F32),
            shape((C, H), F32),
            shape((H, C), F32),
        ),
        in_specs=[whole(4, 16, C), whole(4, 16, C), whole(TOT, C)],
        out_specs=(
            pl.BlockSpec((2, 1, 4, C, C), lambda n: (0, n, 0, 0, 0)),
            whole(C, C),
            whole(8, C, C),
            whole(C, H),
            whole(H, C),
        ),
        compiler_params=pltpu.CompilerParams(vmem_limit_bytes=VMEM_LIMIT),
        name="weight_gradients",
    )(u, g, tot)


def shards(
    flow_field, cotangent, spec_weight, skip_weight, ctx_weight, up_weight, down_weight,
    ctx_level, ctx_offset,
):
    ty, gy, tx, gx = (jnp.asarray(t) for t in wave_tables())
    offset = ctx_offset.reshape(ROWS * COLS, 16)
    s, blocks, big = first_call(ctx_level, offset, flow_field, ty, tx)
    z, arrived, u = exchange(False, s, blocks, spec_weight)
    layer, pre, s, tot, bgrad = middle_call(
        flow_field, cotangent, z.reshape(64, 128, C), arrived, skip_weight, ctx_weight,
        up_weight, down_weight, gy, gx, tx, big,
    )
    z, tot, back, g = exchange(True, s, bgrad, spec_weight, tot.reshape(16, PIECE, C))
    spec, skip, ctx, up, down = outer_call(u, g, tot.reshape(TOT, C))
    grad = last_call(
        ctx_level, offset, pre, z.reshape(64, 128, C), back, skip_weight, gy, gx
    )
    return layer, grad, spec, skip, ctx, up, down


def solution(mesh):
    return jax.shard_map(
        shards,
        mesh=mesh,
        in_specs=(
            P("px", "py", None),
            P("px", "py", None),
            P(None, "px", "py", None, None),
            P(),
            P(),
            P(),
            P(),
            P(),
            P(),
        ),
        out_specs=(
            P("px", "py", None),
            P("px", "py", None),
            P(None, "px", "py", None, None),
            P(),
            P(),
            P(),
            P(),
        ),
        check_vma=False,
    )
```

```python
import functools
import math

import jax
import jax.numpy as jnp
import ml_dtypes
import numpy as np
from jax import lax
from jax.experimental import pallas as pl
from jax.experimental.pallas import tpu as pltpu
from jax.sharding import PartitionSpec as P

BF = jnp.bfloat16
F32 = jnp.float32
TANH_SCALE = 0.7978845608028654
CUBIC_TERM = 0.044715
STEP_ROWS = (-1, -1, -1, 0, 0, 1, 1, 1)
STEP_COLS = (-1, 0, 1, -1, 1, -1, 0, 1)
ROWS, COLS = 8, 16
SIDE, C, H, BLK = 80, 128, 512, 20
NX, NY, MX, MY = 640, 1280, 64, 64
PIECE = 80
TOT = 32 * PIECE
VMEM_LIMIT = 56 * 1024 * 1024
MESH = pl.DeviceIdType.MESH
VM = pl.BlockSpec(memory_space=pltpu.VMEM)
SM = pl.BlockSpec(memory_space=pltpu.SMEM)
HB = pl.BlockSpec(memory_space=pl.ANY)


def wave_tables():
    waves = np.arange(64) - 32

    def parts(length, side):
        turns = (np.arange(length)[:, None] * waves[None, :]) % length
        phase = turns * (2.0 * math.pi / length)
        return np.cos(phase).reshape(-1, side, 64), np.sin(phase).reshape(-1, side, 64)

    cos_y, sin_y = parts(NY, SIDE)
    cos_x, sin_x = parts(NX, SIDE)
    to_modes_y = np.stack([cos_y, -sin_y], axis=-1).reshape(COLS, SIDE, 128) / math.sqrt(NY)
    to_modes_y = to_modes_y.transpose(0, 2, 1)
    to_cells_y = np.stack([cos_y, -sin_y], axis=-1).reshape(COLS, SIDE, 128) / math.sqrt(MY)
    cx, sx = cos_x.transpose(0, 2, 1), -sin_x.transpose(0, 2, 1)
    real = np.concatenate([cx, -sx], axis=2)
    imag = np.concatenate([sx, cx], axis=2)
    to_modes_x = np.stack([real, imag], axis=2).reshape(ROWS, 128, 2 * SIDE) / math.sqrt(NX)
    real = np.stack([cos_x, -sin_x], axis=-1).reshape(ROWS, SIDE, 128)
    imag = np.stack([sin_x, cos_x], axis=-1).reshape(ROWS, SIDE, 128)
    to_cells_x = np.concatenate([real, imag], axis=1) / math.sqrt(MX)

    def rounded(t):
        return np.ascontiguousarray(t).astype(ml_dtypes.bfloat16)

    def rest(t):
        return rounded(t - rounded(t).astype(np.float64))

    high, low = rounded(to_modes_x), rest(to_modes_x)
    wide_modes_x = np.concatenate([high, low, high], axis=2)
    wide_cells_x = np.concatenate([rounded(to_cells_x), rest(to_cells_x)], axis=2)
    return rounded(to_modes_y), rounded(to_cells_y), wide_modes_x, wide_cells_x


def iota(shape, axis):
    return lax.broadcasted_iota(jnp.int32, shape, axis)


def dot(a, b):
    return jnp.dot(a, b, preferred_element_type=F32)


def dot_tb(a, b):
    return lax.dot_general(a, b, (((1,), (1,)), ((), ())), preferred_element_type=F32)


def dot_ta(a, b):
    return lax.dot_general(a, b, (((0,), (0,)), ((), ())), preferred_element_type=F32)


def over_80(v):
    return (v * 52429) >> 22


def over_20(v):
    return (v * 52429) >> 20


def build_to_modes(table, big_ref):
    lane = iota((SIDE, 640), 1)
    tile = (lane - 80 * over_80(lane) == iota((SIDE, 640), 0)).astype(F32).astype(BF)
    for part in range(8):
        rep = ((iota((128, 128), 0) >> 3) + 16 * part == iota((128, 128), 1)).astype(F32)
        rows = dot(dot(rep.astype(BF), table).astype(BF), tile)
        mask = (iota((128, 640), 0) & 7) == over_80(iota((128, 640), 1))
        big_ref[pl.ds(128 * part, 128), :] = jnp.where(mask, rows, 0.0).astype(BF)


def build_to_cells(table, big_ref):
    rep = ((iota((128, 1024), 1) >> 3) == iota((128, 1024), 0)).astype(F32)
    wide = dot(table, rep.astype(BF))
    lane = iota((SIDE, 1024), 1) & 7
    for x in range(8):
        big_ref[pl.ds(SIDE * x, SIDE), :] = jnp.where(lane == x, wide, 0.0).astype(BF)


def x_to_modes(table, ay_ref, kys):
    wide = []
    for ky in kys:
        both = [ay_ref[:, 2 * ky + r].reshape(SIDE, C) for r in range(2)]
        high = [v.astype(BF) for v in both]
        low = [(v - h.astype(F32)).astype(BF) for v, h in zip(both, high)]
        wide.append(jnp.concatenate(high + high + low, axis=0))
    modes = dot(table, jnp.concatenate(wide, axis=1)).astype(BF)
    return modes[:, :C], modes[:, C:]


def x_to_cells(table, z_ref, p_ref):
    def step(pair, carry):
        wide = jnp.concatenate([z_ref[2 * pair], z_ref[2 * pair + 1]], axis=1)
        cells = dot(table, jnp.concatenate([wide, wide], axis=0))
        for h in range(2):
            for r in range(2):
                piece = cells[r * SIDE : (r + 1) * SIDE, h * C : (h + 1) * C]
                p_ref[:, 2 * (2 * pair + h) + r] = piece.reshape(10, 8, C)
        return carry

    lax.fori_loop(0, 32, step, 0, unroll=4)


def y_store(modes, ay_ref, pair):
    ay_ref[2 * pair] = modes[:, :C].reshape(128, 8, C)
    ay_ref[2 * pair + 1] = modes[:, C:].reshape(128, 8, C)


def y_to_modes(big, field, ay):
    def y_step(pair, carry):
        first = field[pl.ds(16 * pair, 8)].reshape(640, C)
        second = field[pl.ds(16 * pair + 8, 8)].reshape(640, C)
        y_store(dot(big[...], jnp.concatenate([first, second], axis=1)), ay, pair)
        return carry

    lax.fori_loop(0, 5, y_step, 0)


def start_of(pick):
    depth = pick & 3
    first, second = (pick >> 2) & 127, pick >> 9

    def choose(zero, one, two):
        return jnp.where(depth == 0, zero, jnp.where(depth == 1, one, two))

    last = choose(SIDE - BLK, SIDE // 2 - BLK, 0)
    sx = jnp.minimum(choose(first, first >> 1, first >> 2), last)
    sy = jnp.minimum(choose(second, second >> 1, second >> 2), last)
    return depth, sx, sy


def pick_of(picks, row, col, d):
    target = lax.rem(row - STEP_ROWS[d] + ROWS, ROWS) * COLS
    return picks[target + lax.rem(col - STEP_COLS[d] + COLS, COLS), d]


def pick_blocks(picks, row, col, field, grid, tmp, blocks):
    def widen(x, carry):
        grid[x, pl.ds(0, SIDE)] = field[x].astype(F32)
        return carry

    lax.fori_loop(0, SIDE, widen, 0, unroll=4)

    def pool1(x, carry):
        total = jnp.zeros((40, C), F32)
        for a in range(2):
            for b in range(2):
                total = total + grid[2 * x + a, pl.ds(b, 40, stride=2)]
        grid[SIDE + x, pl.ds(0, 40)] = (total * 0.25).astype(BF).astype(F32)
        return carry

    lax.fori_loop(0, 40, pool1, 0, unroll=4)

    def pool2(x, carry):
        total = jnp.zeros((20, C), F32)
        for a in range(4):
            for b in range(4):
                total = total + grid[4 * x + a, pl.ds(b, 20, stride=4)]
        grid[SIDE + 40 + x, pl.ds(0, 20)] = (total * 0.0625).astype(BF).astype(F32)
        return carry

    lax.fori_loop(0, 20, pool2, 0, unroll=4)
    for d in range(8):
        depth, sx, sy = start_of(pick_of(picks, row, col, d))
        base = sx + jnp.where(depth == 0, 0, jnp.where(depth == 1, SIDE, SIDE + 40))
        for a in range(BLK):
            tmp[pl.ds(BLK * a, 24)] = grid[base + a, pl.ds(sy, 24)]
        blocks[d] = tmp[pl.ds(0, 400)].astype(BF)


def exchange_kernel(back, *refs):
    refs = list(refs)

    def take(n):
        taken = refs[:n]
        del refs[:n]
        return taken

    if back:
        s, b, w, t = take(4)
        z, bo, u, to = take(4)
    else:
        picks, field, ty, tx, w = take(5)
        z, bo, u, big_out = take(4)
    r0, sa, sb, r1a, r1b, acca, accb, r2a, r2b, ab, r3, zs, zz, za, zb, wv = take(16)
    core_a, core_b, one_a, one_b, two_a, two_b, three, wide3 = take(8)
    wide2_a, wide2_b, wide1_a, wide1_b, share_a, share_b, blocks, local = take(8)
    if back:
        t0, t1s, t1, t2s, t2, t3s, t3, tall = take(8)
        core_t, one_t, two_t, three_t, wide2_t, wide1_t, share_t = take(7)
    else:
        s, b, big, ay, grid, tmp, ty_own, tx_own = take(8)
    i, j = lax.axis_index("px"), lax.axis_index("py")
    y, zh = i // 2, i % 2
    zl, x, c = j // 8, (j // 2) % 4, j % 2
    spot = 2 * zl + zh
    sibling = (i, 8 * zl + 2 * x + 1 - c)

    def at_x(n):
        return (i, 8 * zl + 2 * n + c)

    def at_y(n):
        return (2 * n + zh, j)

    def at_z(n):
        return (2 * y + n % 2, 8 * (n // 2) + 2 * x + c)

    def remote(src, dst, sems, sent, landed, device):
        return pltpu.make_async_remote_copy(
            src_ref=src,
            dst_ref=dst,
            send_sem=sems.at[0, sent],
            recv_sem=sems.at[1, landed],
            device_id=device,
            device_id_type=MESH,
        )

    def neighbour(d, sign):
        return (
            (i + sign * STEP_ROWS[d] + ROWS) % ROWS,
            (j + sign * STEP_COLS[d] + COLS) % COLS,
        )

    def band(n, size=32):
        return pl.ds(pl.multiple_of(n * size, size), size)

    barrier = pltpu.get_barrier_semaphore()
    partners = [sibling]
    for r in (1, 2, 3):
        partners += [at_x((x + r) % 4), at_y((y + r) % 4), at_z((spot + r) % 4)]
    partners += [neighbour(d, 1) for d in range(8)]
    for device in partners:
        pl.semaphore_signal(barrier, inc=1, device_id=device, device_id_type=MESH)
    weights = pltpu.make_async_copy(w, wv, local.at[0])
    weights.start()
    if not back:
        table_y = pltpu.make_async_copy(ty.at[j], ty_own, local.at[3])
        table_y.start()
        table_x = pltpu.make_async_copy(tx.at[i], tx_own, local.at[4])
        table_x.start()
        pick_blocks(picks, i, j, field, grid, tmp, b)
    pl.semaphore_wait(barrier, len(partners))
    waits = []

    def begin(copy):
        copy.start()
        waits.append(copy)

    def core_copy_a(n):
        return remote(s.at[:, n, 1 - c, 0:2], r0.at[:, n, 0:2], core_a, n, n, sibling)

    def core_copy_b(n):
        src = s.at[:, :, 1 - c, 2:4, band(n)]
        return remote(src, r0.at[:, :, 2:4, band(n)], core_b, n, n, sibling)

    def block_copy(d):
        device = neighbour(d, 1 if back else -1)
        return remote(b.at[d], bo.at[d], blocks, d, d, device)

    def fill(n, half):
        def step(m, carry):
            a, e = m // 2, m % 2
            ky = 4 * (8 * a + 2 * n + e) + 2 * half
            first, second = x_to_modes(tx_own[...], ay, (ky, ky + 1))
            s[a, n, e, 2 * half] = first
            s[a, n, e, 2 * half + 1] = second
            return carry

        lax.fori_loop(0, 4, step, 0, unroll=2)

    if back:
        for r in (2, 1, 3, 0):
            begin(core_copy_a((x + r) % 4))
            begin(core_copy_b((y + r) % 4))
    else:
        for d in range(8):
            begin(block_copy(d))
        table_y.wait()
        build_to_modes(ty_own[...], big)
        keep = pltpu.make_async_copy(big, big_out, local.at[5])
        keep.start()
        y_to_modes(big, field, ay)
        table_x.wait()
        for r in (2, 1, 3, 0):
            n = (x + r) % 4
            fill(n, 0)
            begin(core_copy_a(n))
    if back:

        def core_copy_t():
            return remote(t.at[1 - c], t0, core_t, 0, 0, sibling)

        begin(core_copy_t())

    def one_copy_a(n, slot, device):
        return remote(sa.at[n], r1a.at[slot], one_a, n, slot, device)

    def one_copy_b(n, slot, device):
        return remote(sb.at[n], r1b.at[slot], one_b, n, slot, device)

    def sum_a(n):
        core_copy_a(n).wait_recv()
        return s[:, n, c, 0:2].astype(F32) + r0[:, n, 0:2].astype(F32)

    def sum_b(n):
        core_copy_b(n).wait_recv()
        rows = band(n)
        return s[:, :, c, 2:4, rows].astype(F32) + r0[:, :, 2:4, rows].astype(F32)

    def pass_a(r):
        n = (x + r) % 4
        sa[n] = sum_a(n).astype(BF)
        begin(one_copy_a(n, x, at_x(n)))

    def pass_b(r):
        n = (y + r) % 4
        sb[n] = sum_b(n).astype(BF)
        begin(one_copy_b(n, y, at_y(n)))

    if back:
        for r in (2, 1, 3):
            pass_a(r)
            pass_b(r)
        for d in range(8):
            begin(block_copy(d))
    else:
        for r in (2, 1, 3, 0):
            fill((x + r) % 4, 1)
            if r:
                pass_a(r)
        for r in (2, 1, 3, 0):
            begin(core_copy_b((y + r) % 4))
        for r in (2, 1, 3):
            pass_b(r)
    acca[...] = sum_a(x)
    accb[...] = sum_b(y)
    if back:

        def one_copy_t(n, slot, device):
            return remote(t1s.at[n], t1.at[slot], one_t, n, slot, device)

        core_copy_t().wait_recv()
        t1s[...] = (t[c].astype(F32) + t0[...].astype(F32)).astype(BF)
        for r in (2, 1, 3):
            n = (x + r) % 4
            begin(one_copy_t(n, x, at_x(n)))
    for r in (1, 3, 2):
        n = (x + r) % 4
        one_copy_a(n, n, at_x(n)).wait_recv()
        acca[...] = acca[...] + r1a[n].astype(F32)

    def two_copy_a(n, slot, device):
        return remote(acca.at[:, :, band(n)], r2a.at[slot], two_a, n, slot, device)

    def two_copy_b(n, slot, device):
        return remote(accb.at[:, n], r2b.at[slot], two_b, n, slot, device)

    for r in (2, 1, 3):
        n = (y + r) % 4
        begin(two_copy_a(n, y, at_y(n)))
    for r in (1, 3, 2):
        n = (y + r) % 4
        one_copy_b(n, n, at_y(n)).wait_recv()
        accb[...] = accb[...] + r1b[n].astype(F32)
    for r in (2, 1, 3):
        n = (x + r) % 4
        begin(two_copy_b(n, x, at_x(n)))
    ab[:, 0:2] = acca[:, :, band(y)]
    ab[:, 2:4] = accb[:, x]
    for r in (1, 3, 2):
        n = (y + r) % 4
        two_copy_a(n, n, at_y(n)).wait_recv()
        ab[:, 0:2] = ab[:, 0:2] + r2a[n]
    for r in (1, 3, 2):
        n = (x + r) % 4
        two_copy_b(n, n, at_x(n)).wait_recv()
        ab[:, 2:4] = ab[:, 2:4] + r2b[n]

    def three_copy(n, slot, device):
        return remote(ab.at[n // 2, :, band(n % 2, 16)], r3.at[slot], three, n, slot, device)

    for r in (2, 1, 3):
        n = (spot + r) % 4
        begin(three_copy(n, spot, at_z(n)))
    if back:

        def two_copy_t(n, slot, device):
            return remote(t2s.at[n], t2.at[slot], two_t, n, slot, device)

        total = t1s[x].astype(F32)
        for r in (1, 3, 2):
            n = (x + r) % 4
            one_copy_t(n, n, at_x(n)).wait_recv()
            total = total + t1[n].astype(F32)
        t2s[...] = total.astype(BF)
        for r in (2, 1, 3):
            n = (y + r) % 4
            begin(two_copy_t(n, y, at_y(n)))
    u[...] = ab[zl, :, band(zh, 16)]
    for r in (1, 3, 2):
        n = (spot + r) % 4
        three_copy(n, n, at_z(n)).wait_recv()
        u[...] = u[...] + r3[n]
    if back:
        u[...] = u[...] * math.sqrt(NX * NY / (MX * MY))
    weights.wait()
    same = iota((16, 16), 0) ^ 1
    turn = jnp.where(iota((16, 16), 1) == same, 1.0, 0.0)
    odd = (iota((16, 16), 0) & 1) == 1
    flip = odd if back else jnp.logical_not(odd)
    turn = jnp.where(flip, -turn, turn).astype(BF)

    def mix(ky, carry):
        first = u[ky]
        high = first.astype(BF)
        low = (first - high.astype(F32)).astype(BF)
        both = jnp.concatenate([high, low], axis=0)
        turned = jnp.concatenate([dot(turn, high), dot(turn, low)], axis=0).astype(BF)
        both = jnp.concatenate([both, turned], axis=1)
        total = jnp.zeros((16, C), F32)
        for kx in range(8):
            if back:
                mat = jnp.concatenate([wv[0, kx, ky], wv[1, kx, ky]], axis=1).astype(BF)
                res = dot_tb(both, mat)
            else:
                mat = jnp.concatenate([wv[0, kx, ky], wv[1, kx, ky]], axis=0).astype(BF)
                res = dot(both, mat)
            total = jnp.where((iota((16, C), 0) >> 1) == kx, res[:16] + res[16:], total)
        zs[ky] = total.astype(BF)
        return carry

    lax.fori_loop(0, 4, mix, 0)

    def wide_copy3(slot, sent, device):
        dst = zz.at[slot // 2, :, band(slot % 2, 16)]
        return remote(zs, dst, wide3, sent, slot, device)

    for r in (2, 1, 3):
        n = (spot + r) % 4
        begin(wide_copy3(spot, n, at_z(n)))
    zz[zl, :, band(zh, 16)] = zs[...]
    if back:
        t3s[...] = t2s[y]
        total = t3s[...].astype(F32)
        for r in (1, 3, 2):
            n = (y + r) % 4
            two_copy_t(n, n, at_y(n)).wait_recv()
            total = total + t2[n].astype(F32)
        t3s[...] = total.astype(BF)
        t3[spot] = t3s[...]

        def three_copy_t(slot, sent, device):
            return remote(t3s, t3.at[slot], three_t, sent, slot, device)

        for r in (2, 1, 3):
            n = (spot + r) % 4
            begin(three_copy_t(spot, n, at_z(n)))
    for r in (1, 3, 2):
        n = (spot + r) % 4
        wide_copy3(n, n, at_z(n)).wait_recv()

    def wide_copy2_a(slot, sent, device):
        return remote(zz.at[:, 0:2], za.at[:, :, band(slot)], wide2_a, sent, slot, device)

    def wide_copy2_b(slot, sent, device):
        return remote(zz.at[:, 2:4], zb.at[:, slot], wide2_b, sent, slot, device)

    for r in (2, 1, 3):
        n = (y + r) % 4
        begin(wide_copy2_a(y, n, at_y(n)))
        n = (x + r) % 4
        begin(wide_copy2_b(x, n, at_x(n)))
    za[:, :, band(y)] = zz[:, 0:2]
    zb[:, x] = zz[:, 2:4]

    def part_a(n, core):
        return z.at[:, n, core, 0:2]

    def part_b(n, core):
        return z.at[:, :, core, 2:4, band(n)]

    def wide_copy1_a(slot, sent, device):
        return remote(za, part_a(slot, c), wide1_a, sent, slot, device)

    def wide_copy1_b(slot, sent, device):
        return remote(zb, part_b(slot, c), wide1_b, sent, slot, device)

    for r in (1, 3, 2):
        n = (y + r) % 4
        wide_copy2_a(n, n, at_y(n)).wait_recv()
    for r in (2, 1, 3):
        n = (x + r) % 4
        begin(wide_copy1_a(x, n, at_x(n)))
    for r in (1, 3, 2):
        n = (x + r) % 4
        wide_copy2_b(n, n, at_x(n)).wait_recv()
    for r in (2, 1, 3):
        n = (y + r) % 4
        begin(wide_copy1_b(y, n, at_y(n)))
    own_a = pltpu.make_async_copy(za, part_a(x, c), local.at[1])
    own_a.start()
    own_b = pltpu.make_async_copy(zb, part_b(y, c), local.at[2])
    own_b.start()
    begin(remote(za, part_a(x, c), share_a, x, x, sibling))
    begin(remote(zb, part_b(y, c), share_b, y, y, sibling))
    if back:
        for r in (1, 3, 2):
            n = (spot + r) % 4
            three_copy_t(n, n, at_z(n)).wait_recv()
        total = t3[0].astype(F32)
        for n in range(1, 4):
            total = total + t3[n].astype(F32)
        tall[x, y] = total.astype(BF)

        def wide_copy2_t(slot, sent, device):
            piece = tall.at[x, slot]
            return remote(piece, piece, wide2_t, sent, slot, device)

        for r in (2, 1, 3):
            n = (y + r) % 4
            begin(wide_copy2_t(y, n, at_y(n)))
        for r in (1, 3, 2):
            n = (y + r) % 4
            wide_copy2_t(n, n, at_y(n)).wait_recv()

        def wide_copy1_t(slot, sent, device):
            piece = tall.at[slot]
            return remote(piece, piece, wide1_t, sent, slot, device)

        for r in (2, 1, 3):
            n = (x + r) % 4
            begin(wide_copy1_t(x, n, at_x(n)))

    def share_copy_a(n, core):
        return remote(part_a(n, core), part_a(n, core), share_a, n, n, sibling)

    def share_copy_b(n, core):
        return remote(part_b(n, core), part_b(n, core), share_b, n, n, sibling)

    for r in (1, 3, 2):
        n = (x + r) % 4
        wide_copy1_a(n, n, at_x(n)).wait_recv()
        begin(share_copy_a(n, c))
        n = (y + r) % 4
        wide_copy1_b(n, n, at_y(n)).wait_recv()
        begin(share_copy_b(n, c))
    if back:
        for r in (1, 3, 2):
            n = (x + r) % 4
            wide_copy1_t(n, n, at_x(n)).wait_recv()
        share = remote(tall, to.at[c], share_t, 0, 0, sibling)
        begin(share)
        own_t = pltpu.make_async_copy(tall, to.at[c], local.at[3])
        own_t.start()
    for n in range(4):
        share_copy_a(n, 1 - c).wait_recv()
        share_copy_b(n, 1 - c).wait_recv()
    for d in range(8):
        block_copy(d).wait_recv()
    own_a.wait()
    own_b.wait()
    if back:
        share.wait_recv()
        own_t.wait()
    else:
        keep.wait()
    for copy in waits:
        copy.wait_send()


def exchange(back, *operands):
    shape = jax.ShapeDtypeStruct
    out_shape = [shape((2, 4, 2, 4, 128, C), BF), shape((8, 400, C), BF), shape((4, 16, C), F32)]
    out_specs = [HB, HB, VM, HB]
    if back:
        out_shape.append(shape((2, 4, 4, PIECE, C), BF))
        in_specs = [VM, HB, HB, VM]
    else:
        out_shape.append(shape((1024, 640), BF))
        in_specs = [SM, VM, HB, HB, HB]
    sem = pltpu.SemaphoreType.DMA((2, 4))
    scratch = [
        pltpu.VMEM((2, 4, 4, 128, C), BF),
        pltpu.VMEM((4, 2, 2, 128, C), BF),
        pltpu.VMEM((4, 2, 4, 2, 32, C), BF),
        pltpu.VMEM((4, 2, 2, 128, C), BF),
        pltpu.VMEM((4, 2, 4, 2, 32, C), BF),
        pltpu.VMEM((2, 2, 128, C), F32),
        pltpu.VMEM((2, 4, 2, 32, C), F32),
        pltpu.VMEM((4, 2, 2, 32, C), F32),
        pltpu.VMEM((4, 2, 2, 32, C), F32),
        pltpu.VMEM((2, 4, 32, C), F32),
        pltpu.VMEM((4, 4, 16, C), F32),
        pltpu.VMEM((4, 16, C), BF),
        pltpu.VMEM((2, 4, 32, C), BF),
        pltpu.VMEM((2, 2, 128, C), BF),
        pltpu.VMEM((2, 4, 2, 32, C), BF),
        pltpu.VMEM((2, 8, 4, C, C), F32),
    ]
    scratch += [sem] * 14 + [pltpu.SemaphoreType.DMA((2, 8)), pltpu.SemaphoreType.DMA((6,))]
    if back:
        scratch += [
            pltpu.VMEM((4, 4, PIECE, C), BF),
            pltpu.VMEM((4, 4, PIECE, C), BF),
            pltpu.VMEM((4, 4, PIECE, C), BF),
            pltpu.VMEM((4, PIECE, C), BF),
            pltpu.VMEM((4, PIECE, C), BF),
            pltpu.VMEM((PIECE, C), BF),
            pltpu.VMEM((4, PIECE, C), BF),
            pltpu.VMEM((4, 4, PIECE, C), BF),
        ] + [sem] * 7
    else:
        scratch += [
            pltpu.VMEM((2, 4, 2, 4, 128, C), BF),
            pltpu.VMEM((8, 400, C), BF),
            pltpu.VMEM((1024, 640), BF),
            pltpu.VMEM((10, 128, 8, C), F32),
            pltpu.VMEM((SIDE + 60, 88, C), F32),
            pltpu.VMEM((408, C), F32),
            pltpu.VMEM((128, SIDE), BF),
            pltpu.VMEM((128, 480), BF),
        ]
    return pl.pallas_call(
        functools.partial(exchange_kernel, back),
        out_shape=tuple(out_shape),
        in_specs=in_specs,
        out_specs=tuple(out_specs),
        scratch_shapes=scratch,
        compiler_params=pltpu.CompilerParams(
            collective_id=2 if back else 1,
            has_side_effects=True,
            vmem_limit_bytes=VMEM_LIMIT,
        ),
        name="exchange_back" if back else "exchange",
    )(*operands)


def gelu_both(v):
    square = v * v
    t = jnp.tanh(v * (TANH_SCALE + (TANH_SCALE * CUBIC_TERM) * square))
    half = 0.5 + 0.5 * t
    inner = (0.5 * TANH_SCALE) + (1.5 * TANH_SCALE * CUBIC_TERM) * square
    return v * half, half + v * (1.0 - t * t) * inner


def middle_kernel(
    field, cot, z, blk, skip, ctx, up, down, gy, gx, tx, big_in,
    layer, pre_out, s_out, tot, bgrad,
    p, ay, cells_big, spread, gather, coarse, cell, pre, slope, mid, lifted, dh, hid, lg,
    acc_skip, acc_up, acc_down,
):
    step = pl.program_id(0)
    row, col = lax.axis_index("px"), lax.axis_index("py")

    @pl.when(step == 0)
    def _():
        x_to_cells(gx[row], z, p)
        build_to_cells(gy[col], cells_big)
        total = dot(blk[0], ctx[0])
        for d in range(1, 8):
            total = total + dot(blk[d], ctx[d])
        coarse[...] = total
        n, l = iota((1280, 160), 0), iota((1280, 160), 1)
        l = jnp.where(l >= 80, l - 80, l)
        x = over_80(n)
        y = n - 80 * x
        a = over_20(l)
        hit = ((x >> 2) == a) & ((y >> 2) == l - 20 * a)
        spread[...] = jnp.where(hit, 1.0, 0.0).astype(BF)
        l, n = iota((80, 1280), 0), iota((80, 1280), 1)
        x = over_80(n)
        y = n - 80 * x
        a = over_20(l)
        hit = ((x >> 2) == a) & ((y >> 2) == l - 20 * a)
        gather[...] = jnp.where(hit, 1.0, 0.0).astype(BF)
        acc_skip[...] = jnp.zeros_like(acc_skip)
        acc_up[...] = jnp.zeros_like(acc_up)
        acc_down[...] = jnp.zeros_like(acc_down)

    own_rows = pl.ds(pl.multiple_of(80 * step, 8), 80)
    flat = field[...].reshape(1280, C)
    flat_cot = cot[...].reshape(1280, C)
    wide = jnp.concatenate(
        [p[2 * step].reshape(1024, C).astype(BF), p[2 * step + 1].reshape(1024, C).astype(BF)],
        axis=1,
    )
    spectral = dot(cells_big[...], wide)
    own = coarse[own_rows]
    high = own.astype(BF)
    low = (own - high.astype(F32)).astype(BF)
    rest = dot(flat, skip[...]) + dot(spread[...], jnp.concatenate([high, low], axis=0))
    pre[pl.ds(0, 640)] = spectral[:, :C].astype(BF).astype(F32) + rest[:640]
    pre[pl.ds(640, 640)] = spectral[:, C:].astype(BF).astype(F32) + rest[640:]

    def activate(n, carry):
        rows = pl.ds(pl.multiple_of(64 * n, 64), 64)
        value, slant = gelu_both(pre[rows])
        mid[rows] = value.astype(BF)
        slope[rows] = slant
        return carry

    lax.fori_loop(0, 20, activate, 0, unroll=2)
    lifted[...] = dot(mid[...], up[...])
    dh[...] = dot_tb(flat_cot, down[...])

    def activate_wide(n, carry):
        rows = pl.ds(pl.multiple_of(16 * n, 16), 16)
        value, slant = gelu_both(lifted[rows])
        hid[rows] = value.astype(BF)
        lg[rows] = (dh[rows] * slant).astype(BF)
        return carry

    lax.fori_loop(0, 80, activate_wide, 0, unroll=8)
    result = mid[...].astype(F32) + dot(hid[...], down[...])
    layer[...] = result.astype(BF).reshape(16, SIDE, C)
    grad = flat_cot.astype(F32) + dot_tb(lg[...], up[...])
    grad = (grad * slope[...]).astype(BF)
    pre_out[...] = grad.reshape(16, SIDE, C)
    acc_skip[...] += dot_ta(flat, grad)
    acc_up[...] += dot_ta(mid[...], lg[...])
    acc_down[...] += dot_ta(flat_cot, hid[...])
    cell[own_rows] = dot(gather[...], grad)
    y_store(dot(big_in[...], jnp.concatenate([grad[:640], grad[640:]], axis=1)), ay, step)

    @pl.when(step == 4)
    def _():

        def modes_step(pair, carry):
            first, second = x_to_modes(tx[row], ay, (2 * pair, 2 * pair + 1))
            s_out[2 * pair] = first
            s_out[2 * pair + 1] = second
            return carry

        lax.fori_loop(0, 32, modes_step, 0, unroll=4)
        narrow = cell[...].astype(BF)
        tot[pl.ds(0, 128)] = acc_skip[...].astype(BF)
        for d in range(8):
            tot[pl.ds(128 + 128 * d, 128)] = dot_ta(blk[d], narrow).astype(BF)
            bgrad[d] = dot_tb(narrow, ctx[d]).astype(BF)
        for part in range(4):
            cut = slice(128 * part, 128 * part + 128)
            tot[pl.ds(1152 + 128 * part, 128)] = acc_up[:, cut].astype(BF)
            tot[pl.ds(1664 + 128 * part, 128)] = acc_down[:, cut].T.astype(BF)
        tot[pl.ds(2176, TOT - 2176)] = jnp.zeros((TOT - 2176, C), BF)


def whole(*shape):
    zeros = (0,) * len(shape)
    return pl.BlockSpec(shape, lambda n: zeros)


def middle_call(field, cot, z, blk, skip, ctx, up, down, gy, gx, tx, big):
    shape = jax.ShapeDtypeStruct
    tile = pl.BlockSpec((16, SIDE, C), lambda n: (n, 0, 0))
    return pl.pallas_call(
        middle_kernel,
        grid=(5,),
        out_shape=(
            shape((SIDE, SIDE, C), BF),
            shape((SIDE, SIDE, C), BF),
            shape((64, 128, C), BF),
            shape((TOT, C), BF),
            shape((8, 400, C), BF),
        ),
        in_specs=[
            tile, tile, whole(64, 128, C), whole(8, 400, C), whole(C, C), whole(8, C, C),
            whole(C, H), whole(H, C), whole(COLS, SIDE, 128), whole(ROWS, 160, 256),
            whole(ROWS, 128, 480), whole(1024, 640),
        ],
        out_specs=(tile, tile, whole(64, 128, C), whole(TOT, C), whole(8, 400, C)),
        scratch_shapes=[
            pltpu.VMEM((10, 128, 8, C), F32),
            pltpu.VMEM((10, 128, 8, C), F32),
            pltpu.VMEM((640, 1024), BF),
            pltpu.VMEM((1280, 160), BF),
            pltpu.VMEM((80, 1280), BF),
            pltpu.VMEM((400, C), F32),
            pltpu.VMEM((400, C), F32),
            pltpu.VMEM((1280, C), F32),
            pltpu.VMEM((1280, C), F32),
            pltpu.VMEM((1280, C), BF),
            pltpu.VMEM((1280, H), F32),
            pltpu.VMEM((1280, H), F32),
            pltpu.VMEM((1280, H), BF),
            pltpu.VMEM((1280, H), BF),
            pltpu.VMEM((C, C), F32),
            pltpu.VMEM((C, H), F32),
            pltpu.VMEM((C, H), F32),
        ],
        compiler_params=pltpu.CompilerParams(vmem_limit_bytes=VMEM_LIMIT),
        name="cells",
    )(field, cot, z, blk, skip, ctx, up, down, gy, gx, tx, big)


def last_kernel(picks, pre, z, back, skip, gy, gx, out, p, cells_big, place, grads, wide):
    step = pl.program_id(0)
    row, col = lax.axis_index("px"), lax.axis_index("py")
    starts = [start_of(pick_of(picks, row, col, d)) for d in range(8)]

    @pl.when(step == 0)
    def _():
        x_to_cells(gx[row], z, p)
        build_to_cells(gy[col], cells_big)
        y, lane = iota((SIDE, 192), 0), iota((SIDE, 192), 1)
        total = jnp.zeros((SIDE, 192), F32)
        for d in range(8):
            depth, sx, sy = starts[d]
            share = jnp.where(depth == 0, 1.0, jnp.where(depth == 1, 0.25, 0.0625))
            spot = lane - 24 * d
            line = jnp.where(depth == 0, y, jnp.where(depth == 1, y >> 1, y >> 2))
            hit = (spot >= 0) & (spot < BLK) & (line - sy == spot)
            total = jnp.where(hit, share, total)
        place[...] = total.astype(BF)
        wide[pl.ds(400, 8)] = jnp.zeros((8, C), F32)
        for d in range(8):
            wide[pl.ds(0, 400)] = back[d].astype(F32)
            for a in range(BLK):
                grads[d, a] = wide[pl.ds(BLK * a, 24)]
            grads[d, BLK] = jnp.zeros((24, C), F32)

    both = jnp.concatenate(
        [p[2 * step].reshape(1024, C).astype(BF), p[2 * step + 1].reshape(1024, C).astype(BF)],
        axis=1,
    )
    factor = math.sqrt(MX * MY / (NX * NY))
    spectral = dot(cells_big[...], both) * factor
    straight = dot_tb(pre[...].reshape(1280, C), skip[...])
    for x in range(16):
        pieces = []
        for d in range(8):
            depth, sx, sy = starts[d]
            a = ((16 * step + x) >> depth) - sx
            a = jnp.where((a >= 0) & (a < BLK), a, BLK)
            pieces.append(grads[d, a])
        context = dot(place[...], jnp.concatenate(pieces, axis=0).astype(BF))
        h, k = x // 8, x % 8
        total = spectral[80 * k : 80 * k + 80, C * h : C * h + C]
        total = total + straight[80 * x : 80 * x + 80] + context
        out[x] = total.astype(BF)


def last_call(picks, pre, z, back, skip, gy, gx):
    tile = pl.BlockSpec((16, SIDE, C), lambda n: (n, 0, 0))
    return pl.pallas_call(
        last_kernel,
        grid=(5,),
        out_shape=jax.ShapeDtypeStruct((SIDE, SIDE, C), BF),
        in_specs=[
            SM, tile, whole(64, 128, C), whole(8, 400, C), whole(C, C),
            whole(COLS, SIDE, 128), whole(ROWS, 160, 256),
        ],
        out_specs=tile,
        scratch_shapes=[
            pltpu.VMEM((10, 128, 8, C), F32),
            pltpu.VMEM((640, 1024), BF),
            pltpu.VMEM((SIDE, 192), BF),
            pltpu.VMEM((8, BLK + 1, 24, C), F32),
            pltpu.VMEM((408, C), F32),
        ],
        compiler_params=pltpu.CompilerParams(vmem_limit_bytes=VMEM_LIMIT),
        name="field_gradient",
    )(picks, pre, z, back, skip, gy, gx)


def outer_kernel(u, g, tot, spec, skip, ctx, up, down):
    kx = pl.program_id(0)
    mask = (iota((16, C), 0) >> 1) == kx
    turn = jnp.where(iota((16, 16), 1) == (iota((16, 16), 0) ^ 1), 1.0, 0.0)
    turn = jnp.where((iota((16, 16), 0) & 1) == 1, -turn, turn)
    for ky in range(4):
        left = jnp.where(mask, u[ky], 0.0)
        left_high = left.astype(BF)
        left_low = (left - left_high.astype(F32)).astype(BF)
        right = g[ky]
        right_high = right.astype(BF)
        right_low = (right - right_high.astype(F32)).astype(BF)
        narrow = turn.astype(BF)
        high = jnp.concatenate([right_high, dot(narrow, right_high).astype(BF)], axis=1)
        low = jnp.concatenate([right_low, dot(narrow, right_low).astype(BF)], axis=1)
        lefts = jnp.concatenate([left_high, left_high, left_low], axis=0)
        rights = jnp.concatenate([high, low, high], axis=0)
        res = dot_ta(lefts, rights)
        spec[0, 0, ky] = res[:, :C]
        spec[1, 0, ky] = res[:, C:]

    @pl.when(kx == 0)
    def _():
        inv = 1.0 / math.sqrt(NX * NY)
        skip[...] = tot[pl.ds(0, 128)].astype(F32) * inv
        for d in range(8):
            ctx[d] = tot[pl.ds(128 + 128 * d, 128)].astype(F32) * inv
        for part in range(4):
            cut = slice(128 * part, 128 * part + 128)
            up[:, cut] = tot[pl.ds(1152 + 128 * part, 128)].astype(F32) * inv
        down[...] = tot[pl.ds(1664, 512)].astype(F32) * inv


def outer_call(u, g, tot):
    shape = jax.ShapeDtypeStruct
    return pl.pallas_call(
        outer_kernel,
        grid=(8,),
        out_shape=(
            shape((2, 8, 4, C, C), F32),
            shape((C, C), F32),
            shape((8, C, C), F32),
            shape((C, H), F32),
            shape((H, C), F32),
        ),
        in_specs=[whole(4, 16, C), whole(4, 16, C), whole(TOT, C)],
        out_specs=(
            pl.BlockSpec((2, 1, 4, C, C), lambda n: (0, n, 0, 0, 0)),
            whole(C, C),
            whole(8, C, C),
            whole(C, H),
            whole(H, C),
        ),
        compiler_params=pltpu.CompilerParams(vmem_limit_bytes=VMEM_LIMIT),
        name="weight_gradients",
    )(u, g, tot)


def shards(
    flow_field, cotangent, spec_weight, skip_weight, ctx_weight, up_weight, down_weight,
    ctx_level, ctx_offset,
):
    ty, gy, tx, gx = (jnp.asarray(t) for t in wave_tables())
    picks = ctx_level + (ctx_offset[:, :, 0] << 2) + (ctx_offset[:, :, 1] << 9)
    z, arrived, u, big = exchange(False, picks, flow_field, ty, tx, spec_weight)
    layer, pre, s, tot, bgrad = middle_call(
        flow_field, cotangent, z.reshape(64, 128, C), arrived, skip_weight, ctx_weight,
        up_weight, down_weight, gy, gx, tx, big,
    )
    tot = tot.reshape(2, 4, 4, PIECE, C)
    s = s.reshape(2, 4, 2, 4, 128, C)
    z, back, g, tot = exchange(True, s, bgrad, spec_weight, tot)
    spec, skip, ctx, up, down = outer_call(u, g, tot.reshape(TOT, C))
    grad = last_call(picks, pre, z.reshape(64, 128, C), back, skip_weight, gy, gx)
    return layer, grad, spec, skip, ctx, up, down


def solution(mesh):
    return jax.shard_map(
        shards,
        mesh=mesh,
        in_specs=(
            P("px", "py", None),
            P("px", "py", None),
            P(None, "px", "py", None, None),
            P(),
            P(),
            P(),
            P(),
            P(),
            P(),
        ),
        out_specs=(
            P("px", "py", None),
            P("px", "py", None),
            P(None, "px", "py", None, None),
            P(),
            P(),
            P(),
            P(),
        ),
        check_vma=False,
    )
```

```python
import functools
import math

import jax
import jax.numpy as jnp
import ml_dtypes
import numpy as np
from jax import lax
from jax.experimental import pallas as pl
from jax.experimental.pallas import tpu as pltpu
from jax.sharding import PartitionSpec as P

BF = jnp.bfloat16
F32 = jnp.float32
TANH_SCALE = 0.7978845608028654
CUBIC_TERM = 0.044715
STEP_ROWS = (-1, -1, -1, 0, 0, 1, 1, 1)
STEP_COLS = (-1, 0, 1, -1, 1, -1, 0, 1)
ROWS, COLS = 8, 16
SIDE, C, H, BLK = 80, 128, 512, 20
NX, NY, MX, MY = 640, 1280, 64, 64
PIECE = 80
TOT = 32 * PIECE
VMEM_LIMIT = 56 * 1024 * 1024
MESH = pl.DeviceIdType.MESH
VM = pl.BlockSpec(memory_space=pltpu.VMEM)
SM = pl.BlockSpec(memory_space=pltpu.SMEM)
HB = pl.BlockSpec(memory_space=pl.ANY)


def wave_tables():
    waves = np.arange(64) - 32

    def parts(length, side):
        turns = (np.arange(length)[:, None] * waves[None, :]) % length
        phase = turns * (2.0 * math.pi / length)
        return np.cos(phase).reshape(-1, side, 64), np.sin(phase).reshape(-1, side, 64)

    cos_y, sin_y = parts(NY, SIDE)
    cos_x, sin_x = parts(NX, SIDE)
    to_modes_y = np.stack([cos_y, -sin_y], axis=-1).reshape(COLS, SIDE, 128) / math.sqrt(NY)
    to_modes_y = to_modes_y.transpose(0, 2, 1)
    to_cells_y = np.stack([cos_y, -sin_y], axis=-1).reshape(COLS, SIDE, 128) / math.sqrt(MY)
    cx, sx = cos_x.transpose(0, 2, 1), -sin_x.transpose(0, 2, 1)
    real = np.concatenate([cx, -sx], axis=2)
    imag = np.concatenate([sx, cx], axis=2)
    to_modes_x = np.stack([real, imag], axis=2).reshape(ROWS, 128, 2 * SIDE) / math.sqrt(NX)
    real = np.stack([cos_x, -sin_x], axis=-1).reshape(ROWS, SIDE, 128)
    imag = np.stack([sin_x, cos_x], axis=-1).reshape(ROWS, SIDE, 128)
    to_cells_x = np.concatenate([real, imag], axis=1) / math.sqrt(MX)

    def rounded(t):
        return np.ascontiguousarray(t).astype(ml_dtypes.bfloat16)

    def rest(t):
        return rounded(t - rounded(t).astype(np.float64))

    high, low = rounded(to_modes_x), rest(to_modes_x)
    wide_modes_x = np.concatenate([high, low, high], axis=2)
    wide_cells_x = np.concatenate([rounded(to_cells_x), rest(to_cells_x)], axis=2)
    return rounded(to_modes_y), rounded(to_cells_y), wide_modes_x, wide_cells_x


def iota(shape, axis):
    return lax.broadcasted_iota(jnp.int32, shape, axis)


def dot(a, b):
    return jnp.dot(a, b, preferred_element_type=F32)


def dot_tb(a, b):
    return lax.dot_general(a, b, (((1,), (1,)), ((), ())), preferred_element_type=F32)


def dot_ta(a, b):
    return lax.dot_general(a, b, (((0,), (0,)), ((), ())), preferred_element_type=F32)


def over_80(v):
    return (v * 52429) >> 22


def over_20(v):
    return (v * 52429) >> 20


def build_to_modes(table, big_ref):
    lane = iota((SIDE, 640), 1)
    tile = (lane - 80 * over_80(lane) == iota((SIDE, 640), 0)).astype(F32).astype(BF)
    for part in range(8):
        rep = ((iota((128, 128), 0) >> 3) + 16 * part == iota((128, 128), 1)).astype(F32)
        rows = dot(dot(rep.astype(BF), table).astype(BF), tile)
        mask = (iota((128, 640), 0) & 7) == over_80(iota((128, 640), 1))
        big_ref[pl.ds(128 * part, 128), :] = jnp.where(mask, rows, 0.0).astype(BF)


def build_to_cells(table, big_ref):
    rep = ((iota((128, 1024), 1) >> 3) == iota((128, 1024), 0)).astype(F32)
    wide = dot(table, rep.astype(BF))
    lane = iota((SIDE, 1024), 1) & 7
    for x in range(8):
        big_ref[pl.ds(SIDE * x, SIDE), :] = jnp.where(lane == x, wide, 0.0).astype(BF)


def x_to_modes(table, ay_ref, kys):
    wide = []
    for ky in kys:
        both = [ay_ref[:, 2 * ky + r].reshape(SIDE, C) for r in range(2)]
        high = [v.astype(BF) for v in both]
        low = [(v - h.astype(F32)).astype(BF) for v, h in zip(both, high)]
        wide.append(jnp.concatenate(high + high + low, axis=0))
    modes = dot(table, jnp.concatenate(wide, axis=1)).astype(BF)
    return modes[:, :C], modes[:, C:]


def x_to_cells(table, z_ref, p_ref):
    def step(pair, carry):
        wide = jnp.concatenate([z_ref[2 * pair], z_ref[2 * pair + 1]], axis=1)
        cells = dot(table, jnp.concatenate([wide, wide], axis=0))
        for h in range(2):
            for r in range(2):
                piece = cells[r * SIDE : (r + 1) * SIDE, h * C : (h + 1) * C]
                p_ref[:, 2 * (2 * pair + h) + r] = piece.reshape(10, 8, C)
        return carry

    lax.fori_loop(0, 32, step, 0, unroll=16)


def y_store(big, pair_cells, ay_ref, pair):
    for part in range(4):
        modes = dot(big[pl.ds(256 * part, 256)], pair_cells)
        spot = pl.ds(32 * part, 32)
        ay_ref[2 * pair, spot] = modes[:, :C].reshape(32, 8, C)
        ay_ref[2 * pair + 1, spot] = modes[:, C:].reshape(32, 8, C)


def y_to_modes(big, field, ay):
    def y_step(pair, carry):
        first = field[pl.ds(16 * pair, 8)].reshape(640, C)
        second = field[pl.ds(16 * pair + 8, 8)].reshape(640, C)
        y_store(big, jnp.concatenate([first, second], axis=1), ay, pair)
        return carry

    lax.fori_loop(0, 5, y_step, 0)


def start_of(pick):
    depth = pick & 3
    first, second = (pick >> 2) & 127, pick >> 9

    def choose(zero, one, two):
        return jnp.where(depth == 0, zero, jnp.where(depth == 1, one, two))

    last = choose(SIDE - BLK, SIDE // 2 - BLK, 0)
    sx = jnp.minimum(choose(first, first >> 1, first >> 2), last)
    sy = jnp.minimum(choose(second, second >> 1, second >> 2), last)
    return depth, sx, sy


def pick_of(picks, row, col, d):
    target = lax.rem(row - STEP_ROWS[d] + ROWS, ROWS) * COLS
    return picks[target + lax.rem(col - STEP_COLS[d] + COLS, COLS), d]


def pick_blocks(picks, row, col, field, grid, tmp, blocks):
    def widen(x, carry):
        grid[x, pl.ds(0, SIDE)] = field[x].astype(F32)
        return carry

    lax.fori_loop(0, SIDE, widen, 0, unroll=4)

    def pool1(x, carry):
        total = jnp.zeros((40, C), F32)
        for a in range(2):
            for b in range(2):
                total = total + grid[2 * x + a, pl.ds(b, 40, stride=2)]
        grid[SIDE + x, pl.ds(0, 40)] = (total * 0.25).astype(BF).astype(F32)
        return carry

    lax.fori_loop(0, 40, pool1, 0, unroll=4)

    def pool2(x, carry):
        total = jnp.zeros((20, C), F32)
        for a in range(4):
            for b in range(4):
                total = total + grid[4 * x + a, pl.ds(b, 20, stride=4)]
        grid[SIDE + 40 + x, pl.ds(0, 20)] = (total * 0.0625).astype(BF).astype(F32)
        return carry

    lax.fori_loop(0, 20, pool2, 0, unroll=4)
    for d in range(8):
        depth, sx, sy = start_of(pick_of(picks, row, col, d))
        base = sx + jnp.where(depth == 0, 0, jnp.where(depth == 1, SIDE, SIDE + 40))
        for a in range(BLK):
            tmp[pl.ds(BLK * a, 24)] = grid[base + a, pl.ds(sy, 24)]
        blocks[d] = tmp[pl.ds(0, 400)].astype(BF)


def exchange_kernel(back, *refs):
    refs = list(refs)

    def take(n):
        taken = refs[:n]
        del refs[:n]
        return taken

    if back:
        cells_in = take(10)
        tx, big_in, w = take(3)
        layer_out, pre_out, z, bo, u, to = take(6)
    else:
        picks, field, ty, tx, w = take(5)
        z, bo, u, big_out = take(4)
    r0, sa, sb, r1a, r1b, acca, accb, r2a, r2b, ab, r3, zs, zz, za, zb, wv = take(16)
    core_a, core_b, one_a, one_b, two_a, two_b, three, wide3 = take(8)
    wide2_a, wide2_b, wide1_a, wide1_b, share_a, share_b, blocks, local = take(8)
    if back:
        t0, t1s, t1, t2s, t2, t3s, t3, tall = take(8)
        core_t, one_t, two_t, three_t, wide2_t, wide1_t, share_t = take(7)
        s, b, big, ay, tx_own, t = take(6)
        step = pl.program_id(0)
    else:
        s, b, big, ay, tx_own, grid, tmp, ty_own = take(8)
    i, j = lax.axis_index("px"), lax.axis_index("py")
    y, zh = i // 2, i % 2
    zl, x, c = j // 8, (j // 2) % 4, j % 2
    spot = 2 * zl + zh
    sibling = (i, 8 * zl + 2 * x + 1 - c)

    def at_x(n):
        return (i, 8 * zl + 2 * n + c)

    def at_y(n):
        return (2 * n + zh, j)

    def at_z(n):
        return (2 * y + n % 2, 8 * (n // 2) + 2 * x + c)

    def remote(src, dst, sems, sent, landed, device):
        return pltpu.make_async_remote_copy(
            src_ref=src,
            dst_ref=dst,
            send_sem=sems.at[0, sent],
            recv_sem=sems.at[1, landed],
            device_id=device,
            device_id_type=MESH,
        )

    def neighbour(d, sign):
        return (
            (i + sign * STEP_ROWS[d] + ROWS) % ROWS,
            (j + sign * STEP_COLS[d] + COLS) % COLS,
        )

    def band(n, size=32):
        return pl.ds(pl.multiple_of(n * size, size), size)

    barrier = pltpu.get_barrier_semaphore()
    partners = [sibling]
    for r in (1, 2, 3):
        partners += [at_x((x + r) % 4), at_y((y + r) % 4), at_z((spot + r) % 4)]
    partners += [neighbour(d, 1) for d in range(8)]
    weights = pltpu.make_async_copy(w, wv, local.at[0])
    table_x = pltpu.make_async_copy(tx.at[i], tx_own, local.at[4])
    if back:
        keep = pltpu.make_async_copy(big_in, big, local.at[5])
    else:
        keep = pltpu.make_async_copy(big, big_out, local.at[5])

    def greet():
        for device in partners:
            pl.semaphore_signal(barrier, inc=1, device_id=device, device_id_type=MESH)
        weights.start()
        table_x.start()

    if back:

        @pl.when(step == 0)
        def _():
            keep.start()
            greet()

        tail = cells_body(
            step, i, j, keep, cells_in, layer_out, pre_out, ay, big, b, t, refs
        )
    else:
        greet()
        table_y = pltpu.make_async_copy(ty.at[j], ty_own, local.at[3])
        table_y.start()
        pick_blocks(picks, i, j, field, grid, tmp, b)

    def run():
        pl.semaphore_wait(barrier, len(partners))
        waits = []

        def begin(copy):
            copy.start()
            waits.append(copy)

        def core_copy_a(n):
            return remote(s.at[:, n, 1 - c, 0:2], r0.at[:, n, 0:2], core_a, n, n, sibling)

        def core_copy_b(n):
            src = s.at[:, :, 1 - c, 2:4, band(n)]
            return remote(src, r0.at[:, :, 2:4, band(n)], core_b, n, n, sibling)

        def block_copy(d):
            device = neighbour(d, 1 if back else -1)
            return remote(b.at[d], bo.at[d], blocks, d, d, device)

        def fill(n, half):
            def step(m, carry):
                a, e = m // 2, m % 2
                ky = 4 * (8 * a + 2 * n + e) + 2 * half
                first, second = x_to_modes(tx_own[...], ay, (ky, ky + 1))
                s[a, n, e, 2 * half] = first
                s[a, n, e, 2 * half + 1] = second
                return carry

            lax.fori_loop(0, 4, step, 0, unroll=4)

        if not back:
            for d in range(8):
                begin(block_copy(d))
            table_y.wait()
            build_to_modes(ty_own[...], big)
            keep.start()
            y_to_modes(big, field, ay)
        table_x.wait()
        for r in (2, 1, 3, 0):
            n = (x + r) % 4
            fill(n, 0)
            begin(core_copy_a(n))
        if back:

            def core_copy_t():
                return remote(t.at[1 - c], t0, core_t, 0, 0, sibling)

        def one_copy_a(n, slot, device):
            return remote(sa.at[n], r1a.at[slot], one_a, n, slot, device)

        def one_copy_b(n, slot, device):
            return remote(sb.at[n], r1b.at[slot], one_b, n, slot, device)

        def sum_a(n):
            core_copy_a(n).wait_recv()
            return s[:, n, c, 0:2].astype(F32) + r0[:, n, 0:2].astype(F32)

        def sum_b(n):
            core_copy_b(n).wait_recv()
            rows = band(n)
            return s[:, :, c, 2:4, rows].astype(F32) + r0[:, :, 2:4, rows].astype(F32)

        def pass_a(r):
            n = (x + r) % 4
            sa[n] = sum_a(n).astype(BF)
            begin(one_copy_a(n, x, at_x(n)))

        def pass_b(r):
            n = (y + r) % 4
            sb[n] = sum_b(n).astype(BF)
            begin(one_copy_b(n, y, at_y(n)))

        for r in (2, 1, 3, 0):
            fill((x + r) % 4, 1)
            if r:
                pass_a(r)
        for r in (2, 1, 3, 0):
            begin(core_copy_b((y + r) % 4))
        for r in (2, 1, 3):
            pass_b(r)
        if back:
            tail()
            begin(core_copy_t())
            for d in range(8):
                begin(block_copy(d))
        acca[...] = sum_a(x)
        accb[...] = sum_b(y)
        if back:

            def one_copy_t(n, slot, device):
                return remote(t1s.at[n], t1.at[slot], one_t, n, slot, device)

            core_copy_t().wait_recv()
            t1s[...] = (t[c].astype(F32) + t0[...].astype(F32)).astype(BF)
            for r in (2, 1, 3):
                n = (x + r) % 4
                begin(one_copy_t(n, x, at_x(n)))
        for r in (1, 3, 2):
            n = (x + r) % 4
            one_copy_a(n, n, at_x(n)).wait_recv()
            acca[...] = acca[...] + r1a[n].astype(F32)

        def two_copy_a(n, slot, device):
            return remote(acca.at[:, :, band(n)], r2a.at[slot], two_a, n, slot, device)

        def two_copy_b(n, slot, device):
            return remote(accb.at[:, n], r2b.at[slot], two_b, n, slot, device)

        for r in (2, 1, 3):
            n = (y + r) % 4
            begin(two_copy_a(n, y, at_y(n)))
        for r in (1, 3, 2):
            n = (y + r) % 4
            one_copy_b(n, n, at_y(n)).wait_recv()
            accb[...] = accb[...] + r1b[n].astype(F32)
        for r in (2, 1, 3):
            n = (x + r) % 4
            begin(two_copy_b(n, x, at_x(n)))
        ab[:, 0:2] = acca[:, :, band(y)]
        ab[:, 2:4] = accb[:, x]
        for r in (1, 3, 2):
            n = (y + r) % 4
            two_copy_a(n, n, at_y(n)).wait_recv()
            ab[:, 0:2] = ab[:, 0:2] + r2a[n]
        for r in (1, 3, 2):
            n = (x + r) % 4
            two_copy_b(n, n, at_x(n)).wait_recv()
            ab[:, 2:4] = ab[:, 2:4] + r2b[n]

        def three_copy(n, slot, device):
            return remote(ab.at[n // 2, :, band(n % 2, 16)], r3.at[slot], three, n, slot, device)

        for r in (2, 1, 3):
            n = (spot + r) % 4
            begin(three_copy(n, spot, at_z(n)))
        if back:

            def two_copy_t(n, slot, device):
                return remote(t2s.at[n], t2.at[slot], two_t, n, slot, device)

            total = t1s[x].astype(F32)
            for r in (1, 3, 2):
                n = (x + r) % 4
                one_copy_t(n, n, at_x(n)).wait_recv()
                total = total + t1[n].astype(F32)
            t2s[...] = total.astype(BF)
            for r in (2, 1, 3):
                n = (y + r) % 4
                begin(two_copy_t(n, y, at_y(n)))
        u[...] = ab[zl, :, band(zh, 16)]
        for r in (1, 3, 2):
            n = (spot + r) % 4
            three_copy(n, n, at_z(n)).wait_recv()
            u[...] = u[...] + r3[n]
        if back:
            u[...] = u[...] * math.sqrt(NX * NY / (MX * MY))
        weights.wait()
        same = iota((16, 16), 0) ^ 1
        turn = jnp.where(iota((16, 16), 1) == same, 1.0, 0.0)
        odd = (iota((16, 16), 0) & 1) == 1
        flip = odd if back else jnp.logical_not(odd)
        turn = jnp.where(flip, -turn, turn).astype(BF)

        def mix(ky, carry):
            first = u[ky]
            high = first.astype(BF)
            low = (first - high.astype(F32)).astype(BF)
            both = jnp.concatenate([high, low], axis=0)
            turned = jnp.concatenate([dot(turn, high), dot(turn, low)], axis=0).astype(BF)
            both = jnp.concatenate([both, turned], axis=1)
            total = jnp.zeros((16, C), F32)
            for kx in range(8):
                if back:
                    mat = jnp.concatenate([wv[0, kx, ky], wv[1, kx, ky]], axis=1).astype(BF)
                    res = dot_tb(both, mat)
                else:
                    mat = jnp.concatenate([wv[0, kx, ky], wv[1, kx, ky]], axis=0).astype(BF)
                    res = dot(both, mat)
                total = jnp.where((iota((16, C), 0) >> 1) == kx, res[:16] + res[16:], total)
            zs[ky] = total.astype(BF)
            return carry

        lax.fori_loop(0, 4, mix, 0)

        def wide_copy3(slot, sent, device):
            dst = zz.at[slot // 2, :, band(slot % 2, 16)]
            return remote(zs, dst, wide3, sent, slot, device)

        for r in (2, 1, 3):
            n = (spot + r) % 4
            begin(wide_copy3(spot, n, at_z(n)))
        zz[zl, :, band(zh, 16)] = zs[...]
        if back:
            t3s[...] = t2s[y]
            total = t3s[...].astype(F32)
            for r in (1, 3, 2):
                n = (y + r) % 4
                two_copy_t(n, n, at_y(n)).wait_recv()
                total = total + t2[n].astype(F32)
            t3s[...] = total.astype(BF)
            t3[spot] = t3s[...]

            def three_copy_t(slot, sent, device):
                return remote(t3s, t3.at[slot], three_t, sent, slot, device)

            for r in (2, 1, 3):
                n = (spot + r) % 4
                begin(three_copy_t(spot, n, at_z(n)))
        for r in (1, 3, 2):
            n = (spot + r) % 4
            wide_copy3(n, n, at_z(n)).wait_recv()

        def wide_copy2_a(slot, sent, device):
            return remote(zz.at[:, 0:2], za.at[:, :, band(slot)], wide2_a, sent, slot, device)

        def wide_copy2_b(slot, sent, device):
            return remote(zz.at[:, 2:4], zb.at[:, slot], wide2_b, sent, slot, device)

        for r in (2, 1, 3):
            n = (y + r) % 4
            begin(wide_copy2_a(y, n, at_y(n)))
            n = (x + r) % 4
            begin(wide_copy2_b(x, n, at_x(n)))
        za[:, :, band(y)] = zz[:, 0:2]
        zb[:, x] = zz[:, 2:4]

        def part_a(n, core):
            return z.at[:, n, core, 0:2]

        def part_b(n, core):
            return z.at[:, :, core, 2:4, band(n)]

        def wide_copy1_a(slot, sent, device):
            return remote(za, part_a(slot, c), wide1_a, sent, slot, device)

        def wide_copy1_b(slot, sent, device):
            return remote(zb, part_b(slot, c), wide1_b, sent, slot, device)

        for r in (1, 3, 2):
            n = (y + r) % 4
            wide_copy2_a(n, n, at_y(n)).wait_recv()
        for r in (2, 1, 3):
            n = (x + r) % 4
            begin(wide_copy1_a(x, n, at_x(n)))
        for r in (1, 3, 2):
            n = (x + r) % 4
            wide_copy2_b(n, n, at_x(n)).wait_recv()
        for r in (2, 1, 3):
            n = (y + r) % 4
            begin(wide_copy1_b(y, n, at_y(n)))
        own_a = pltpu.make_async_copy(za, part_a(x, c), local.at[1])
        own_a.start()
        own_b = pltpu.make_async_copy(zb, part_b(y, c), local.at[2])
        own_b.start()
        begin(remote(za, part_a(x, c), share_a, x, x, sibling))
        begin(remote(zb, part_b(y, c), share_b, y, y, sibling))
        if back:
            for r in (1, 3, 2):
                n = (spot + r) % 4
                three_copy_t(n, n, at_z(n)).wait_recv()
            total = t3[0].astype(F32)
            for n in range(1, 4):
                total = total + t3[n].astype(F32)
            tall[x, y] = total.astype(BF)

            def wide_copy2_t(slot, sent, device):
                piece = tall.at[x, slot]
                return remote(piece, piece, wide2_t, sent, slot, device)

            for r in (2, 1, 3):
                n = (y + r) % 4
                begin(wide_copy2_t(y, n, at_y(n)))
            for r in (1, 3, 2):
                n = (y + r) % 4
                wide_copy2_t(n, n, at_y(n)).wait_recv()

            def wide_copy1_t(slot, sent, device):
                piece = tall.at[slot]
                return remote(piece, piece, wide1_t, sent, slot, device)

            for r in (2, 1, 3):
                n = (x + r) % 4
                begin(wide_copy1_t(x, n, at_x(n)))

        def share_copy_a(n, core):
            return remote(part_a(n, core), part_a(n, core), share_a, n, n, sibling)

        def share_copy_b(n, core):
            return remote(part_b(n, core), part_b(n, core), share_b, n, n, sibling)

        for r in (1, 3, 2):
            n = (x + r) % 4
            wide_copy1_a(n, n, at_x(n)).wait_recv()
            begin(share_copy_a(n, c))
            n = (y + r) % 4
            wide_copy1_b(n, n, at_y(n)).wait_recv()
            begin(share_copy_b(n, c))
        if back:
            for r in (1, 3, 2):
                n = (x + r) % 4
                wide_copy1_t(n, n, at_x(n)).wait_recv()
            share = remote(tall, to.at[c], share_t, 0, 0, sibling)
            begin(share)
            own_t = pltpu.make_async_copy(tall, to.at[c], local.at[3])
            own_t.start()
        for n in range(4):
            share_copy_a(n, 1 - c).wait_recv()
            share_copy_b(n, 1 - c).wait_recv()
        for d in range(8):
            block_copy(d).wait_recv()
        own_a.wait()
        own_b.wait()
        if back:
            share.wait_recv()
            own_t.wait()
        else:
            keep.wait()
        for copy in waits:
            copy.wait_send()

    if back:
        pl.when(step == 4)(run)
    else:
        run()


def whole(*shape):
    zeros = (0,) * len(shape)
    return pl.BlockSpec(shape, lambda n: zeros)


def exchange(back, *operands):
    shape = jax.ShapeDtypeStruct
    out_shape = [shape((2, 4, 2, 4, 128, C), BF), shape((8, 400, C), BF), shape((4, 16, C), F32)]
    if back:
        tile = pl.BlockSpec((16, SIDE, C), lambda n: (n, 0, 0))
        field = shape((SIDE, SIDE, C), BF)
        out_shape = [field, field] + out_shape + [shape((2, 4, 4, PIECE, C), BF)]
        out_specs = [tile, tile, HB, HB, whole(4, 16, C), HB]
        in_specs = [tile, tile, whole(64, 128, C), whole(8, 400, C), whole(C, C)]
        in_specs += [whole(8, C, C), whole(C, H), whole(H, C), whole(COLS, SIDE, 128)]
        in_specs += [whole(ROWS, 160, 256), HB, HB, HB]
    else:
        out_shape.append(shape((1024, 640), BF))
        out_specs = [HB, HB, VM, HB]
        in_specs = [SM, VM, HB, HB, HB]
    sem = pltpu.SemaphoreType.DMA((2, 4))
    scratch = [
        pltpu.VMEM((2, 4, 4, 128, C), BF),
        pltpu.VMEM((4, 2, 2, 128, C), BF),
        pltpu.VMEM((4, 2, 4, 2, 32, C), BF),
        pltpu.VMEM((4, 2, 2, 128, C), BF),
        pltpu.VMEM((4, 2, 4, 2, 32, C), BF),
        pltpu.VMEM((2, 2, 128, C), F32),
        pltpu.VMEM((2, 4, 2, 32, C), F32),
        pltpu.VMEM((4, 2, 2, 32, C), F32),
        pltpu.VMEM((4, 2, 2, 32, C), F32),
        pltpu.VMEM((2, 4, 32, C), F32),
        pltpu.VMEM((4, 4, 16, C), F32),
        pltpu.VMEM((4, 16, C), BF),
        pltpu.VMEM((2, 4, 32, C), BF),
        pltpu.VMEM((2, 2, 128, C), BF),
        pltpu.VMEM((2, 4, 2, 32, C), BF),
        pltpu.VMEM((2, 8, 4, C, C), F32),
    ]
    scratch += [sem] * 14 + [pltpu.SemaphoreType.DMA((2, 8)), pltpu.SemaphoreType.DMA((6,))]
    if back:
        scratch += [
            pltpu.VMEM((4, 4, PIECE, C), BF),
            pltpu.VMEM((4, 4, PIECE, C), BF),
            pltpu.VMEM((4, 4, PIECE, C), BF),
            pltpu.VMEM((4, PIECE, C), BF),
            pltpu.VMEM((4, PIECE, C), BF),
            pltpu.VMEM((PIECE, C), BF),
            pltpu.VMEM((4, PIECE, C), BF),
            pltpu.VMEM((4, 4, PIECE, C), BF),
        ] + [sem] * 7
    scratch += [
        pltpu.VMEM((2, 4, 2, 4, 128, C), BF),
        pltpu.VMEM((8, 400, C), BF),
        pltpu.VMEM((1024, 640), BF),
        pltpu.VMEM((10, 128, 8, C), F32),
        pltpu.VMEM((128, 480), BF),
    ]
    if back:
        scratch += [
            pltpu.VMEM((2, 4, 4, PIECE, C), BF),
            pltpu.VMEM((10, 128, 8, C), F32),
            pltpu.VMEM((640, 1024), BF),
            pltpu.VMEM((1280, 160), BF),
            pltpu.VMEM((80, 1280), BF),
            pltpu.VMEM((400, C), F32),
            pltpu.VMEM((400, C), F32),
            pltpu.VMEM((1280, C), F32),
            pltpu.VMEM((1280, C), F32),
            pltpu.VMEM((1280, C), BF),
            pltpu.VMEM((1280, H), F32),
            pltpu.VMEM((1280, H), F32),
            pltpu.VMEM((1280, H), BF),
            pltpu.VMEM((1280, H), BF),
            pltpu.VMEM((C, C), F32),
            pltpu.VMEM((C, H), F32),
            pltpu.VMEM((C, H), F32),
        ]
    else:
        scratch += [
            pltpu.VMEM((SIDE + 60, 88, C), F32),
            pltpu.VMEM((408, C), F32),
            pltpu.VMEM((128, SIDE), BF),
        ]
    return pl.pallas_call(
        functools.partial(exchange_kernel, back),
        out_shape=tuple(out_shape),
        in_specs=in_specs,
        out_specs=tuple(out_specs),
        scratch_shapes=scratch,
        grid=(5,) if back else (),
        compiler_params=pltpu.CompilerParams(
            collective_id=2 if back else 1,
            has_side_effects=True,
            vmem_limit_bytes=VMEM_LIMIT,
        ),
        name="cells_and_exchange" if back else "forward_and_exchange",
    )(*operands)


def gelu_both(v):
    square = v * v
    t = jnp.tanh(v * (TANH_SCALE + (TANH_SCALE * CUBIC_TERM) * square))
    half = 0.5 + 0.5 * t
    inner = (0.5 * TANH_SCALE) + (1.5 * TANH_SCALE * CUBIC_TERM) * square
    return v * half, half + v * (1.0 - t * t) * inner


def store_rows(tot, first, rows):
    done = 0
    while done < rows.shape[0]:
        place, inside = divmod(first + done, PIECE)
        count = min(PIECE - inside, rows.shape[0] - done)
        spot = (place // 16, place // 4 % 4, place % 4)
        tot[spot + (pl.ds(inside, count),)] = rows[done : done + count]
        done += count


def cells_body(step, row, col, keep, inputs, layer, pre_out, ay, big, bgrad, tot, scratch):
    field, cot, z, blk, skip, ctx, up, down, gy, gx = inputs
    p, cells_big, spread, gather, coarse, cell, pre, slope, mid = scratch[:9]
    lifted, dh, hid, lg, acc_skip, acc_up, acc_down = scratch[9:]

    @pl.when(step == 0)
    def _():
        x_to_cells(gx[row], z, p)
        build_to_cells(gy[col], cells_big)
        total = dot(blk[0], ctx[0])
        for d in range(1, 8):
            total = total + dot(blk[d], ctx[d])
        coarse[...] = total
        n, l = iota((1280, 160), 0), iota((1280, 160), 1)
        l = jnp.where(l >= 80, l - 80, l)
        x = over_80(n)
        y = n - 80 * x
        a = over_20(l)
        hit = ((x >> 2) == a) & ((y >> 2) == l - 20 * a)
        spread[...] = jnp.where(hit, 1.0, 0.0).astype(BF)
        l, n = iota((80, 1280), 0), iota((80, 1280), 1)
        x = over_80(n)
        y = n - 80 * x
        a = over_20(l)
        hit = ((x >> 2) == a) & ((y >> 2) == l - 20 * a)
        gather[...] = jnp.where(hit, 1.0, 0.0).astype(BF)
        acc_skip[...] = jnp.zeros_like(acc_skip)
        acc_up[...] = jnp.zeros_like(acc_up)
        acc_down[...] = jnp.zeros_like(acc_down)

    own_rows = pl.ds(pl.multiple_of(80 * step, 8), 80)
    flat = field[...].reshape(1280, C)
    flat_cot = cot[...].reshape(1280, C)
    wide = jnp.concatenate(
        [p[2 * step].reshape(1024, C).astype(BF), p[2 * step + 1].reshape(1024, C).astype(BF)],
        axis=1,
    )
    own = coarse[own_rows]
    high = own.astype(BF)
    low = (own - high.astype(F32)).astype(BF)
    rest = dot(flat, skip[...]) + dot(spread[...], jnp.concatenate([high, low], axis=0))
    for part in range(640 // 160):
        lo, hi = 160 * part, 160 * part + 160
        spectral = dot(cells_big[pl.ds(lo, 160)], wide)
        pre[pl.ds(lo, 160)] = spectral[:, :C].astype(BF).astype(F32) + rest[lo:hi]
        pre[pl.ds(640 + lo, 160)] = spectral[:, C:].astype(BF).astype(F32) + rest[640 + lo : 640 + hi]

    def activate(n, carry):
        rows = pl.ds(pl.multiple_of(64 * n, 64), 64)
        value, slant = gelu_both(pre[rows])
        mid[rows] = value.astype(BF)
        slope[rows] = slant
        return carry

    lax.fori_loop(0, 20, activate, 0, unroll=20)
    lifted[...] = dot(mid[...], up[...])
    dh[...] = dot_tb(flat_cot, down[...])

    def activate_wide(n, carry):
        rows = pl.ds(pl.multiple_of(16 * n, 16), 16)
        value, slant = gelu_both(lifted[rows])
        hid[rows] = value.astype(BF)
        lg[rows] = (dh[rows] * slant).astype(BF)
        return carry

    lax.fori_loop(0, 80, activate_wide, 0, unroll=80)
    result = mid[...].astype(F32) + dot(hid[...], down[...])
    layer[...] = result.astype(BF).reshape(16, SIDE, C)
    grad = flat_cot.astype(F32) + dot_tb(lg[...], up[...])
    grad = (grad * slope[...]).astype(BF)
    pre_out[...] = grad.reshape(16, SIDE, C)
    acc_skip[...] += dot_ta(flat, grad)
    acc_up[...] += dot_ta(mid[...], lg[...])
    acc_down[...] += dot_ta(flat_cot, hid[...])
    cell[own_rows] = dot(gather[...], grad)
    pl.when(step == 0)(keep.wait)
    y_store(big, jnp.concatenate([grad[:640], grad[640:]], axis=1), ay, step)

    def tail():
        narrow = cell[...].astype(BF)
        store_rows(tot, 0, acc_skip[...].astype(BF))
        for d in range(8):
            store_rows(tot, 128 + 128 * d, dot_ta(blk[d], narrow).astype(BF))
            bgrad[d] = dot_tb(narrow, ctx[d]).astype(BF)
        for part in range(4):
            cut = slice(128 * part, 128 * part + 128)
            store_rows(tot, 1152 + 128 * part, acc_up[:, cut].astype(BF))
            store_rows(tot, 1664 + 128 * part, acc_down[:, cut].T.astype(BF))
        store_rows(tot, 2176, jnp.zeros((TOT - 2176, C), BF))

    return tail


def outer(u, g, spec):
    turn = jnp.where(iota((16, 16), 1) == (iota((16, 16), 0) ^ 1), 1.0, 0.0)
    turn = jnp.where((iota((16, 16), 0) & 1) == 1, -turn, turn).astype(BF)
    left_high = u.astype(BF)
    left_low = (u - left_high.astype(F32)).astype(BF)
    right_high = g.astype(BF)
    right_low = (g - right_high.astype(F32)).astype(BF)
    high = jnp.concatenate([right_high, dot(turn, right_high).astype(BF)], axis=1)
    low = jnp.concatenate([right_low, dot(turn, right_low).astype(BF)], axis=1)
    lefts = jnp.concatenate([left_high, left_high, left_low], axis=0).astype(F32).T.astype(BF)
    rights = jnp.concatenate([high, low, high], axis=0)
    row = (iota((48, 2 * C), 0) & 15) >> 1
    for kx in range(8):
        res = dot(lefts, jnp.where(row == kx, rights, jnp.zeros_like(rights)))
        spec[0, kx, 0] = res[:, :C]
        spec[1, kx, 0] = res[:, C:]


def weight_sums(tot, skip, ctx, up, down):
    inv = 1.0 / math.sqrt(NX * NY)
    skip[...] = tot[pl.ds(0, 128)].astype(F32) * inv
    for d in range(8):
        ctx[d] = tot[pl.ds(128 + 128 * d, 128)].astype(F32) * inv
    for part in range(4):
        cut = slice(128 * part, 128 * part + 128)
        up[:, cut] = tot[pl.ds(1152 + 128 * part, 128)].astype(F32) * inv
    down[...] = tot[pl.ds(1664, 512)].astype(F32) * inv


def last_kernel(
    picks, pre, z, back, skip, gy, gx, u, g, tot,
    out, spec, skip_out, ctx_out, up_out, down_out, p, cells_big, place, grads, wide,
):
    step = pl.program_id(0)
    row, col = lax.axis_index("px"), lax.axis_index("py")
    starts = [start_of(pick_of(picks, row, col, d)) for d in range(8)]

    @pl.when(step == 0)
    def _():
        x_to_cells(gx[row], z, p)
        build_to_cells(gy[col], cells_big)
        y, lane = iota((SIDE, 192), 0), iota((SIDE, 192), 1)
        total = jnp.zeros((SIDE, 192), F32)
        for d in range(8):
            depth, sx, sy = starts[d]
            share = jnp.where(depth == 0, 1.0, jnp.where(depth == 1, 0.25, 0.0625))
            spot = lane - 24 * d
            line = jnp.where(depth == 0, y, jnp.where(depth == 1, y >> 1, y >> 2))
            hit = (spot >= 0) & (spot < BLK) & (line - sy == spot)
            total = jnp.where(hit, share, total)
        place[...] = total.astype(BF)
        wide[pl.ds(400, 8)] = jnp.zeros((8, C), F32)
        for d in range(8):
            wide[pl.ds(0, 400)] = back[d].astype(F32)
            for a in range(BLK):
                grads[d, a] = wide[pl.ds(BLK * a, 24)]
            grads[d, BLK] = jnp.zeros((24, C), F32)

    @pl.when(step < 4)
    def _():
        outer(u[step], g[step], spec)

    pl.when(step == 4)(lambda: weight_sums(tot, skip_out, ctx_out, up_out, down_out))
    both = jnp.concatenate(
        [p[2 * step].reshape(1024, C).astype(BF), p[2 * step + 1].reshape(1024, C).astype(BF)],
        axis=1,
    )
    factor = math.sqrt(MX * MY / (NX * NY))
    straight = dot_tb(pre[...].reshape(1280, C), skip[...])
    for k in range(8):
        spectral = dot(cells_big[pl.ds(SIDE * k, SIDE)], both) * factor
        wide_pieces = []
        for x in (k, k + 8):
            pieces = []
            for d in range(8):
                depth, sx, sy = starts[d]
                a = ((16 * step + x) >> depth) - sx
                a = jnp.where((a >= 0) & (a < BLK), a, BLK)
                pieces.append(grads[d, a])
            wide_pieces.append(jnp.concatenate(pieces, axis=0).astype(BF))
        total = spectral + dot(place[...], jnp.concatenate(wide_pieces, axis=1))
        out[k] = (total[:, :C] + straight[80 * k : 80 * k + 80]).astype(BF)
        x = k + 8
        out[x] = (total[:, C:] + straight[80 * x : 80 * x + 80]).astype(BF)


def last_call(picks, pre, z, back, skip, gy, gx, u, g, tot):
    tile = pl.BlockSpec((16, SIDE, C), lambda n: (n, 0, 0))
    shape = jax.ShapeDtypeStruct
    return pl.pallas_call(
        last_kernel,
        grid=(5,),
        out_shape=(
            shape((SIDE, SIDE, C), BF),
            shape((2, 8, 4, C, C), F32),
            shape((C, C), F32),
            shape((8, C, C), F32),
            shape((C, H), F32),
            shape((H, C), F32),
        ),
        in_specs=[
            SM, tile, whole(64, 128, C), whole(8, 400, C), whole(C, C),
            whole(COLS, SIDE, 128), whole(ROWS, 160, 256), whole(4, 16, C), whole(4, 16, C),
            whole(TOT, C),
        ],
        out_specs=(
            tile,
            pl.BlockSpec((2, 8, 1, C, C), lambda n: (0, 0, jnp.minimum(n, 3), 0, 0)),
            whole(C, C),
            whole(8, C, C),
            whole(C, H),
            whole(H, C),
        ),
        scratch_shapes=[
            pltpu.VMEM((10, 128, 8, C), F32),
            pltpu.VMEM((640, 1024), BF),
            pltpu.VMEM((SIDE, 192), BF),
            pltpu.VMEM((8, BLK + 1, 24, C), F32),
            pltpu.VMEM((408, C), F32),
        ],
        compiler_params=pltpu.CompilerParams(vmem_limit_bytes=VMEM_LIMIT),
        name="field_gradient",
    )(picks, pre, z, back, skip, gy, gx, u, g, tot)


def shards(
    flow_field, cotangent, spec_weight, skip_weight, ctx_weight, up_weight, down_weight,
    ctx_level, ctx_offset,
):
    ty, gy, tx, gx = (jnp.asarray(t) for t in wave_tables())
    picks = ctx_level + (ctx_offset[:, :, 0] << 2) + (ctx_offset[:, :, 1] << 9)
    z, arrived, u, big = exchange(False, picks, flow_field, ty, tx, spec_weight)
    layer, pre, z, back, g, tot = exchange(
        True, flow_field, cotangent, z.reshape(64, 128, C), arrived, skip_weight, ctx_weight,
        up_weight, down_weight, gy, gx, tx, big, spec_weight,
    )
    grad, spec, skip, ctx, up, down = last_call(
        picks, pre, z.reshape(64, 128, C), back, skip_weight, gy, gx, u, g, tot.reshape(TOT, C)
    )
    return layer, grad, spec, skip, ctx, up, down


def solution(mesh):
    return jax.shard_map(
        shards,
        mesh=mesh,
        in_specs=(
            P("px", "py", None),
            P("px", "py", None),
            P(None, "px", "py", None, None),
            P(),
            P(),
            P(),
            P(),
            P(),
            P(),
        ),
        out_specs=(
            P("px", "py", None),
            P("px", "py", None),
            P(None, "px", "py", None, None),
            P(),
            P(),
            P(),
            P(),
        ),
        check_vma=False,
    )
```

```python
import math

import jax
import jax.numpy as jnp
import ml_dtypes
import numpy as np
from jax import lax
from jax.experimental import pallas as pl
from jax.experimental.pallas import tpu as pltpu
from jax.sharding import PartitionSpec as P

BF = jnp.bfloat16
F32 = jnp.float32
TANH_SCALE = 0.7978845608028654
CUBIC_TERM = 0.044715
STEP_ROWS = (-1, -1, -1, 0, 0, 1, 1, 1)
STEP_COLS = (-1, 0, 1, -1, 1, -1, 0, 1)
ROWS, COLS = 8, 16
SIDE, C, H, BLK = 80, 128, 512, 20
NX, NY, MX, MY = 640, 1280, 64, 64
PIECE = 80
TOT = 32 * PIECE
VMEM_LIMIT = 56 * 1024 * 1024
MESH = pl.DeviceIdType.MESH
VM = pl.BlockSpec(memory_space=pltpu.VMEM)
SM = pl.BlockSpec(memory_space=pltpu.SMEM)
HB = pl.BlockSpec(memory_space=pl.ANY)


def wave_tables():
    waves = np.arange(64) - 32

    def parts(length, side):
        turns = (np.arange(length)[:, None] * waves[None, :]) % length
        phase = turns * (2.0 * math.pi / length)
        return np.cos(phase).reshape(-1, side, 64), np.sin(phase).reshape(-1, side, 64)

    cos_y, sin_y = parts(NY, SIDE)
    cos_x, sin_x = parts(NX, SIDE)
    to_modes_y = np.stack([cos_y, -sin_y], axis=-1).reshape(COLS, SIDE, 128) / math.sqrt(NY)
    to_modes_y = to_modes_y.transpose(0, 2, 1)
    to_cells_y = np.stack([cos_y, -sin_y], axis=-1).reshape(COLS, SIDE, 128) / math.sqrt(MY)
    cx, sx = cos_x.transpose(0, 2, 1), -sin_x.transpose(0, 2, 1)
    real = np.concatenate([cx, -sx], axis=2)
    imag = np.concatenate([sx, cx], axis=2)
    to_modes_x = np.stack([real, imag], axis=2).reshape(ROWS, 128, 2 * SIDE) / math.sqrt(NX)
    real = np.stack([cos_x, -sin_x], axis=-1).reshape(ROWS, SIDE, 128)
    imag = np.stack([sin_x, cos_x], axis=-1).reshape(ROWS, SIDE, 128)
    to_cells_x = np.concatenate([real, imag], axis=1) / math.sqrt(MX)

    def rounded(t):
        return np.ascontiguousarray(t).astype(ml_dtypes.bfloat16)

    def rest(t):
        return rounded(t - rounded(t).astype(np.float64))

    high, low = rounded(to_modes_x), rest(to_modes_x)
    wide_modes_x = np.concatenate([high, low, high], axis=2)
    wide_cells_x = np.concatenate([rounded(to_cells_x), rest(to_cells_x)], axis=2)
    return rounded(to_modes_y), rounded(to_cells_y), wide_modes_x, wide_cells_x


def iota(shape, axis):
    return lax.broadcasted_iota(jnp.int32, shape, axis)


def dot(a, b):
    return jnp.dot(a, b, preferred_element_type=F32)


def dot_tb(a, b):
    return lax.dot_general(a, b, (((1,), (1,)), ((), ())), preferred_element_type=F32)


def dot_ta(a, b):
    return lax.dot_general(a, b, (((0,), (0,)), ((), ())), preferred_element_type=F32)


def over_80(v):
    return (v * 52429) >> 22


def over_20(v):
    return (v * 52429) >> 20


def build_to_modes(table, big_ref):
    lane = iota((SIDE, 640), 1)
    tile = (lane - 80 * over_80(lane) == iota((SIDE, 640), 0)).astype(F32).astype(BF)
    for part in range(8):
        rep = ((iota((128, 128), 0) >> 3) + 16 * part == iota((128, 128), 1)).astype(F32)
        rows = dot(dot(rep.astype(BF), table).astype(BF), tile)
        mask = (iota((128, 640), 0) & 7) == over_80(iota((128, 640), 1))
        big_ref[pl.ds(128 * part, 128), :] = jnp.where(mask, rows, 0.0).astype(BF)


def build_to_cells(table, big_ref):
    rep = ((iota((128, 1024), 1) >> 3) == iota((128, 1024), 0)).astype(F32)
    wide = dot(table, rep.astype(BF))
    lane = iota((SIDE, 1024), 1) & 7
    for x in range(8):
        big_ref[pl.ds(SIDE * x, SIDE), :] = jnp.where(lane == x, wide, 0.0).astype(BF)


def x_to_modes(table, ay_ref, kys):
    wide = []
    for ky in kys:
        both = [ay_ref[:, 2 * ky + r].reshape(SIDE, C) for r in range(2)]
        high = [v.astype(BF) for v in both]
        low = [(v - h.astype(F32)).astype(BF) for v, h in zip(both, high)]
        wide.append(jnp.concatenate(high + high + low, axis=0))
    modes = dot(table, jnp.concatenate(wide, axis=1)).astype(BF)
    return modes[:, :C], modes[:, C:]


def x_to_cells(table, z_ref, p_ref):
    def step(pair, carry):
        wide = jnp.concatenate([z_ref[2 * pair], z_ref[2 * pair + 1]], axis=1)
        cells = dot(table, jnp.concatenate([wide, wide], axis=0))
        for h in range(2):
            for r in range(2):
                piece = cells[r * SIDE : (r + 1) * SIDE, h * C : (h + 1) * C]
                p_ref[:, 2 * (2 * pair + h) + r] = piece.reshape(10, 8, C)
        return carry

    lax.fori_loop(0, 32, step, 0, unroll=16)


def y_store(big, pair_cells, ay_ref, pair):
    for part in range(4):
        modes = dot(big[pl.ds(256 * part, 256)], pair_cells)
        spot = pl.ds(32 * part, 32)
        ay_ref[2 * pair, spot] = modes[:, :C].reshape(32, 8, C)
        ay_ref[2 * pair + 1, spot] = modes[:, C:].reshape(32, 8, C)


def y_to_modes(big, field, ay):
    def y_step(pair, carry):
        first = field[pl.ds(16 * pair, 8)].reshape(640, C)
        second = field[pl.ds(16 * pair + 8, 8)].reshape(640, C)
        y_store(big, jnp.concatenate([first, second], axis=1), ay, pair)
        return carry

    lax.fori_loop(0, 5, y_step, 0)


def start_of(pick):
    depth = pick & 3
    first, second = (pick >> 2) & 127, pick >> 9

    def choose(zero, one, two):
        return jnp.where(depth == 0, zero, jnp.where(depth == 1, one, two))

    last = choose(SIDE - BLK, SIDE // 2 - BLK, 0)
    sx = jnp.minimum(choose(first, first >> 1, first >> 2), last)
    sy = jnp.minimum(choose(second, second >> 1, second >> 2), last)
    return depth, sx, sy


def pick_of(picks, row, col, d):
    target = lax.rem(row - STEP_ROWS[d] + ROWS, ROWS) * COLS
    return picks[target + lax.rem(col - STEP_COLS[d] + COLS, COLS), d]


def pick_blocks(picks, row, col, field, grid, tmp, blocks):
    def widen(x, carry):
        grid[x, pl.ds(0, SIDE)] = field[x].astype(F32)
        return carry

    lax.fori_loop(0, SIDE, widen, 0, unroll=4)

    def pool1(x, carry):
        total = jnp.zeros((40, C), F32)
        for a in range(2):
            for b in range(2):
                total = total + grid[2 * x + a, pl.ds(b, 40, stride=2)]
        grid[SIDE + x, pl.ds(0, 40)] = (total * 0.25).astype(BF).astype(F32)
        return carry

    lax.fori_loop(0, 40, pool1, 0, unroll=4)

    def pool2(x, carry):
        total = jnp.zeros((20, C), F32)
        for a in range(4):
            for b in range(4):
                total = total + grid[4 * x + a, pl.ds(b, 20, stride=4)]
        grid[SIDE + 40 + x, pl.ds(0, 20)] = (total * 0.0625).astype(BF).astype(F32)
        return carry

    lax.fori_loop(0, 20, pool2, 0, unroll=4)
    for d in range(8):
        depth, sx, sy = start_of(pick_of(picks, row, col, d))
        base = sx + jnp.where(depth == 0, 0, jnp.where(depth == 1, SIDE, SIDE + 40))
        for a in range(BLK):
            tmp[pl.ds(BLK * a, 24)] = grid[base + a, pl.ds(sy, 24)]
        blocks[d] = tmp[pl.ds(0, 400)].astype(BF)


def forward_kernel(*refs):
    refs = list(refs)

    def take(n):
        taken = refs[:n]
        del refs[:n]
        return taken

    picks, field, ty, tx, w = take(5)
    z, bo, u, big_out = take(4)
    r0, sa, sb, r1a, r1b, acca, accb, r2a, r2b, zs, za, zb, wv = take(13)
    core_a, core_b, one_a, one_b, wide1_a, wide1_b, share_a, share_b = take(8)
    two_a, two_b, wide2_a, wide2_b, blocks, local = take(6)
    s, b, big, ay, tx_own, grid, tmp, ty_own = take(8)
    i, j = lax.axis_index("px"), lax.axis_index("py")
    y, zh = i // 2, i % 2
    zl, x, c = j // 8, (j // 2) % 4, j % 2
    spot = 2 * zl + zh
    sibling = (i, 8 * zl + 2 * x + 1 - c)

    def at_x(n):
        return (i, 8 * zl + 2 * n + c)

    def at_y(n):
        return (2 * n + zh, j)

    def at_z(n):
        return (2 * y + n % 2, 8 * (n // 2) + 2 * x + c)

    def at_yz(n):
        return (2 * (n // 4) + n % 2, 8 * (n // 2 % 2) + 2 * x + c)

    def at_xz(n):
        return (2 * y + n % 2, 8 * (n // 2 % 2) + 2 * (n // 4) + c)

    def partner(base, r):
        return 4 * ((base + r // 4) % 4) + (spot + r % 4) % 4

    def sender(base, r):
        return 4 * ((base - r // 4 + 4) % 4) + (spot - r % 4 + 4) % 4

    def loop15(body):
        def step(r, carry):
            body(r)
            return carry

        lax.fori_loop(1, 16, step, 0)

    def remote(src, dst, sems, sent, landed, device):
        return pltpu.make_async_remote_copy(
            src_ref=src,
            dst_ref=dst,
            send_sem=sems.at[0, sent],
            recv_sem=sems.at[1, landed],
            device_id=device,
            device_id_type=MESH,
        )

    def neighbour(d, sign):
        return (
            (i + sign * STEP_ROWS[d] + ROWS) % ROWS,
            (j + sign * STEP_COLS[d] + COLS) % COLS,
        )

    def band(n, size=32):
        return pl.ds(pl.multiple_of(n * size, size), size)

    barrier = pltpu.get_barrier_semaphore()
    partners = [sibling]
    for r in range(1, 16):
        partners.append(at_yz(partner(y, r)))
        if r > 3:
            partners.append(at_xz(partner(x, r)))
    partners += [neighbour(d, 1) for d in range(8)]
    weights = pltpu.make_async_copy(w, wv, local.at[0])
    table_x = pltpu.make_async_copy(tx.at[i], tx_own, local.at[4])
    keep = pltpu.make_async_copy(big, big_out, local.at[5])

    def greet():
        for device in partners:
            pl.semaphore_signal(barrier, inc=1, device_id=device, device_id_type=MESH)
        weights.start()
        table_x.start()

    greet()
    table_y = pltpu.make_async_copy(ty.at[j], ty_own, local.at[3])
    table_y.start()
    pick_blocks(picks, i, j, field, grid, tmp, b)

    def run():
        pl.semaphore_wait(barrier, len(partners))
        waits = []

        def begin(copy):
            copy.start()
            waits.append(copy)

        def core_copy_a(n):
            return remote(s.at[:, n, 1 - c, 0:2], r0.at[:, n, 0:2], core_a, n, n, sibling)

        def core_copy_b(n):
            src = s.at[:, :, 1 - c, 2:4, band(n)]
            return remote(src, r0.at[:, :, 2:4, band(n)], core_b, n, n, sibling)

        def block_copy(d):
            device = neighbour(d, -1)
            return remote(b.at[d], bo.at[d], blocks, d, d, device)

        def fill(n, half):
            def step(m, carry):
                a, e = m // 2, m % 2
                ky = 4 * (8 * a + 2 * n + e) + 2 * half
                first, second = x_to_modes(tx_own[...], ay, (ky, ky + 1))
                s[a, n, e, 2 * half] = first
                s[a, n, e, 2 * half + 1] = second
                return carry

            lax.fori_loop(0, 4, step, 0, unroll=4)

        for d in range(8):
            begin(block_copy(d))
        table_y.wait()
        build_to_modes(ty_own[...], big)
        keep.start()
        y_to_modes(big, field, ay)
        table_x.wait()
        for r in (2, 1, 3, 0):
            n = (x + r) % 4
            fill(n, 0)
            begin(core_copy_a(n))
        def one_copy_a(n, slot, device):
            return remote(sa.at[n], r1a.at[slot], one_a, n, slot, device)

        def one_copy_b(n, slot, device):
            return remote(sb.at[n], r1b.at[slot], one_b, n, slot, device)

        def sum_a(n):
            core_copy_a(n).wait_recv()
            return s[:, n, c, 0:2].astype(F32) + r0[:, n, 0:2].astype(F32)

        def sum_b(n):
            core_copy_b(n).wait_recv()
            rows = band(n)
            return s[:, :, c, 2:4, rows].astype(F32) + r0[:, :, 2:4, rows].astype(F32)

        def pass_a(r):
            n = (x + r) % 4
            sa[n] = sum_a(n).astype(BF)
            begin(one_copy_a(n, x, at_x(n)))

        def pass_b(r):
            n = (y + r) % 4
            sb[n] = sum_b(n).astype(BF)
            begin(one_copy_b(n, y, at_y(n)))

        for r in (2, 1, 3, 0):
            fill((x + r) % 4, 1)
            if r:
                pass_a(r)
        for r in (2, 1, 3, 0):
            begin(core_copy_b((y + r) % 4))
        for r in (2, 1, 3):
            pass_b(r)
        acca[...] = sum_a(x)
        accb[...] = sum_b(y)
        for r in (1, 3, 2):
            n = (x + r) % 4
            one_copy_a(n, n, at_x(n)).wait_recv()
            acca[...] = acca[...] + r1a[n].astype(F32)

        def two_copy_a(n, slot, device):
            src = acca.at[n // 2 % 2, :, band(2 * (n // 4) + n % 2, 16)]
            return remote(src, r2a.at[slot], two_a, n, slot, device)

        def two_copy_b(n, slot, device):
            src = accb.at[n // 2 % 2, n // 4, :, band(n % 2, 16)]
            return remote(src, r2b.at[slot], two_b, n, slot, device)

        def send_two_a(r):
            n = partner(y, r)
            two_copy_a(n, 4 * y + spot, at_yz(n)).start()

        def send_two_b(r):
            n = partner(x, r)
            two_copy_b(n, 4 * x + spot, at_xz(n)).start()

        loop15(send_two_a)
        for r in (1, 3, 2):
            n = (y + r) % 4
            one_copy_b(n, n, at_y(n)).wait_recv()
            accb[...] = accb[...] + r1b[n].astype(F32)
        loop15(send_two_b)
        u[0:2] = acca[zl, :, band(i, 16)]
        u[2:4] = accb[zl, x, :, band(zh, 16)]

        def gather_two_a(r):
            n = sender(y, r)
            two_copy_a(n, n, at_yz(n)).wait_recv()
            u[0:2] = u[0:2] + r2a[n]

        def gather_two_b(r):
            n = sender(x, r)
            two_copy_b(n, n, at_xz(n)).wait_recv()
            u[2:4] = u[2:4] + r2b[n]

        loop15(gather_two_a)
        loop15(gather_two_b)
        weights.wait()
        same = iota((16, 16), 0) ^ 1
        turn = jnp.where(iota((16, 16), 1) == same, 1.0, 0.0)
        odd = (iota((16, 16), 0) & 1) == 1
        flip = jnp.logical_not(odd)
        turn = jnp.where(flip, -turn, turn).astype(BF)

        def mix(ky, carry):
            first = u[ky]
            high = first.astype(BF)
            low = (first - high.astype(F32)).astype(BF)
            both = jnp.concatenate([high, low], axis=0)
            turned = jnp.concatenate([dot(turn, high), dot(turn, low)], axis=0).astype(BF)
            both = jnp.concatenate([both, turned], axis=1)
            total = jnp.zeros((16, C), F32)
            for kx in range(8):
                mat = jnp.concatenate([wv[0, kx, ky], wv[1, kx, ky]], axis=0).astype(BF)
                res = dot(both, mat)
                total = jnp.where((iota((16, C), 0) >> 1) == kx, res[:16] + res[16:], total)
            zs[ky] = total.astype(BF)
            return carry

        lax.fori_loop(0, 4, mix, 0)

        def wide_copy2_a(slot, sent, device):
            dst = za.at[slot // 2 % 2, :, band(2 * (slot // 4) + slot % 2, 16)]
            return remote(zs.at[0:2], dst, wide2_a, sent, slot, device)

        def wide_copy2_b(slot, sent, device):
            dst = zb.at[slot // 2 % 2, slot // 4, :, band(slot % 2, 16)]
            return remote(zs.at[2:4], dst, wide2_b, sent, slot, device)

        def send_wide_a(r):
            n = partner(y, r)
            wide_copy2_a(4 * y + spot, n, at_yz(n)).start()

        def send_wide_b(r):
            n = partner(x, r)
            wide_copy2_b(4 * x + spot, n, at_xz(n)).start()

        loop15(send_wide_a)
        loop15(send_wide_b)
        za[zl, :, band(i, 16)] = zs[0:2]
        zb[zl, x, :, band(zh, 16)] = zs[2:4]
        def part_a(n, core):
            return z.at[:, n, core, 0:2]

        def part_b(n, core):
            return z.at[:, :, core, 2:4, band(n)]

        def wide_copy1_a(slot, sent, device):
            return remote(za, part_a(slot, c), wide1_a, sent, slot, device)

        def wide_copy1_b(slot, sent, device):
            return remote(zb, part_b(slot, c), wide1_b, sent, slot, device)

        def gather_wide_a(r):
            n = sender(y, r)
            wide_copy2_a(n, n, at_yz(n)).wait_recv()

        def gather_wide_b(r):
            n = sender(x, r)
            wide_copy2_b(n, n, at_xz(n)).wait_recv()

        loop15(gather_wide_a)
        for r in (2, 1, 3):
            n = (x + r) % 4
            begin(wide_copy1_a(x, n, at_x(n)))
        loop15(gather_wide_b)
        for r in (2, 1, 3):
            n = (y + r) % 4
            begin(wide_copy1_b(y, n, at_y(n)))
        own_a = pltpu.make_async_copy(za, part_a(x, c), local.at[1])
        own_a.start()
        own_b = pltpu.make_async_copy(zb, part_b(y, c), local.at[2])
        own_b.start()
        begin(remote(za, part_a(x, c), share_a, x, x, sibling))
        begin(remote(zb, part_b(y, c), share_b, y, y, sibling))
        def share_copy_a(n, core):
            return remote(part_a(n, core), part_a(n, core), share_a, n, n, sibling)

        def share_copy_b(n, core):
            return remote(part_b(n, core), part_b(n, core), share_b, n, n, sibling)

        for r in (1, 3, 2):
            n = (x + r) % 4
            wide_copy1_a(n, n, at_x(n)).wait_recv()
            begin(share_copy_a(n, c))
            n = (y + r) % 4
            wide_copy1_b(n, n, at_y(n)).wait_recv()
            begin(share_copy_b(n, c))
        for n in range(4):
            share_copy_a(n, 1 - c).wait_recv()
            share_copy_b(n, 1 - c).wait_recv()
        for d in range(8):
            block_copy(d).wait_recv()
        own_a.wait()
        own_b.wait()
        keep.wait()
        for copy in waits:
            copy.wait_send()

        def settle(r):
            n, m = partner(y, r), partner(x, r)
            two_copy_a(n, 4 * y + spot, at_yz(n)).wait_send()
            two_copy_b(m, 4 * x + spot, at_xz(m)).wait_send()
            wide_copy2_a(4 * y + spot, n, at_yz(n)).wait_send()
            wide_copy2_b(4 * x + spot, m, at_xz(m)).wait_send()

        loop15(settle)

    run()


def cells_kernel(*refs):
    refs = list(refs)

    def take(n):
        taken = refs[:n]
        del refs[:n]
        return taken

    cells_in = take(10)
    tx, big_in, w = take(3)
    layer_out, pre_out, z, bo, u, to = take(6)
    r0, sa, sb, r1a, r1b, acca, accb, r2a, r2b, ab, r3, zs, zz, za, zb, wv = take(16)
    core_a, core_b, one_a, one_b, two_a, two_b, three, wide3 = take(8)
    wide2_a, wide2_b, wide1_a, wide1_b, share_a, share_b, blocks, local = take(8)
    t0, t1s, t1, t2s, t2, t3s, t3, tall = take(8)
    core_t, one_t, two_t, three_t, wide2_t, wide1_t, share_t = take(7)
    s, b, big, ay, tx_own, t = take(6)
    step = pl.program_id(0)
    i, j = lax.axis_index("px"), lax.axis_index("py")
    y, zh = i // 2, i % 2
    zl, x, c = j // 8, (j // 2) % 4, j % 2
    spot = 2 * zl + zh
    sibling = (i, 8 * zl + 2 * x + 1 - c)

    def at_x(n):
        return (i, 8 * zl + 2 * n + c)

    def at_y(n):
        return (2 * n + zh, j)

    def at_z(n):
        return (2 * y + n % 2, 8 * (n // 2) + 2 * x + c)

    def remote(src, dst, sems, sent, landed, device):
        return pltpu.make_async_remote_copy(
            src_ref=src,
            dst_ref=dst,
            send_sem=sems.at[0, sent],
            recv_sem=sems.at[1, landed],
            device_id=device,
            device_id_type=MESH,
        )

    def neighbour(d, sign):
        return (
            (i + sign * STEP_ROWS[d] + ROWS) % ROWS,
            (j + sign * STEP_COLS[d] + COLS) % COLS,
        )

    def band(n, size=32):
        return pl.ds(pl.multiple_of(n * size, size), size)

    barrier = pltpu.get_barrier_semaphore()
    partners = [sibling]
    for r in (1, 2, 3):
        partners += [at_x((x + r) % 4), at_y((y + r) % 4), at_z((spot + r) % 4)]
    partners += [neighbour(d, 1) for d in range(8)]
    weights = pltpu.make_async_copy(w, wv, local.at[0])
    table_x = pltpu.make_async_copy(tx.at[i], tx_own, local.at[4])
    keep = pltpu.make_async_copy(big_in, big, local.at[5])
    def greet():
        for device in partners:
            pl.semaphore_signal(barrier, inc=1, device_id=device, device_id_type=MESH)
        weights.start()
        table_x.start()


    @pl.when(step == 0)
    def _():
        keep.start()
        greet()

    tail = cells_body(
        step, i, j, keep, cells_in, layer_out, pre_out, ay, big, b, t, refs
    )
    def run():
        pl.semaphore_wait(barrier, len(partners))
        waits = []

        def begin(copy):
            copy.start()
            waits.append(copy)

        def core_copy_a(n):
            return remote(s.at[:, n, 1 - c, 0:2], r0.at[:, n, 0:2], core_a, n, n, sibling)

        def core_copy_b(n):
            src = s.at[:, :, 1 - c, 2:4, band(n)]
            return remote(src, r0.at[:, :, 2:4, band(n)], core_b, n, n, sibling)

        def block_copy(d):
            device = neighbour(d, 1)
            return remote(b.at[d], bo.at[d], blocks, d, d, device)

        def fill(n, half):
            def step(m, carry):
                a, e = m // 2, m % 2
                ky = 4 * (8 * a + 2 * n + e) + 2 * half
                first, second = x_to_modes(tx_own[...], ay, (ky, ky + 1))
                s[a, n, e, 2 * half] = first
                s[a, n, e, 2 * half + 1] = second
                return carry

            lax.fori_loop(0, 4, step, 0, unroll=4)

        table_x.wait()
        for r in (2, 1, 3, 0):
            n = (x + r) % 4
            fill(n, 0)
            begin(core_copy_a(n))

        def core_copy_t():
            return remote(t.at[1 - c], t0, core_t, 0, 0, sibling)

        def one_copy_a(n, slot, device):
            return remote(sa.at[n], r1a.at[slot], one_a, n, slot, device)

        def one_copy_b(n, slot, device):
            return remote(sb.at[n], r1b.at[slot], one_b, n, slot, device)

        def sum_a(n):
            core_copy_a(n).wait_recv()
            return s[:, n, c, 0:2].astype(F32) + r0[:, n, 0:2].astype(F32)

        def sum_b(n):
            core_copy_b(n).wait_recv()
            rows = band(n)
            return s[:, :, c, 2:4, rows].astype(F32) + r0[:, :, 2:4, rows].astype(F32)

        def pass_a(r):
            n = (x + r) % 4
            sa[n] = sum_a(n).astype(BF)
            begin(one_copy_a(n, x, at_x(n)))

        def pass_b(r):
            n = (y + r) % 4
            sb[n] = sum_b(n).astype(BF)
            begin(one_copy_b(n, y, at_y(n)))

        for r in (2, 1, 3, 0):
            fill((x + r) % 4, 1)
            if r:
                pass_a(r)
        for r in (2, 1, 3, 0):
            begin(core_copy_b((y + r) % 4))
        for r in (2, 1, 3):
            pass_b(r)
        tail()
        begin(core_copy_t())
        for d in range(8):
            begin(block_copy(d))
        acca[...] = sum_a(x)
        accb[...] = sum_b(y)

        def one_copy_t(n, slot, device):
            return remote(t1s.at[n], t1.at[slot], one_t, n, slot, device)

        core_copy_t().wait_recv()
        t1s[...] = (t[c].astype(F32) + t0[...].astype(F32)).astype(BF)
        for r in (2, 1, 3):
            n = (x + r) % 4
            begin(one_copy_t(n, x, at_x(n)))
        for r in (1, 3, 2):
            n = (x + r) % 4
            one_copy_a(n, n, at_x(n)).wait_recv()
            acca[...] = acca[...] + r1a[n].astype(F32)

        def two_copy_a(n, slot, device):
            return remote(acca.at[:, :, band(n)], r2a.at[slot], two_a, n, slot, device)

        def two_copy_b(n, slot, device):
            return remote(accb.at[:, n], r2b.at[slot], two_b, n, slot, device)

        for r in (2, 1, 3):
            n = (y + r) % 4
            begin(two_copy_a(n, y, at_y(n)))
        for r in (1, 3, 2):
            n = (y + r) % 4
            one_copy_b(n, n, at_y(n)).wait_recv()
            accb[...] = accb[...] + r1b[n].astype(F32)
        for r in (2, 1, 3):
            n = (x + r) % 4
            begin(two_copy_b(n, x, at_x(n)))
        ab[:, 0:2] = acca[:, :, band(y)]
        ab[:, 2:4] = accb[:, x]
        for r in (1, 3, 2):
            n = (y + r) % 4
            two_copy_a(n, n, at_y(n)).wait_recv()
            ab[:, 0:2] = ab[:, 0:2] + r2a[n]
        for r in (1, 3, 2):
            n = (x + r) % 4
            two_copy_b(n, n, at_x(n)).wait_recv()
            ab[:, 2:4] = ab[:, 2:4] + r2b[n]

        def three_copy(n, slot, device):
            return remote(ab.at[n // 2, :, band(n % 2, 16)], r3.at[slot], three, n, slot, device)

        for r in (2, 1, 3):
            n = (spot + r) % 4
            begin(three_copy(n, spot, at_z(n)))

        def two_copy_t(n, slot, device):
            return remote(t2s.at[n], t2.at[slot], two_t, n, slot, device)

        total = t1s[x].astype(F32)
        for r in (1, 3, 2):
            n = (x + r) % 4
            one_copy_t(n, n, at_x(n)).wait_recv()
            total = total + t1[n].astype(F32)
        t2s[...] = total.astype(BF)
        for r in (2, 1, 3):
            n = (y + r) % 4
            begin(two_copy_t(n, y, at_y(n)))
        u[...] = ab[zl, :, band(zh, 16)]
        for r in (1, 3, 2):
            n = (spot + r) % 4
            three_copy(n, n, at_z(n)).wait_recv()
            u[...] = u[...] + r3[n]
        u[...] = u[...] * math.sqrt(NX * NY / (MX * MY))
        weights.wait()
        same = iota((16, 16), 0) ^ 1
        turn = jnp.where(iota((16, 16), 1) == same, 1.0, 0.0)
        odd = (iota((16, 16), 0) & 1) == 1
        flip = odd
        turn = jnp.where(flip, -turn, turn).astype(BF)

        def mix(ky, carry):
            first = u[ky]
            high = first.astype(BF)
            low = (first - high.astype(F32)).astype(BF)
            both = jnp.concatenate([high, low], axis=0)
            turned = jnp.concatenate([dot(turn, high), dot(turn, low)], axis=0).astype(BF)
            both = jnp.concatenate([both, turned], axis=1)
            total = jnp.zeros((16, C), F32)
            for kx in range(8):
                mat = jnp.concatenate([wv[0, kx, ky], wv[1, kx, ky]], axis=1).astype(BF)
                res = dot_tb(both, mat)
                total = jnp.where((iota((16, C), 0) >> 1) == kx, res[:16] + res[16:], total)
            zs[ky] = total.astype(BF)
            return carry

        lax.fori_loop(0, 4, mix, 0)

        def wide_copy3(slot, sent, device):
            dst = zz.at[slot // 2, :, band(slot % 2, 16)]
            return remote(zs, dst, wide3, sent, slot, device)

        for r in (2, 1, 3):
            n = (spot + r) % 4
            begin(wide_copy3(spot, n, at_z(n)))
        zz[zl, :, band(zh, 16)] = zs[...]
        t3s[...] = t2s[y]
        total = t3s[...].astype(F32)
        for r in (1, 3, 2):
            n = (y + r) % 4
            two_copy_t(n, n, at_y(n)).wait_recv()
            total = total + t2[n].astype(F32)
        t3s[...] = total.astype(BF)
        t3[spot] = t3s[...]

        def three_copy_t(slot, sent, device):
            return remote(t3s, t3.at[slot], three_t, sent, slot, device)

        for r in (2, 1, 3):
            n = (spot + r) % 4
            begin(three_copy_t(spot, n, at_z(n)))
        for r in (1, 3, 2):
            n = (spot + r) % 4
            wide_copy3(n, n, at_z(n)).wait_recv()

        def wide_copy2_a(slot, sent, device):
            return remote(zz.at[:, 0:2], za.at[:, :, band(slot)], wide2_a, sent, slot, device)

        def wide_copy2_b(slot, sent, device):
            return remote(zz.at[:, 2:4], zb.at[:, slot], wide2_b, sent, slot, device)

        for r in (2, 1, 3):
            n = (y + r) % 4
            begin(wide_copy2_a(y, n, at_y(n)))
            n = (x + r) % 4
            begin(wide_copy2_b(x, n, at_x(n)))
        za[:, :, band(y)] = zz[:, 0:2]
        zb[:, x] = zz[:, 2:4]
        for r in (1, 3, 2):
            n = (spot + r) % 4
            three_copy_t(n, n, at_z(n)).wait_recv()
        total = t3[0].astype(F32)
        for n in range(1, 4):
            total = total + t3[n].astype(F32)
        tall[x, y] = total.astype(BF)

        def wide_copy2_t(slot, sent, device):
            piece = tall.at[x, slot]
            return remote(piece, piece, wide2_t, sent, slot, device)

        for r in (2, 1, 3):
            n = (y + r) % 4
            begin(wide_copy2_t(y, n, at_y(n)))

        def part_a(n, core):
            return z.at[:, n, core, 0:2]

        def part_b(n, core):
            return z.at[:, :, core, 2:4, band(n)]

        def wide_copy1_a(slot, sent, device):
            return remote(za, part_a(slot, c), wide1_a, sent, slot, device)

        def wide_copy1_b(slot, sent, device):
            return remote(zb, part_b(slot, c), wide1_b, sent, slot, device)

        for r in (1, 3, 2):
            n = (y + r) % 4
            wide_copy2_a(n, n, at_y(n)).wait_recv()
        for r in (2, 1, 3):
            n = (x + r) % 4
            begin(wide_copy1_a(x, n, at_x(n)))
        for r in (1, 3, 2):
            n = (x + r) % 4
            wide_copy2_b(n, n, at_x(n)).wait_recv()
        for r in (2, 1, 3):
            n = (y + r) % 4
            begin(wide_copy1_b(y, n, at_y(n)))
        own_a = pltpu.make_async_copy(za, part_a(x, c), local.at[1])
        own_a.start()
        own_b = pltpu.make_async_copy(zb, part_b(y, c), local.at[2])
        own_b.start()
        begin(remote(za, part_a(x, c), share_a, x, x, sibling))
        begin(remote(zb, part_b(y, c), share_b, y, y, sibling))
        for r in (1, 3, 2):
            n = (y + r) % 4
            wide_copy2_t(n, n, at_y(n)).wait_recv()

        def wide_copy1_t(slot, sent, device):
            piece = tall.at[slot]
            return remote(piece, piece, wide1_t, sent, slot, device)

        for r in (2, 1, 3):
            n = (x + r) % 4
            begin(wide_copy1_t(x, n, at_x(n)))

        def share_copy_a(n, core):
            return remote(part_a(n, core), part_a(n, core), share_a, n, n, sibling)

        def share_copy_b(n, core):
            return remote(part_b(n, core), part_b(n, core), share_b, n, n, sibling)

        for r in (1, 3, 2):
            n = (x + r) % 4
            wide_copy1_a(n, n, at_x(n)).wait_recv()
            begin(share_copy_a(n, c))
            n = (y + r) % 4
            wide_copy1_b(n, n, at_y(n)).wait_recv()
            begin(share_copy_b(n, c))
        for r in (1, 3, 2):
            n = (x + r) % 4
            wide_copy1_t(n, n, at_x(n)).wait_recv()
        share = remote(tall, to.at[c], share_t, 0, 0, sibling)
        begin(share)
        own_t = pltpu.make_async_copy(tall, to.at[c], local.at[3])
        own_t.start()
        for n in range(4):
            share_copy_a(n, 1 - c).wait_recv()
            share_copy_b(n, 1 - c).wait_recv()
        for d in range(8):
            block_copy(d).wait_recv()
        own_a.wait()
        own_b.wait()
        share.wait_recv()
        own_t.wait()
        for copy in waits:
            copy.wait_send()

    pl.when(step == 4)(run)


def whole(*shape):
    zeros = (0,) * len(shape)
    return pl.BlockSpec(shape, lambda n: zeros)


def forward_call(*operands):
    shape = jax.ShapeDtypeStruct
    out_shape = [shape((2, 4, 2, 4, 128, C), BF), shape((8, 400, C), BF), shape((4, 16, C), F32)]
    out_shape.append(shape((1024, 640), BF))
    out_specs = [HB, HB, VM, HB]
    in_specs = [SM, VM, HB, HB, HB]
    sem = pltpu.SemaphoreType.DMA((2, 4))
    scratch = [
        pltpu.VMEM((2, 4, 4, 128, C), BF),
        pltpu.VMEM((4, 2, 2, 128, C), BF),
        pltpu.VMEM((4, 2, 4, 2, 32, C), BF),
        pltpu.VMEM((4, 2, 2, 128, C), BF),
        pltpu.VMEM((4, 2, 4, 2, 32, C), BF),
        pltpu.VMEM((2, 2, 128, C), F32),
        pltpu.VMEM((2, 4, 2, 32, C), F32),
        pltpu.VMEM((16, 2, 16, C), F32),
        pltpu.VMEM((16, 2, 16, C), F32),
        pltpu.VMEM((4, 16, C), BF),
        pltpu.VMEM((2, 2, 128, C), BF),
        pltpu.VMEM((2, 4, 2, 32, C), BF),
        pltpu.VMEM((2, 8, 4, C, C), F32),
    ]
    scratch += [sem] * 8 + [pltpu.SemaphoreType.DMA((2, 16))] * 4 + [pltpu.SemaphoreType.DMA((2, 8)), pltpu.SemaphoreType.DMA((6,))]
    scratch += [
        pltpu.VMEM((2, 4, 2, 4, 128, C), BF),
        pltpu.VMEM((8, 400, C), BF),
        pltpu.VMEM((1024, 640), BF),
        pltpu.VMEM((10, 128, 8, C), F32),
        pltpu.VMEM((128, 480), BF),
    ]
    scratch += [
        pltpu.VMEM((SIDE + 60, 88, C), F32),
        pltpu.VMEM((408, C), F32),
        pltpu.VMEM((128, SIDE), BF),
    ]
    return pl.pallas_call(
        forward_kernel,
        out_shape=tuple(out_shape),
        in_specs=in_specs,
        out_specs=tuple(out_specs),
        scratch_shapes=scratch,
        compiler_params=pltpu.CompilerParams(
            collective_id=1,
            has_side_effects=True,
            vmem_limit_bytes=VMEM_LIMIT,
        ),
        name="forward_and_exchange",
    )(*operands)


def cells_call(*operands):
    shape = jax.ShapeDtypeStruct
    out_shape = [shape((2, 4, 2, 4, 128, C), BF), shape((8, 400, C), BF), shape((4, 16, C), F32)]
    tile = pl.BlockSpec((16, SIDE, C), lambda n: (n, 0, 0))
    field = shape((SIDE, SIDE, C), BF)
    out_shape = [field, field] + out_shape + [shape((2, 4, 4, PIECE, C), BF)]
    out_specs = [tile, tile, HB, HB, whole(4, 16, C), HB]
    in_specs = [tile, tile, whole(64, 128, C), whole(8, 400, C), whole(C, C)]
    in_specs += [whole(8, C, C), whole(C, H), whole(H, C), whole(COLS, SIDE, 128)]
    in_specs += [whole(ROWS, 160, 256), HB, HB, HB]
    sem = pltpu.SemaphoreType.DMA((2, 4))
    scratch = [
        pltpu.VMEM((2, 4, 4, 128, C), BF),
        pltpu.VMEM((4, 2, 2, 128, C), BF),
        pltpu.VMEM((4, 2, 4, 2, 32, C), BF),
        pltpu.VMEM((4, 2, 2, 128, C), BF),
        pltpu.VMEM((4, 2, 4, 2, 32, C), BF),
        pltpu.VMEM((2, 2, 128, C), F32),
        pltpu.VMEM((2, 4, 2, 32, C), F32),
        pltpu.VMEM((4, 2, 2, 32, C), F32),
        pltpu.VMEM((4, 2, 2, 32, C), F32),
        pltpu.VMEM((2, 4, 32, C), F32),
        pltpu.VMEM((4, 4, 16, C), F32),
        pltpu.VMEM((4, 16, C), BF),
        pltpu.VMEM((2, 4, 32, C), BF),
        pltpu.VMEM((2, 2, 128, C), BF),
        pltpu.VMEM((2, 4, 2, 32, C), BF),
        pltpu.VMEM((2, 8, 4, C, C), F32),
    ]
    scratch += [sem] * 14 + [pltpu.SemaphoreType.DMA((2, 8)), pltpu.SemaphoreType.DMA((6,))]
    scratch += [
        pltpu.VMEM((4, 4, PIECE, C), BF),
        pltpu.VMEM((4, 4, PIECE, C), BF),
        pltpu.VMEM((4, 4, PIECE, C), BF),
        pltpu.VMEM((4, PIECE, C), BF),
        pltpu.VMEM((4, PIECE, C), BF),
        pltpu.VMEM((PIECE, C), BF),
        pltpu.VMEM((4, PIECE, C), BF),
        pltpu.VMEM((4, 4, PIECE, C), BF),
    ] + [sem] * 7
    scratch += [
        pltpu.VMEM((2, 4, 2, 4, 128, C), BF),
        pltpu.VMEM((8, 400, C), BF),
        pltpu.VMEM((1024, 640), BF),
        pltpu.VMEM((10, 128, 8, C), F32),
        pltpu.VMEM((128, 480), BF),
    ]
    scratch += [
        pltpu.VMEM((2, 4, 4, PIECE, C), BF),
        pltpu.VMEM((10, 128, 8, C), F32),
        pltpu.VMEM((640, 1024), BF),
        pltpu.VMEM((1280, 160), BF),
        pltpu.VMEM((80, 1280), BF),
        pltpu.VMEM((400, C), F32),
        pltpu.VMEM((400, C), F32),
        pltpu.VMEM((1280, C), F32),
        pltpu.VMEM((1280, C), F32),
        pltpu.VMEM((1280, C), BF),
        pltpu.VMEM((1280, H), F32),
        pltpu.VMEM((1280, H), F32),
        pltpu.VMEM((1280, H), BF),
        pltpu.VMEM((1280, H), BF),
        pltpu.VMEM((C, C), F32),
        pltpu.VMEM((C, H), F32),
        pltpu.VMEM((C, H), F32),
    ]
    return pl.pallas_call(
        cells_kernel,
        out_shape=tuple(out_shape),
        in_specs=in_specs,
        out_specs=tuple(out_specs),
        scratch_shapes=scratch,
        grid=(5,),
        compiler_params=pltpu.CompilerParams(
            collective_id=2,
            has_side_effects=True,
            vmem_limit_bytes=VMEM_LIMIT,
        ),
        name="cells_and_exchange",
    )(*operands)


def gelu_both(v):
    square = v * v
    t = jnp.tanh(v * (TANH_SCALE + (TANH_SCALE * CUBIC_TERM) * square))
    half = 0.5 + 0.5 * t
    inner = (0.5 * TANH_SCALE) + (1.5 * TANH_SCALE * CUBIC_TERM) * square
    return v * half, half + v * (1.0 - t * t) * inner


def store_rows(tot, first, rows):
    done = 0
    while done < rows.shape[0]:
        place, inside = divmod(first + done, PIECE)
        count = min(PIECE - inside, rows.shape[0] - done)
        spot = (place // 16, place // 4 % 4, place % 4)
        tot[spot + (pl.ds(inside, count),)] = rows[done : done + count]
        done += count


def cells_body(step, row, col, keep, inputs, layer, pre_out, ay, big, bgrad, tot, scratch):
    field, cot, z, blk, skip, ctx, up, down, gy, gx = inputs
    p, cells_big, spread, gather, coarse, cell, pre, slope, mid = scratch[:9]
    lifted, dh, hid, lg, acc_skip, acc_up, acc_down = scratch[9:]

    @pl.when(step == 0)
    def _():
        x_to_cells(gx[row], z, p)
        build_to_cells(gy[col], cells_big)
        total = dot(blk[0], ctx[0])
        for d in range(1, 8):
            total = total + dot(blk[d], ctx[d])
        coarse[...] = total
        n, l = iota((1280, 160), 0), iota((1280, 160), 1)
        l = jnp.where(l >= 80, l - 80, l)
        x = over_80(n)
        y = n - 80 * x
        a = over_20(l)
        hit = ((x >> 2) == a) & ((y >> 2) == l - 20 * a)
        spread[...] = jnp.where(hit, 1.0, 0.0).astype(BF)
        l, n = iota((80, 1280), 0), iota((80, 1280), 1)
        x = over_80(n)
        y = n - 80 * x
        a = over_20(l)
        hit = ((x >> 2) == a) & ((y >> 2) == l - 20 * a)
        gather[...] = jnp.where(hit, 1.0, 0.0).astype(BF)
        acc_skip[...] = jnp.zeros_like(acc_skip)
        acc_up[...] = jnp.zeros_like(acc_up)
        acc_down[...] = jnp.zeros_like(acc_down)

    own_rows = pl.ds(pl.multiple_of(80 * step, 8), 80)
    flat = field[...].reshape(1280, C)
    flat_cot = cot[...].reshape(1280, C)
    wide = jnp.concatenate(
        [p[2 * step].reshape(1024, C).astype(BF), p[2 * step + 1].reshape(1024, C).astype(BF)],
        axis=1,
    )
    own = coarse[own_rows]
    high = own.astype(BF)
    low = (own - high.astype(F32)).astype(BF)
    rest = dot(flat, skip[...]) + dot(spread[...], jnp.concatenate([high, low], axis=0))
    for part in range(640 // 160):
        lo, hi = 160 * part, 160 * part + 160
        spectral = dot(cells_big[pl.ds(lo, 160)], wide)
        pre[pl.ds(lo, 160)] = spectral[:, :C].astype(BF).astype(F32) + rest[lo:hi]
        pre[pl.ds(640 + lo, 160)] = spectral[:, C:].astype(BF).astype(F32) + rest[640 + lo : 640 + hi]

    def activate(n, carry):
        rows = pl.ds(pl.multiple_of(64 * n, 64), 64)
        value, slant = gelu_both(pre[rows])
        mid[rows] = value.astype(BF)
        slope[rows] = slant
        return carry

    lax.fori_loop(0, 20, activate, 0, unroll=20)
    lifted[...] = dot(mid[...], up[...])
    dh[...] = dot_tb(flat_cot, down[...])

    def activate_wide(n, carry):
        rows = pl.ds(pl.multiple_of(16 * n, 16), 16)
        value, slant = gelu_both(lifted[rows])
        hid[rows] = value.astype(BF)
        lg[rows] = (dh[rows] * slant).astype(BF)
        return carry

    lax.fori_loop(0, 80, activate_wide, 0, unroll=80)
    result = mid[...].astype(F32) + dot(hid[...], down[...])
    layer[...] = result.astype(BF).reshape(16, SIDE, C)
    grad = flat_cot.astype(F32) + dot_tb(lg[...], up[...])
    grad = (grad * slope[...]).astype(BF)
    pre_out[...] = grad.reshape(16, SIDE, C)
    acc_skip[...] += dot_ta(flat, grad)
    acc_up[...] += dot_ta(mid[...], lg[...])
    acc_down[...] += dot_ta(flat_cot, hid[...])
    cell[own_rows] = dot(gather[...], grad)
    pl.when(step == 0)(keep.wait)
    y_store(big, jnp.concatenate([grad[:640], grad[640:]], axis=1), ay, step)

    def tail():
        narrow = cell[...].astype(BF)
        store_rows(tot, 0, acc_skip[...].astype(BF))
        for d in range(8):
            store_rows(tot, 128 + 128 * d, dot_ta(blk[d], narrow).astype(BF))
            bgrad[d] = dot_tb(narrow, ctx[d]).astype(BF)
        for part in range(4):
            cut = slice(128 * part, 128 * part + 128)
            store_rows(tot, 1152 + 128 * part, acc_up[:, cut].astype(BF))
            store_rows(tot, 1664 + 128 * part, acc_down[:, cut].T.astype(BF))
        store_rows(tot, 2176, jnp.zeros((TOT - 2176, C), BF))

    return tail


def outer(u, g, spec):
    turn = jnp.where(iota((16, 16), 1) == (iota((16, 16), 0) ^ 1), 1.0, 0.0)
    turn = jnp.where((iota((16, 16), 0) & 1) == 1, -turn, turn).astype(BF)
    left_high = u.astype(BF)
    left_low = (u - left_high.astype(F32)).astype(BF)
    right_high = g.astype(BF)
    right_low = (g - right_high.astype(F32)).astype(BF)
    high = jnp.concatenate([right_high, dot(turn, right_high).astype(BF)], axis=1)
    low = jnp.concatenate([right_low, dot(turn, right_low).astype(BF)], axis=1)
    lefts = jnp.concatenate([left_high, left_high, left_low], axis=0).astype(F32).T.astype(BF)
    rights = jnp.concatenate([high, low, high], axis=0)
    row = (iota((48, 2 * C), 0) & 15) >> 1
    for kx in range(8):
        res = dot(lefts, jnp.where(row == kx, rights, jnp.zeros_like(rights)))
        spec[0, kx, 0] = res[:, :C]
        spec[1, kx, 0] = res[:, C:]


def weight_sums(tot, skip, ctx, up, down):
    inv = 1.0 / math.sqrt(NX * NY)
    skip[...] = tot[pl.ds(0, 128)].astype(F32) * inv
    for d in range(8):
        ctx[d] = tot[pl.ds(128 + 128 * d, 128)].astype(F32) * inv
    for part in range(4):
        cut = slice(128 * part, 128 * part + 128)
        up[:, cut] = tot[pl.ds(1152 + 128 * part, 128)].astype(F32) * inv
    down[...] = tot[pl.ds(1664, 512)].astype(F32) * inv


def last_kernel(
    picks, pre, z, back, skip, gy, gx, u, g, tot,
    out, spec, skip_out, ctx_out, up_out, down_out, p, cells_big, place, grads, wide,
):
    step = pl.program_id(0)
    row, col = lax.axis_index("px"), lax.axis_index("py")
    starts = [start_of(pick_of(picks, row, col, d)) for d in range(8)]

    @pl.when(step == 0)
    def _():
        x_to_cells(gx[row], z, p)
        build_to_cells(gy[col], cells_big)
        y, lane = iota((SIDE, 192), 0), iota((SIDE, 192), 1)
        total = jnp.zeros((SIDE, 192), F32)
        for d in range(8):
            depth, sx, sy = starts[d]
            share = jnp.where(depth == 0, 1.0, jnp.where(depth == 1, 0.25, 0.0625))
            spot = lane - 24 * d
            line = jnp.where(depth == 0, y, jnp.where(depth == 1, y >> 1, y >> 2))
            hit = (spot >= 0) & (spot < BLK) & (line - sy == spot)
            total = jnp.where(hit, share, total)
        place[...] = total.astype(BF)
        wide[pl.ds(400, 8)] = jnp.zeros((8, C), F32)
        for d in range(8):
            wide[pl.ds(0, 400)] = back[d].astype(F32)
            for a in range(BLK):
                grads[d, a] = wide[pl.ds(BLK * a, 24)]
            grads[d, BLK] = jnp.zeros((24, C), F32)

    @pl.when(step < 4)
    def _():
        outer(u[step], g[step], spec)

    pl.when(step == 4)(lambda: weight_sums(tot, skip_out, ctx_out, up_out, down_out))
    both = jnp.concatenate(
        [p[2 * step].reshape(1024, C).astype(BF), p[2 * step + 1].reshape(1024, C).astype(BF)],
        axis=1,
    )
    factor = math.sqrt(MX * MY / (NX * NY))
    straight = dot_tb(pre[...].reshape(1280, C), skip[...])
    for k in range(8):
        spectral = dot(cells_big[pl.ds(SIDE * k, SIDE)], both) * factor
        wide_pieces = []
        for x in (k, k + 8):
            pieces = []
            for d in range(8):
                depth, sx, sy = starts[d]
                a = ((16 * step + x) >> depth) - sx
                a = jnp.where((a >= 0) & (a < BLK), a, BLK)
                pieces.append(grads[d, a])
            wide_pieces.append(jnp.concatenate(pieces, axis=0).astype(BF))
        total = spectral + dot(place[...], jnp.concatenate(wide_pieces, axis=1))
        out[k] = (total[:, :C] + straight[80 * k : 80 * k + 80]).astype(BF)
        x = k + 8
        out[x] = (total[:, C:] + straight[80 * x : 80 * x + 80]).astype(BF)


def last_call(picks, pre, z, back, skip, gy, gx, u, g, tot):
    tile = pl.BlockSpec((16, SIDE, C), lambda n: (n, 0, 0))
    shape = jax.ShapeDtypeStruct
    return pl.pallas_call(
        last_kernel,
        grid=(5,),
        out_shape=(
            shape((SIDE, SIDE, C), BF),
            shape((2, 8, 4, C, C), F32),
            shape((C, C), F32),
            shape((8, C, C), F32),
            shape((C, H), F32),
            shape((H, C), F32),
        ),
        in_specs=[
            SM, tile, whole(64, 128, C), whole(8, 400, C), whole(C, C),
            whole(COLS, SIDE, 128), whole(ROWS, 160, 256), whole(4, 16, C), whole(4, 16, C),
            whole(TOT, C),
        ],
        out_specs=(
            tile,
            pl.BlockSpec((2, 8, 1, C, C), lambda n: (0, 0, jnp.minimum(n, 3), 0, 0)),
            whole(C, C),
            whole(8, C, C),
            whole(C, H),
            whole(H, C),
        ),
        scratch_shapes=[
            pltpu.VMEM((10, 128, 8, C), F32),
            pltpu.VMEM((640, 1024), BF),
            pltpu.VMEM((SIDE, 192), BF),
            pltpu.VMEM((8, BLK + 1, 24, C), F32),
            pltpu.VMEM((408, C), F32),
        ],
        compiler_params=pltpu.CompilerParams(vmem_limit_bytes=VMEM_LIMIT),
        name="field_gradient",
    )(picks, pre, z, back, skip, gy, gx, u, g, tot)


def shards(
    flow_field, cotangent, spec_weight, skip_weight, ctx_weight, up_weight, down_weight,
    ctx_level, ctx_offset,
):
    ty, gy, tx, gx = (jnp.asarray(t) for t in wave_tables())
    picks = ctx_level + (ctx_offset[:, :, 0] << 2) + (ctx_offset[:, :, 1] << 9)
    z, arrived, u, big = forward_call(picks, flow_field, ty, tx, spec_weight)
    layer, pre, z, back, g, tot = cells_call(
        flow_field, cotangent, z.reshape(64, 128, C), arrived, skip_weight, ctx_weight,
        up_weight, down_weight, gy, gx, tx, big, spec_weight,
    )
    grad, spec, skip, ctx, up, down = last_call(
        picks, pre, z.reshape(64, 128, C), back, skip_weight, gy, gx, u, g, tot.reshape(TOT, C)
    )
    return layer, grad, spec, skip, ctx, up, down


def solution(mesh):
    return jax.shard_map(
        shards,
        mesh=mesh,
        in_specs=(
            P("px", "py", None),
            P("px", "py", None),
            P(None, "px", "py", None, None),
            P(),
            P(),
            P(),
            P(),
            P(),
            P(),
        ),
        out_specs=(
            P("px", "py", None),
            P("px", "py", None),
            P(None, "px", "py", None, None),
            P(),
            P(),
            P(),
            P(),
        ),
        check_vma=False,
    )
```

```python
import math

import jax
import jax.numpy as jnp
import ml_dtypes
import numpy as np
from jax import lax
from jax.experimental import pallas as pl
from jax.experimental.pallas import tpu as pltpu
from jax.sharding import PartitionSpec as P

BF = jnp.bfloat16
F32 = jnp.float32
TANH_SCALE = 0.7978845608028654
CUBIC_TERM = 0.044715
STEP_ROWS = (-1, -1, -1, 0, 0, 1, 1, 1)
STEP_COLS = (-1, 0, 1, -1, 1, -1, 0, 1)
ROWS, COLS = 8, 16
SIDE, C, H, BLK = 80, 128, 512, 20
NX, NY, MX, MY = 640, 1280, 64, 64
PIECE = 80
TOT = 32 * PIECE
VMEM_LIMIT = 56 * 1024 * 1024
MESH = pl.DeviceIdType.MESH
VM = pl.BlockSpec(memory_space=pltpu.VMEM)
SM = pl.BlockSpec(memory_space=pltpu.SMEM)
HB = pl.BlockSpec(memory_space=pl.ANY)


def wave_tables():
    waves = np.arange(64) - 32

    def parts(length, side):
        turns = (np.arange(length)[:, None] * waves[None, :]) % length
        phase = turns * (2.0 * math.pi / length)
        return np.cos(phase).reshape(-1, side, 64), np.sin(phase).reshape(-1, side, 64)

    cos_y, sin_y = parts(NY, SIDE)
    cos_x, sin_x = parts(NX, SIDE)
    to_modes_y = np.stack([cos_y, -sin_y], axis=-1).reshape(COLS, SIDE, 128) / math.sqrt(NY)
    to_modes_y = to_modes_y.transpose(0, 2, 1)
    to_cells_y = np.stack([cos_y, -sin_y], axis=-1).reshape(COLS, SIDE, 128) / math.sqrt(MY)
    cx, sx = cos_x.transpose(0, 2, 1), -sin_x.transpose(0, 2, 1)
    real = np.concatenate([cx, -sx], axis=2)
    imag = np.concatenate([sx, cx], axis=2)
    to_modes_x = np.stack([real, imag], axis=2).reshape(ROWS, 128, 2 * SIDE) / math.sqrt(NX)
    real = np.stack([cos_x, -sin_x], axis=-1).reshape(ROWS, SIDE, 128)
    imag = np.stack([sin_x, cos_x], axis=-1).reshape(ROWS, SIDE, 128)
    to_cells_x = np.concatenate([real, imag], axis=1) / math.sqrt(MX)

    def rounded(t):
        return np.ascontiguousarray(t).astype(ml_dtypes.bfloat16)

    def rest(t):
        return rounded(t - rounded(t).astype(np.float64))

    high, low = rounded(to_modes_x), rest(to_modes_x)
    wide_modes_x = np.concatenate([high, low, high], axis=2)
    wide_cells_x = np.concatenate([rounded(to_cells_x), rest(to_cells_x)], axis=2)
    return rounded(to_modes_y), rounded(to_cells_y), wide_modes_x, wide_cells_x


def iota(shape, axis):
    return lax.broadcasted_iota(jnp.int32, shape, axis)


def dot(a, b):
    return jnp.dot(a, b, preferred_element_type=F32)


def dot_tb(a, b):
    return lax.dot_general(a, b, (((1,), (1,)), ((), ())), preferred_element_type=F32)


def dot_ta(a, b):
    return lax.dot_general(a, b, (((0,), (0,)), ((), ())), preferred_element_type=F32)


def over_80(v):
    return (v * 52429) >> 22


def over_20(v):
    return (v * 52429) >> 20


def build_to_modes(table, big_ref):
    lane = iota((SIDE, 640), 1)
    tile = (lane - 80 * over_80(lane) == iota((SIDE, 640), 0)).astype(F32).astype(BF)
    for part in range(8):
        rep = ((iota((128, 128), 0) >> 3) + 16 * part == iota((128, 128), 1)).astype(F32)
        rows = dot(dot(rep.astype(BF), table).astype(BF), tile)
        mask = (iota((128, 640), 0) & 7) == over_80(iota((128, 640), 1))
        big_ref[pl.ds(128 * part, 128), :] = jnp.where(mask, rows, 0.0).astype(BF)


def build_to_cells(table, big_ref):
    rep = ((iota((128, 1024), 1) >> 3) == iota((128, 1024), 0)).astype(F32)
    wide = dot(table, rep.astype(BF))
    lane = iota((SIDE, 1024), 1) & 7
    for x in range(8):
        big_ref[pl.ds(SIDE * x, SIDE), :] = jnp.where(lane == x, wide, 0.0).astype(BF)


def x_to_modes(table, ay_ref, kys):
    wide = []
    for ky in kys:
        both = [ay_ref[:, 2 * ky + r].reshape(SIDE, C) for r in range(2)]
        high = [v.astype(BF) for v in both]
        low = [(v - h.astype(F32)).astype(BF) for v, h in zip(both, high)]
        wide.append(jnp.concatenate(high + high + low, axis=0))
    modes = dot(table, jnp.concatenate(wide, axis=1)).astype(BF)
    return modes[:, :C], modes[:, C:]


def x_to_cells(table, z_ref, p_ref):
    def step(pair, carry):
        wide = jnp.concatenate([z_ref[2 * pair], z_ref[2 * pair + 1]], axis=1)
        cells = dot(table, jnp.concatenate([wide, wide], axis=0))
        for h in range(2):
            for r in range(2):
                piece = cells[r * SIDE : (r + 1) * SIDE, h * C : (h + 1) * C]
                p_ref[:, 2 * (2 * pair + h) + r] = piece.reshape(10, 8, C)
        return carry

    lax.fori_loop(0, 32, step, 0, unroll=32)


def y_store(big, pair_cells, ay_ref, pair):
    for part in range(4):
        modes = dot(big[pl.ds(256 * part, 256)], pair_cells)
        spot = pl.ds(32 * part, 32)
        ay_ref[2 * pair, spot] = modes[:, :C].reshape(32, 8, C)
        ay_ref[2 * pair + 1, spot] = modes[:, C:].reshape(32, 8, C)


def y_to_modes(big, field, ay):
    def y_step(pair, carry):
        first = field[pl.ds(16 * pair, 8)].reshape(640, C)
        second = field[pl.ds(16 * pair + 8, 8)].reshape(640, C)
        y_store(big, jnp.concatenate([first, second], axis=1), ay, pair)
        return carry

    lax.fori_loop(0, 5, y_step, 0)


def start_of(pick):
    depth = pick & 3
    first, second = (pick >> 2) & 127, pick >> 9

    def choose(zero, one, two):
        return jnp.where(depth == 0, zero, jnp.where(depth == 1, one, two))

    last = choose(SIDE - BLK, SIDE // 2 - BLK, 0)
    sx = jnp.minimum(choose(first, first >> 1, first >> 2), last)
    sy = jnp.minimum(choose(second, second >> 1, second >> 2), last)
    return depth, sx, sy


def pick_of(picks, row, col, d):
    target = lax.rem(row - STEP_ROWS[d] + ROWS, ROWS) * COLS
    return picks[d, target + lax.rem(col - STEP_COLS[d] + COLS, COLS)]


def pick_blocks(picks, row, col, field, grid, tmp, blocks):
    def widen(x, carry):
        grid[x, pl.ds(0, SIDE)] = field[x].astype(F32)
        return carry

    lax.fori_loop(0, SIDE, widen, 0, unroll=4)

    def pool1(x, carry):
        total = jnp.zeros((40, C), F32)
        for a in range(2):
            for b in range(2):
                total = total + grid[2 * x + a, pl.ds(b, 40, stride=2)]
        grid[SIDE + x, pl.ds(0, 40)] = (total * 0.25).astype(BF).astype(F32)
        return carry

    lax.fori_loop(0, 40, pool1, 0, unroll=4)

    def pool2(x, carry):
        total = jnp.zeros((20, C), F32)
        for a in range(4):
            for b in range(4):
                total = total + grid[4 * x + a, pl.ds(b, 20, stride=4)]
        grid[SIDE + 40 + x, pl.ds(0, 20)] = (total * 0.0625).astype(BF).astype(F32)
        return carry

    lax.fori_loop(0, 20, pool2, 0, unroll=4)
    for d in range(8):
        depth, sx, sy = start_of(pick_of(picks, row, col, d))
        base = sx + jnp.where(depth == 0, 0, jnp.where(depth == 1, SIDE, SIDE + 40))
        for a in range(BLK):
            tmp[pl.ds(BLK * a, 24)] = grid[base + a, pl.ds(sy, 24)]
        blocks[d] = tmp[pl.ds(0, 400)].astype(BF)


def forward_kernel(*refs):
    refs = list(refs)

    def take(n):
        taken = refs[:n]
        del refs[:n]
        return taken

    picks, field, ty, tx, w = take(5)
    z, bo, u, big_out = take(4)
    r0, sa, sb, r1a, r1b, acca, accb, r2a, r2b, zs, za, zb, wv = take(13)
    core_a, core_b, one_a, one_b, wide1_a, wide1_b, share_a, share_b = take(8)
    two_a, two_b, wide2_a, wide2_b, blocks, local = take(6)
    s, b, big, ay, tx_own, grid, tmp, ty_own = take(8)
    i, j = lax.axis_index("px"), lax.axis_index("py")
    y, zh = i // 2, i % 2
    zl, x, c = j // 8, (j // 2) % 4, j % 2
    spot = 2 * zl + zh
    sibling = (i, 8 * zl + 2 * x + 1 - c)

    def at_x(n):
        return (i, 8 * zl + 2 * n + c)

    def at_y(n):
        return (2 * n + zh, j)

    def at_z(n):
        return (2 * y + n % 2, 8 * (n // 2) + 2 * x + c)

    def at_yz(n):
        return (2 * (n // 4) + n % 2, 8 * (n // 2 % 2) + 2 * x + c)

    def at_xz(n):
        return (2 * y + n % 2, 8 * (n // 2 % 2) + 2 * (n // 4) + c)

    def partner(base, r):
        return 4 * ((base + r // 4) % 4) + (spot + r % 4) % 4

    def sender(base, r):
        return 4 * ((base - r // 4 + 4) % 4) + (spot - r % 4 + 4) % 4

    def loop15(body):
        def step(r, carry):
            body(r)
            return carry

        lax.fori_loop(1, 16, step, 0)

    def remote(src, dst, sems, sent, landed, device):
        return pltpu.make_async_remote_copy(
            src_ref=src,
            dst_ref=dst,
            send_sem=sems.at[0, sent],
            recv_sem=sems.at[1, landed],
            device_id=device,
            device_id_type=MESH,
        )

    def neighbour(d, sign):
        return (
            (i + sign * STEP_ROWS[d] + ROWS) % ROWS,
            (j + sign * STEP_COLS[d] + COLS) % COLS,
        )

    def band(n, size=32):
        return pl.ds(pl.multiple_of(n * size, size), size)

    barrier = pltpu.get_barrier_semaphore()
    partners = [sibling]
    for r in range(1, 16):
        partners.append(at_yz(partner(y, r)))
        if r > 3:
            partners.append(at_xz(partner(x, r)))
    partners += [neighbour(d, 1) for d in range(8)]
    weights = pltpu.make_async_copy(w, wv, local.at[0])
    table_x = pltpu.make_async_copy(tx.at[i], tx_own, local.at[4])
    keep = pltpu.make_async_copy(big, big_out, local.at[5])

    def greet():
        for device in partners:
            pl.semaphore_signal(barrier, inc=1, device_id=device, device_id_type=MESH)
        weights.start()
        table_x.start()

    greet()
    table_y = pltpu.make_async_copy(ty.at[j], ty_own, local.at[3])
    table_y.start()
    pick_blocks(picks, i, j, field, grid, tmp, b)

    def run():
        pl.semaphore_wait(barrier, len(partners))
        waits = []

        def begin(copy):
            copy.start()
            waits.append(copy)

        def core_copy_a(n):
            return remote(s.at[:, n, 1 - c, 0:2], r0.at[:, n, 0:2], core_a, n, n, sibling)

        def core_copy_b(n):
            src = s.at[:, :, 1 - c, 2:4, band(n)]
            return remote(src, r0.at[:, :, 2:4, band(n)], core_b, n, n, sibling)

        def block_copy(d):
            device = neighbour(d, -1)
            return remote(b.at[d], bo.at[d], blocks, d, d, device)

        def fill(n, half):
            def step(m, carry):
                a, e = m // 2, m % 2
                ky = 4 * (8 * a + 2 * n + e) + 2 * half
                first, second = x_to_modes(tx_own[...], ay, (ky, ky + 1))
                s[a, n, e, 2 * half] = first
                s[a, n, e, 2 * half + 1] = second
                return carry

            lax.fori_loop(0, 4, step, 0, unroll=4)

        for d in range(8):
            begin(block_copy(d))
        table_y.wait()
        build_to_modes(ty_own[...], big)
        keep.start()
        y_to_modes(big, field, ay)
        table_x.wait()
        for r in (2, 1, 3, 0):
            n = (x + r) % 4
            fill(n, 0)
            begin(core_copy_a(n))
        def one_copy_a(n, slot, device):
            return remote(sa.at[n], r1a.at[slot], one_a, n, slot, device)

        def one_copy_b(n, slot, device):
            return remote(sb.at[n], r1b.at[slot], one_b, n, slot, device)

        def sum_a(n):
            core_copy_a(n).wait_recv()
            return s[:, n, c, 0:2].astype(F32) + r0[:, n, 0:2].astype(F32)

        def sum_b(n):
            core_copy_b(n).wait_recv()
            rows = band(n)
            return s[:, :, c, 2:4, rows].astype(F32) + r0[:, :, 2:4, rows].astype(F32)

        def pass_a(r):
            n = (x + r) % 4
            sa[n] = sum_a(n).astype(BF)
            begin(one_copy_a(n, x, at_x(n)))

        def pass_b(r):
            n = (y + r) % 4
            sb[n] = sum_b(n).astype(BF)
            begin(one_copy_b(n, y, at_y(n)))

        for r in (2, 1, 3, 0):
            fill((x + r) % 4, 1)
            if r:
                pass_a(r)
        for r in (2, 1, 3, 0):
            begin(core_copy_b((y + r) % 4))
        for r in (2, 1, 3):
            pass_b(r)
        acca[...] = sum_a(x)
        accb[...] = sum_b(y)
        for r in (1, 3, 2):
            n = (x + r) % 4
            one_copy_a(n, n, at_x(n)).wait_recv()
            acca[...] = acca[...] + r1a[n].astype(F32)

        def two_copy_a(n, slot, device):
            src = acca.at[n // 2 % 2, :, band(2 * (n // 4) + n % 2, 16)]
            return remote(src, r2a.at[slot], two_a, n, slot, device)

        def two_copy_b(n, slot, device):
            src = accb.at[n // 2 % 2, n // 4, :, band(n % 2, 16)]
            return remote(src, r2b.at[slot], two_b, n, slot, device)

        def send_two_a(r):
            n = partner(y, r)
            two_copy_a(n, 4 * y + spot, at_yz(n)).start()

        def send_two_b(r):
            n = partner(x, r)
            two_copy_b(n, 4 * x + spot, at_xz(n)).start()

        loop15(send_two_a)
        for r in (1, 3, 2):
            n = (y + r) % 4
            one_copy_b(n, n, at_y(n)).wait_recv()
            accb[...] = accb[...] + r1b[n].astype(F32)
        loop15(send_two_b)
        u[0:2] = acca[zl, :, band(i, 16)]
        u[2:4] = accb[zl, x, :, band(zh, 16)]

        def gather_two_a(r):
            n = sender(y, r)
            two_copy_a(n, n, at_yz(n)).wait_recv()
            u[0:2] = u[0:2] + r2a[n]

        def gather_two_b(r):
            n = sender(x, r)
            two_copy_b(n, n, at_xz(n)).wait_recv()
            u[2:4] = u[2:4] + r2b[n]

        loop15(gather_two_a)
        loop15(gather_two_b)
        weights.wait()
        same = iota((16, 16), 0) ^ 1
        turn = jnp.where(iota((16, 16), 1) == same, 1.0, 0.0)
        odd = (iota((16, 16), 0) & 1) == 1
        flip = jnp.logical_not(odd)
        turn = jnp.where(flip, -turn, turn).astype(BF)

        def mix(ky, carry):
            first = u[ky]
            high = first.astype(BF)
            low = (first - high.astype(F32)).astype(BF)
            both = jnp.concatenate([high, low], axis=0)
            turned = jnp.concatenate([dot(turn, high), dot(turn, low)], axis=0).astype(BF)
            both = jnp.concatenate([both, turned], axis=1)
            total = jnp.zeros((16, C), F32)
            for kx in range(8):
                mat = jnp.concatenate([wv[0, kx, ky], wv[1, kx, ky]], axis=0).astype(BF)
                res = dot(both, mat)
                total = jnp.where((iota((16, C), 0) >> 1) == kx, res[:16] + res[16:], total)
            zs[ky] = total.astype(BF)
            return carry

        lax.fori_loop(0, 4, mix, 0)

        def wide_copy2_a(slot, sent, device):
            dst = za.at[slot // 2 % 2, :, band(2 * (slot // 4) + slot % 2, 16)]
            return remote(zs.at[0:2], dst, wide2_a, sent, slot, device)

        def wide_copy2_b(slot, sent, device):
            dst = zb.at[slot // 2 % 2, slot // 4, :, band(slot % 2, 16)]
            return remote(zs.at[2:4], dst, wide2_b, sent, slot, device)

        def send_wide_a(r):
            n = partner(y, r)
            wide_copy2_a(4 * y + spot, n, at_yz(n)).start()

        def send_wide_b(r):
            n = partner(x, r)
            wide_copy2_b(4 * x + spot, n, at_xz(n)).start()

        loop15(send_wide_a)
        loop15(send_wide_b)
        za[zl, :, band(i, 16)] = zs[0:2]
        zb[zl, x, :, band(zh, 16)] = zs[2:4]
        def part_a(n, core):
            return z.at[:, n, core, 0:2]

        def part_b(n, core):
            return z.at[:, :, core, 2:4, band(n)]

        def wide_copy1_a(slot, sent, device):
            return remote(za, part_a(slot, c), wide1_a, sent, slot, device)

        def wide_copy1_b(slot, sent, device):
            return remote(zb, part_b(slot, c), wide1_b, sent, slot, device)

        def gather_wide_a(r):
            n = sender(y, r)
            wide_copy2_a(n, n, at_yz(n)).wait_recv()

        def gather_wide_b(r):
            n = sender(x, r)
            wide_copy2_b(n, n, at_xz(n)).wait_recv()

        loop15(gather_wide_a)
        for r in (2, 1, 3):
            n = (x + r) % 4
            begin(wide_copy1_a(x, n, at_x(n)))
        loop15(gather_wide_b)
        for r in (2, 1, 3):
            n = (y + r) % 4
            begin(wide_copy1_b(y, n, at_y(n)))
        own_a = pltpu.make_async_copy(za, part_a(x, c), local.at[1])
        own_a.start()
        own_b = pltpu.make_async_copy(zb, part_b(y, c), local.at[2])
        own_b.start()
        begin(remote(za, part_a(x, c), share_a, x, x, sibling))
        begin(remote(zb, part_b(y, c), share_b, y, y, sibling))
        def share_copy_a(n, core):
            return remote(part_a(n, core), part_a(n, core), share_a, n, n, sibling)

        def share_copy_b(n, core):
            return remote(part_b(n, core), part_b(n, core), share_b, n, n, sibling)

        for r in (1, 3, 2):
            n = (x + r) % 4
            wide_copy1_a(n, n, at_x(n)).wait_recv()
            begin(share_copy_a(n, c))
            n = (y + r) % 4
            wide_copy1_b(n, n, at_y(n)).wait_recv()
            begin(share_copy_b(n, c))
        for n in range(4):
            share_copy_a(n, 1 - c).wait_recv()
            share_copy_b(n, 1 - c).wait_recv()
        for d in range(8):
            block_copy(d).wait_recv()
        own_a.wait()
        own_b.wait()
        keep.wait()
        for copy in waits:
            copy.wait_send()

        def settle(r):
            n, m = partner(y, r), partner(x, r)
            two_copy_a(n, 4 * y + spot, at_yz(n)).wait_send()
            two_copy_b(m, 4 * x + spot, at_xz(m)).wait_send()
            wide_copy2_a(4 * y + spot, n, at_yz(n)).wait_send()
            wide_copy2_b(4 * x + spot, m, at_xz(m)).wait_send()

        loop15(settle)

    run()


def cells_kernel(*refs):
    refs = list(refs)

    def take(n):
        taken = refs[:n]
        del refs[:n]
        return taken

    cells_in = take(10)
    tx, big_in, w = take(3)
    layer_out, pre_out, z, bo, u, to = take(6)
    r0, sa, sb, r1a, r1b, acca, accb, r2a, r2b, ab, r3, zs, zz, za, zb, wv = take(16)
    core_a, core_b, one_a, one_b, two_a, two_b, three, wide3 = take(8)
    wide2_a, wide2_b, wide1_a, wide1_b, share_a, share_b, blocks, local = take(8)
    t0, t1s, t1, t2s, t2, t3s, t3, tall = take(8)
    core_t, one_t, two_t, three_t, wide2_t, wide1_t, share_t = take(7)
    s, b, big, ay, tx_own, t = take(6)
    step = pl.program_id(0)
    i, j = lax.axis_index("px"), lax.axis_index("py")
    y, zh = i // 2, i % 2
    zl, x, c = j // 8, (j // 2) % 4, j % 2
    spot = 2 * zl + zh
    sibling = (i, 8 * zl + 2 * x + 1 - c)

    def at_x(n):
        return (i, 8 * zl + 2 * n + c)

    def at_y(n):
        return (2 * n + zh, j)

    def at_z(n):
        return (2 * y + n % 2, 8 * (n // 2) + 2 * x + c)

    def remote(src, dst, sems, sent, landed, device):
        return pltpu.make_async_remote_copy(
            src_ref=src,
            dst_ref=dst,
            send_sem=sems.at[0, sent],
            recv_sem=sems.at[1, landed],
            device_id=device,
            device_id_type=MESH,
        )

    def neighbour(d, sign):
        return (
            (i + sign * STEP_ROWS[d] + ROWS) % ROWS,
            (j + sign * STEP_COLS[d] + COLS) % COLS,
        )

    def band(n, size=32):
        return pl.ds(pl.multiple_of(n * size, size), size)

    barrier = pltpu.get_barrier_semaphore()
    partners = [sibling]
    for r in (1, 2, 3):
        partners += [at_x((x + r) % 4), at_y((y + r) % 4), at_z((spot + r) % 4)]
    partners += [neighbour(d, 1) for d in range(8)]
    weights = pltpu.make_async_copy(w, wv, local.at[0])
    table_x = pltpu.make_async_copy(tx.at[i], tx_own, local.at[4])
    keep = pltpu.make_async_copy(big_in, big, local.at[5])
    def greet():
        for device in partners:
            pl.semaphore_signal(barrier, inc=1, device_id=device, device_id_type=MESH)
        weights.start()
        table_x.start()


    @pl.when(step == 0)
    def _():
        keep.start()
        greet()

    tail = cells_body(
        step, i, j, keep, cells_in, layer_out, pre_out, ay, big, b, t, refs
    )
    def run():
        pl.semaphore_wait(barrier, len(partners))
        waits = []

        def begin(copy):
            copy.start()
            waits.append(copy)

        def core_copy_a(n):
            return remote(s.at[:, n, 1 - c, 0:2], r0.at[:, n, 0:2], core_a, n, n, sibling)

        def core_copy_b(n):
            src = s.at[:, :, 1 - c, 2:4, band(n)]
            return remote(src, r0.at[:, :, 2:4, band(n)], core_b, n, n, sibling)

        def block_copy(d):
            device = neighbour(d, 1)
            return remote(b.at[d], bo.at[d], blocks, d, d, device)

        def fill(n, half):
            def step(m, carry):
                a, e = m // 2, m % 2
                ky = 4 * (8 * a + 2 * n + e) + 2 * half
                first, second = x_to_modes(tx_own[...], ay, (ky, ky + 1))
                s[a, n, e, 2 * half] = first
                s[a, n, e, 2 * half + 1] = second
                return carry

            lax.fori_loop(0, 4, step, 0, unroll=4)

        table_x.wait()
        for r in (2, 1, 3, 0):
            n = (x + r) % 4
            fill(n, 0)
            begin(core_copy_a(n))

        def core_copy_t():
            return remote(t.at[1 - c], t0, core_t, 0, 0, sibling)

        def one_copy_a(n, slot, device):
            return remote(sa.at[n], r1a.at[slot], one_a, n, slot, device)

        def one_copy_b(n, slot, device):
            return remote(sb.at[n], r1b.at[slot], one_b, n, slot, device)

        def sum_a(n):
            core_copy_a(n).wait_recv()
            return s[:, n, c, 0:2].astype(F32) + r0[:, n, 0:2].astype(F32)

        def sum_b(n):
            core_copy_b(n).wait_recv()
            rows = band(n)
            return s[:, :, c, 2:4, rows].astype(F32) + r0[:, :, 2:4, rows].astype(F32)

        def pass_a(r):
            n = (x + r) % 4
            sa[n] = sum_a(n).astype(BF)
            begin(one_copy_a(n, x, at_x(n)))

        def pass_b(r):
            n = (y + r) % 4
            sb[n] = sum_b(n).astype(BF)
            begin(one_copy_b(n, y, at_y(n)))

        for r in (2, 1, 3, 0):
            fill((x + r) % 4, 1)
            if r:
                pass_a(r)
        for r in (2, 1, 3, 0):
            begin(core_copy_b((y + r) % 4))
        for r in (2, 1, 3):
            pass_b(r)
        tail()
        begin(core_copy_t())
        for d in range(8):
            begin(block_copy(d))
        acca[...] = sum_a(x)
        accb[...] = sum_b(y)

        def one_copy_t(n, slot, device):
            return remote(t1s.at[n], t1.at[slot], one_t, n, slot, device)

        core_copy_t().wait_recv()
        t1s[...] = (t[c].astype(F32) + t0[...].astype(F32)).astype(BF)
        for r in (2, 1, 3):
            n = (x + r) % 4
            begin(one_copy_t(n, x, at_x(n)))
        for r in (1, 3, 2):
            n = (x + r) % 4
            one_copy_a(n, n, at_x(n)).wait_recv()
            acca[...] = acca[...] + r1a[n].astype(F32)

        def two_copy_a(n, slot, device):
            return remote(acca.at[:, :, band(n)], r2a.at[slot], two_a, n, slot, device)

        def two_copy_b(n, slot, device):
            return remote(accb.at[:, n], r2b.at[slot], two_b, n, slot, device)

        for r in (2, 1, 3):
            n = (y + r) % 4
            begin(two_copy_a(n, y, at_y(n)))
        for r in (1, 3, 2):
            n = (y + r) % 4
            one_copy_b(n, n, at_y(n)).wait_recv()
            accb[...] = accb[...] + r1b[n].astype(F32)
        for r in (2, 1, 3):
            n = (x + r) % 4
            begin(two_copy_b(n, x, at_x(n)))
        ab[:, 0:2] = acca[:, :, band(y)]
        ab[:, 2:4] = accb[:, x]
        for r in (1, 3, 2):
            n = (y + r) % 4
            two_copy_a(n, n, at_y(n)).wait_recv()
            ab[:, 0:2] = ab[:, 0:2] + r2a[n]
        for r in (1, 3, 2):
            n = (x + r) % 4
            two_copy_b(n, n, at_x(n)).wait_recv()
            ab[:, 2:4] = ab[:, 2:4] + r2b[n]

        def three_copy(n, slot, device):
            return remote(ab.at[n // 2, :, band(n % 2, 16)], r3.at[slot], three, n, slot, device)

        for r in (2, 1, 3):
            n = (spot + r) % 4
            begin(three_copy(n, spot, at_z(n)))

        def two_copy_t(n, slot, device):
            return remote(t2s.at[n], t2.at[slot], two_t, n, slot, device)

        total = t1s[x].astype(F32)
        for r in (1, 3, 2):
            n = (x + r) % 4
            one_copy_t(n, n, at_x(n)).wait_recv()
            total = total + t1[n].astype(F32)
        t2s[...] = total.astype(BF)
        for r in (2, 1, 3):
            n = (y + r) % 4
            begin(two_copy_t(n, y, at_y(n)))
        u[...] = ab[zl, :, band(zh, 16)]
        for r in (1, 3, 2):
            n = (spot + r) % 4
            three_copy(n, n, at_z(n)).wait_recv()
            u[...] = u[...] + r3[n]
        u[...] = u[...] * math.sqrt(NX * NY / (MX * MY))
        weights.wait()
        same = iota((16, 16), 0) ^ 1
        turn = jnp.where(iota((16, 16), 1) == same, 1.0, 0.0)
        odd = (iota((16, 16), 0) & 1) == 1
        flip = odd
        turn = jnp.where(flip, -turn, turn).astype(BF)

        def mix(ky, carry):
            first = u[ky]
            high = first.astype(BF)
            low = (first - high.astype(F32)).astype(BF)
            both = jnp.concatenate([high, low], axis=0)
            turned = jnp.concatenate([dot(turn, high), dot(turn, low)], axis=0).astype(BF)
            both = jnp.concatenate([both, turned], axis=1)
            total = jnp.zeros((16, C), F32)
            for kx in range(8):
                mat = jnp.concatenate([wv[0, kx, ky], wv[1, kx, ky]], axis=1).astype(BF)
                res = dot_tb(both, mat)
                total = jnp.where((iota((16, C), 0) >> 1) == kx, res[:16] + res[16:], total)
            zs[ky] = total.astype(BF)
            return carry

        lax.fori_loop(0, 4, mix, 0)

        def wide_copy3(slot, sent, device):
            dst = zz.at[slot // 2, :, band(slot % 2, 16)]
            return remote(zs, dst, wide3, sent, slot, device)

        for r in (2, 1, 3):
            n = (spot + r) % 4
            begin(wide_copy3(spot, n, at_z(n)))
        zz[zl, :, band(zh, 16)] = zs[...]
        t3s[...] = t2s[y]
        total = t3s[...].astype(F32)
        for r in (1, 3, 2):
            n = (y + r) % 4
            two_copy_t(n, n, at_y(n)).wait_recv()
            total = total + t2[n].astype(F32)
        t3s[...] = total.astype(BF)
        t3[spot] = t3s[...]

        def three_copy_t(slot, sent, device):
            return remote(t3s, t3.at[slot], three_t, sent, slot, device)

        for r in (2, 1, 3):
            n = (spot + r) % 4
            begin(three_copy_t(spot, n, at_z(n)))
        for r in (1, 3, 2):
            n = (spot + r) % 4
            wide_copy3(n, n, at_z(n)).wait_recv()

        def wide_copy2_a(slot, sent, device):
            return remote(zz.at[:, 0:2], za.at[:, :, band(slot)], wide2_a, sent, slot, device)

        def wide_copy2_b(slot, sent, device):
            return remote(zz.at[:, 2:4], zb.at[:, slot], wide2_b, sent, slot, device)

        for r in (2, 1, 3):
            n = (y + r) % 4
            begin(wide_copy2_a(y, n, at_y(n)))
            n = (x + r) % 4
            begin(wide_copy2_b(x, n, at_x(n)))
        za[:, :, band(y)] = zz[:, 0:2]
        zb[:, x] = zz[:, 2:4]
        for r in (1, 3, 2):
            n = (spot + r) % 4
            three_copy_t(n, n, at_z(n)).wait_recv()
        total = t3[0].astype(F32)
        for n in range(1, 4):
            total = total + t3[n].astype(F32)
        tall[x, y] = total.astype(BF)

        def wide_copy2_t(slot, sent, device):
            piece = tall.at[x, slot]
            return remote(piece, piece, wide2_t, sent, slot, device)

        for r in (2, 1, 3):
            n = (y + r) % 4
            begin(wide_copy2_t(y, n, at_y(n)))

        def part_a(n, core):
            return z.at[:, n, core, 0:2]

        def part_b(n, core):
            return z.at[:, :, core, 2:4, band(n)]

        def wide_copy1_a(slot, sent, device):
            return remote(za, part_a(slot, c), wide1_a, sent, slot, device)

        def wide_copy1_b(slot, sent, device):
            return remote(zb, part_b(slot, c), wide1_b, sent, slot, device)

        for r in (1, 3, 2):
            n = (y + r) % 4
            wide_copy2_a(n, n, at_y(n)).wait_recv()
        for r in (2, 1, 3):
            n = (x + r) % 4
            begin(wide_copy1_a(x, n, at_x(n)))
        for r in (1, 3, 2):
            n = (x + r) % 4
            wide_copy2_b(n, n, at_x(n)).wait_recv()
        for r in (2, 1, 3):
            n = (y + r) % 4
            begin(wide_copy1_b(y, n, at_y(n)))
        own_a = pltpu.make_async_copy(za, part_a(x, c), local.at[1])
        own_a.start()
        own_b = pltpu.make_async_copy(zb, part_b(y, c), local.at[2])
        own_b.start()
        begin(remote(za, part_a(x, c), share_a, x, x, sibling))
        begin(remote(zb, part_b(y, c), share_b, y, y, sibling))
        for r in (1, 3, 2):
            n = (y + r) % 4
            wide_copy2_t(n, n, at_y(n)).wait_recv()

        def wide_copy1_t(slot, sent, device):
            piece = tall.at[slot]
            return remote(piece, piece, wide1_t, sent, slot, device)

        for r in (2, 1, 3):
            n = (x + r) % 4
            begin(wide_copy1_t(x, n, at_x(n)))

        def share_copy_a(n, core):
            return remote(part_a(n, core), part_a(n, core), share_a, n, n, sibling)

        def share_copy_b(n, core):
            return remote(part_b(n, core), part_b(n, core), share_b, n, n, sibling)

        for r in (1, 3, 2):
            n = (x + r) % 4
            wide_copy1_a(n, n, at_x(n)).wait_recv()
            begin(share_copy_a(n, c))
            n = (y + r) % 4
            wide_copy1_b(n, n, at_y(n)).wait_recv()
            begin(share_copy_b(n, c))
        for r in (1, 3, 2):
            n = (x + r) % 4
            wide_copy1_t(n, n, at_x(n)).wait_recv()
        share = remote(tall, to.at[c], share_t, 0, 0, sibling)
        begin(share)
        own_t = pltpu.make_async_copy(tall, to.at[c], local.at[3])
        own_t.start()
        for n in range(4):
            share_copy_a(n, 1 - c).wait_recv()
            share_copy_b(n, 1 - c).wait_recv()
        for d in range(8):
            block_copy(d).wait_recv()
        own_a.wait()
        own_b.wait()
        share.wait_recv()
        own_t.wait()
        for copy in waits:
            copy.wait_send()

    pl.when(step == 4)(run)


def whole(*shape):
    zeros = (0,) * len(shape)
    return pl.BlockSpec(shape, lambda n: zeros)


def forward_call(*operands):
    shape = jax.ShapeDtypeStruct
    out_shape = [shape((2, 4, 2, 4, 128, C), BF), shape((8, 400, C), BF), shape((4, 16, C), F32)]
    out_shape.append(shape((1024, 640), BF))
    out_specs = [HB, HB, VM, HB]
    in_specs = [SM, VM, HB, HB, HB]
    sem = pltpu.SemaphoreType.DMA((2, 4))
    scratch = [
        pltpu.VMEM((2, 4, 4, 128, C), BF),
        pltpu.VMEM((4, 2, 2, 128, C), BF),
        pltpu.VMEM((4, 2, 4, 2, 32, C), BF),
        pltpu.VMEM((4, 2, 2, 128, C), BF),
        pltpu.VMEM((4, 2, 4, 2, 32, C), BF),
        pltpu.VMEM((2, 2, 128, C), F32),
        pltpu.VMEM((2, 4, 2, 32, C), F32),
        pltpu.VMEM((16, 2, 16, C), F32),
        pltpu.VMEM((16, 2, 16, C), F32),
        pltpu.VMEM((4, 16, C), BF),
        pltpu.VMEM((2, 2, 128, C), BF),
        pltpu.VMEM((2, 4, 2, 32, C), BF),
        pltpu.VMEM((2, 8, 4, C, C), F32),
    ]
    scratch += [sem] * 8 + [pltpu.SemaphoreType.DMA((2, 16))] * 4 + [pltpu.SemaphoreType.DMA((2, 8)), pltpu.SemaphoreType.DMA((6,))]
    scratch += [
        pltpu.VMEM((2, 4, 2, 4, 128, C), BF),
        pltpu.VMEM((8, 400, C), BF),
        pltpu.VMEM((1024, 640), BF),
        pltpu.VMEM((10, 128, 8, C), F32),
        pltpu.VMEM((128, 480), BF),
    ]
    scratch += [
        pltpu.VMEM((SIDE + 60, 88, C), F32),
        pltpu.VMEM((408, C), F32),
        pltpu.VMEM((128, SIDE), BF),
    ]
    return pl.pallas_call(
        forward_kernel,
        out_shape=tuple(out_shape),
        in_specs=in_specs,
        out_specs=tuple(out_specs),
        scratch_shapes=scratch,
        compiler_params=pltpu.CompilerParams(
            collective_id=1,
            has_side_effects=True,
            vmem_limit_bytes=VMEM_LIMIT,
        ),
        name="forward_and_exchange",
    )(*operands)


def cells_call(*operands):
    shape = jax.ShapeDtypeStruct
    out_shape = [shape((2, 4, 2, 4, 128, C), BF), shape((8, 400, C), BF), shape((4, 16, C), F32)]
    tile = pl.BlockSpec((16, SIDE, C), lambda n: (n, 0, 0))
    field = shape((SIDE, SIDE, C), BF)
    out_shape = [field, field] + out_shape + [shape((2, 4, 4, PIECE, C), BF)]
    out_specs = [tile, tile, HB, HB, whole(4, 16, C), HB]
    in_specs = [tile, tile, whole(64, 128, C), whole(8, 400, C), whole(C, C)]
    in_specs += [whole(8, C, C), whole(C, H), whole(H, C), whole(COLS, SIDE, 128)]
    in_specs += [whole(ROWS, 160, 256), HB, HB, HB]
    sem = pltpu.SemaphoreType.DMA((2, 4))
    scratch = [
        pltpu.VMEM((2, 4, 4, 128, C), BF),
        pltpu.VMEM((4, 2, 2, 128, C), BF),
        pltpu.VMEM((4, 2, 4, 2, 32, C), BF),
        pltpu.VMEM((4, 2, 2, 128, C), BF),
        pltpu.VMEM((4, 2, 4, 2, 32, C), BF),
        pltpu.VMEM((2, 2, 128, C), F32),
        pltpu.VMEM((2, 4, 2, 32, C), F32),
        pltpu.VMEM((4, 2, 2, 32, C), F32),
        pltpu.VMEM((4, 2, 2, 32, C), F32),
        pltpu.VMEM((2, 4, 32, C), F32),
        pltpu.VMEM((4, 4, 16, C), F32),
        pltpu.VMEM((4, 16, C), BF),
        pltpu.VMEM((2, 4, 32, C), BF),
        pltpu.VMEM((2, 2, 128, C), BF),
        pltpu.VMEM((2, 4, 2, 32, C), BF),
        pltpu.VMEM((2, 8, 4, C, C), F32),
    ]
    scratch += [sem] * 14 + [pltpu.SemaphoreType.DMA((2, 8)), pltpu.SemaphoreType.DMA((6,))]
    scratch += [
        pltpu.VMEM((4, 4, PIECE, C), BF),
        pltpu.VMEM((4, 4, PIECE, C), BF),
        pltpu.VMEM((4, 4, PIECE, C), BF),
        pltpu.VMEM((4, PIECE, C), BF),
        pltpu.VMEM((4, PIECE, C), BF),
        pltpu.VMEM((PIECE, C), BF),
        pltpu.VMEM((4, PIECE, C), BF),
        pltpu.VMEM((4, 4, PIECE, C), BF),
    ] + [sem] * 7
    scratch += [
        pltpu.VMEM((2, 4, 2, 4, 128, C), BF),
        pltpu.VMEM((8, 400, C), BF),
        pltpu.VMEM((1024, 640), BF),
        pltpu.VMEM((10, 128, 8, C), F32),
        pltpu.VMEM((128, 480), BF),
    ]
    scratch += [
        pltpu.VMEM((2, 4, 4, PIECE, C), BF),
        pltpu.VMEM((10, 128, 8, C), F32),
        pltpu.VMEM((640, 1024), BF),
        pltpu.VMEM((1280, 160), BF),
        pltpu.VMEM((80, 1280), BF),
        pltpu.VMEM((400, C), F32),
        pltpu.VMEM((400, C), F32),
        pltpu.VMEM((1280, C), F32),
        pltpu.VMEM((1280, C), F32),
        pltpu.VMEM((1280, C), BF),
        pltpu.VMEM((1280, H), F32),
        pltpu.VMEM((1280, H), F32),
        pltpu.VMEM((1280, H), BF),
        pltpu.VMEM((1280, H), BF),
        pltpu.VMEM((C, C), F32),
        pltpu.VMEM((C, H), F32),
        pltpu.VMEM((C, H), F32),
    ]
    return pl.pallas_call(
        cells_kernel,
        out_shape=tuple(out_shape),
        in_specs=in_specs,
        out_specs=tuple(out_specs),
        scratch_shapes=scratch,
        grid=(5,),
        compiler_params=pltpu.CompilerParams(
            collective_id=2,
            has_side_effects=True,
            vmem_limit_bytes=VMEM_LIMIT,
        ),
        name="cells_and_exchange",
    )(*operands)


def gelu_both(v):
    square = v * v
    t = jnp.tanh(v * (TANH_SCALE + (TANH_SCALE * CUBIC_TERM) * square))
    half = 0.5 + 0.5 * t
    inner = (0.5 * TANH_SCALE) + (1.5 * TANH_SCALE * CUBIC_TERM) * square
    return v * half, half + v * (1.0 - t * t) * inner


def store_rows(tot, first, rows):
    done = 0
    while done < rows.shape[0]:
        place, inside = divmod(first + done, PIECE)
        count = min(PIECE - inside, rows.shape[0] - done)
        spot = (place // 16, place // 4 % 4, place % 4)
        tot[spot + (pl.ds(inside, count),)] = rows[done : done + count]
        done += count


def cells_body(step, row, col, keep, inputs, layer, pre_out, ay, big, bgrad, tot, scratch):
    field, cot, z, blk, skip, ctx, up, down, gy, gx = inputs
    p, cells_big, spread, gather, coarse, cell, pre, slope, mid = scratch[:9]
    lifted, dh, hid, lg, acc_skip, acc_up, acc_down = scratch[9:]

    @pl.when(step == 0)
    def _():
        x_to_cells(gx[row], z, p)
        build_to_cells(gy[col], cells_big)
        total = dot(blk[0], ctx[0])
        for d in range(1, 8):
            total = total + dot(blk[d], ctx[d])
        coarse[...] = total
        n, l = iota((1280, 160), 0), iota((1280, 160), 1)
        l = jnp.where(l >= 80, l - 80, l)
        x = over_80(n)
        y = n - 80 * x
        a = over_20(l)
        hit = ((x >> 2) == a) & ((y >> 2) == l - 20 * a)
        spread[...] = jnp.where(hit, 1.0, 0.0).astype(BF)
        l, n = iota((80, 1280), 0), iota((80, 1280), 1)
        x = over_80(n)
        y = n - 80 * x
        a = over_20(l)
        hit = ((x >> 2) == a) & ((y >> 2) == l - 20 * a)
        gather[...] = jnp.where(hit, 1.0, 0.0).astype(BF)
        acc_skip[...] = jnp.zeros_like(acc_skip)
        acc_up[...] = jnp.zeros_like(acc_up)
        acc_down[...] = jnp.zeros_like(acc_down)

    own_rows = pl.ds(pl.multiple_of(80 * step, 8), 80)
    flat = field[...].reshape(1280, C)
    flat_cot = cot[...].reshape(1280, C)
    wide = jnp.concatenate(
        [p[2 * step].reshape(1024, C).astype(BF), p[2 * step + 1].reshape(1024, C).astype(BF)],
        axis=1,
    )
    own = coarse[own_rows]
    high = own.astype(BF)
    low = (own - high.astype(F32)).astype(BF)
    rest = dot(flat, skip[...]) + dot(spread[...], jnp.concatenate([high, low], axis=0))
    for part in range(640 // 160):
        lo, hi = 160 * part, 160 * part + 160
        spectral = dot(cells_big[pl.ds(lo, 160)], wide)
        pre[pl.ds(lo, 160)] = spectral[:, :C].astype(BF).astype(F32) + rest[lo:hi]
        pre[pl.ds(640 + lo, 160)] = spectral[:, C:].astype(BF).astype(F32) + rest[640 + lo : 640 + hi]

    def activate(n, carry):
        rows = pl.ds(pl.multiple_of(64 * n, 64), 64)
        value, slant = gelu_both(pre[rows])
        mid[rows] = value.astype(BF)
        slope[rows] = slant
        return carry

    lax.fori_loop(0, 20, activate, 0, unroll=20)
    lifted[...] = dot(mid[...], up[...])
    dh[...] = dot_tb(flat_cot, down[...])

    def activate_wide(n, carry):
        rows = pl.ds(pl.multiple_of(16 * n, 16), 16)
        value, slant = gelu_both(lifted[rows])
        hid[rows] = value.astype(BF)
        lg[rows] = (dh[rows] * slant).astype(BF)
        return carry

    lax.fori_loop(0, 80, activate_wide, 0, unroll=80)
    result = mid[...].astype(F32) + dot(hid[...], down[...])
    layer[...] = result.astype(BF).reshape(16, SIDE, C)
    grad = flat_cot.astype(F32) + dot_tb(lg[...], up[...])
    grad = (grad * slope[...]).astype(BF)
    pre_out[...] = grad.reshape(16, SIDE, C)
    acc_skip[...] += dot_ta(flat, grad)
    acc_up[...] += dot_ta(mid[...], lg[...])
    acc_down[...] += dot_ta(flat_cot, hid[...])
    cell[own_rows] = dot(gather[...], grad)
    pl.when(step == 0)(keep.wait)
    y_store(big, jnp.concatenate([grad[:640], grad[640:]], axis=1), ay, step)

    def tail():
        narrow = cell[...].astype(BF)
        store_rows(tot, 0, acc_skip[...].astype(BF))
        for d in range(8):
            store_rows(tot, 128 + 128 * d, dot_ta(blk[d], narrow).astype(BF))
            bgrad[d] = dot_tb(narrow, ctx[d]).astype(BF)
        for part in range(4):
            cut = slice(128 * part, 128 * part + 128)
            store_rows(tot, 1152 + 128 * part, acc_up[:, cut].astype(BF))
            store_rows(tot, 1664 + 128 * part, acc_down[:, cut].T.astype(BF))
        store_rows(tot, 2176, jnp.zeros((TOT - 2176, C), BF))

    return tail


def outer(u, g, spec):
    turn = jnp.where(iota((16, 16), 1) == (iota((16, 16), 0) ^ 1), 1.0, 0.0)
    turn = jnp.where((iota((16, 16), 0) & 1) == 1, -turn, turn).astype(BF)
    left_high = u.astype(BF)
    left_low = (u - left_high.astype(F32)).astype(BF)
    right_high = g.astype(BF)
    right_low = (g - right_high.astype(F32)).astype(BF)
    high = jnp.concatenate([right_high, dot(turn, right_high).astype(BF)], axis=1)
    low = jnp.concatenate([right_low, dot(turn, right_low).astype(BF)], axis=1)
    lefts = jnp.concatenate([left_high, left_high, left_low], axis=0).astype(F32).T.astype(BF)
    rights = jnp.concatenate([high, low, high], axis=0)
    row = (iota((48, 2 * C), 0) & 15) >> 1
    for kx in range(8):
        res = dot(lefts, jnp.where(row == kx, rights, jnp.zeros_like(rights)))
        spec[0, kx, 0] = res[:, :C]
        spec[1, kx, 0] = res[:, C:]


def weight_sums(tot, skip, ctx, up, down):
    inv = 1.0 / math.sqrt(NX * NY)
    skip[...] = tot[pl.ds(0, 128)].astype(F32) * inv
    for d in range(8):
        ctx[d] = tot[pl.ds(128 + 128 * d, 128)].astype(F32) * inv
    for part in range(4):
        cut = slice(128 * part, 128 * part + 128)
        up[:, cut] = tot[pl.ds(1152 + 128 * part, 128)].astype(F32) * inv
    down[...] = tot[pl.ds(1664, 512)].astype(F32) * inv


def last_kernel(
    picks, pre, z, back, skip, gy, gx, u, g, tot,
    out, spec, skip_out, ctx_out, up_out, down_out, p, cells_big, place, grads, wide,
):
    step = pl.program_id(0)
    row, col = lax.axis_index("px"), lax.axis_index("py")
    starts = [start_of(pick_of(picks, row, col, d)) for d in range(8)]

    @pl.when(step == 0)
    def _():
        x_to_cells(gx[row], z, p)
        build_to_cells(gy[col], cells_big)
        y, lane = iota((SIDE, 192), 0), iota((SIDE, 192), 1)
        total = jnp.zeros((SIDE, 192), F32)
        for d in range(8):
            depth, sx, sy = starts[d]
            share = jnp.where(depth == 0, 1.0, jnp.where(depth == 1, 0.25, 0.0625))
            spot = lane - 24 * d
            line = jnp.where(depth == 0, y, jnp.where(depth == 1, y >> 1, y >> 2))
            hit = (spot >= 0) & (spot < BLK) & (line - sy == spot)
            total = jnp.where(hit, share, total)
        place[...] = total.astype(BF)
        wide[pl.ds(400, 8)] = jnp.zeros((8, C), F32)
        for d in range(8):
            wide[pl.ds(0, 400)] = back[d].astype(F32)
            for a in range(BLK):
                grads[d, a] = wide[pl.ds(BLK * a, 24)]
            grads[d, BLK] = jnp.zeros((24, C), F32)

    @pl.when(step < 4)
    def _():
        outer(u[step], g[step], spec)

    pl.when(step == 4)(lambda: weight_sums(tot, skip_out, ctx_out, up_out, down_out))
    both = jnp.concatenate(
        [p[2 * step].reshape(1024, C).astype(BF), p[2 * step + 1].reshape(1024, C).astype(BF)],
        axis=1,
    )
    factor = math.sqrt(MX * MY / (NX * NY))
    straight = dot_tb(pre[...].reshape(1280, C), skip[...])
    for k in range(8):
        spectral = dot(cells_big[pl.ds(SIDE * k, SIDE)], both) * factor
        wide_pieces = []
        for x in (k, k + 8):
            pieces = []
            for d in range(8):
                depth, sx, sy = starts[d]
                a = ((16 * step + x) >> depth) - sx
                a = jnp.where((a >= 0) & (a < BLK), a, BLK)
                pieces.append(grads[d, a])
            wide_pieces.append(jnp.concatenate(pieces, axis=0).astype(BF))
        total = spectral + dot(place[...], jnp.concatenate(wide_pieces, axis=1))
        out[k] = (total[:, :C] + straight[80 * k : 80 * k + 80]).astype(BF)
        x = k + 8
        out[x] = (total[:, C:] + straight[80 * x : 80 * x + 80]).astype(BF)


def last_call(picks, pre, z, back, skip, gy, gx, u, g, tot):
    tile = pl.BlockSpec((16, SIDE, C), lambda n: (n, 0, 0))
    shape = jax.ShapeDtypeStruct
    return pl.pallas_call(
        last_kernel,
        grid=(5,),
        out_shape=(
            shape((SIDE, SIDE, C), BF),
            shape((2, 8, 4, C, C), F32),
            shape((C, C), F32),
            shape((8, C, C), F32),
            shape((C, H), F32),
            shape((H, C), F32),
        ),
        in_specs=[
            SM, tile, whole(64, 128, C), whole(8, 400, C), whole(C, C),
            whole(COLS, SIDE, 128), whole(ROWS, 160, 256), whole(4, 16, C), whole(4, 16, C),
            whole(TOT, C),
        ],
        out_specs=(
            tile,
            pl.BlockSpec((2, 8, 1, C, C), lambda n: (0, 0, jnp.minimum(n, 3), 0, 0)),
            whole(C, C),
            whole(8, C, C),
            whole(C, H),
            whole(H, C),
        ),
        scratch_shapes=[
            pltpu.VMEM((10, 128, 8, C), F32),
            pltpu.VMEM((640, 1024), BF),
            pltpu.VMEM((SIDE, 192), BF),
            pltpu.VMEM((8, BLK + 1, 24, C), F32),
            pltpu.VMEM((408, C), F32),
        ],
        compiler_params=pltpu.CompilerParams(vmem_limit_bytes=VMEM_LIMIT),
        name="field_gradient",
    )(picks, pre, z, back, skip, gy, gx, u, g, tot)


def shards(
    flow_field, cotangent, spec_weight, skip_weight, ctx_weight, up_weight, down_weight,
    ctx_level, ctx_offset,
):
    ty, gy, tx, gx = (jnp.asarray(t) for t in wave_tables())
    picks = ctx_level.T + (ctx_offset[:, :, 0].T << 2) + (ctx_offset[:, :, 1].T << 9)
    z, arrived, u, big = forward_call(picks, flow_field, ty, tx, spec_weight)
    layer, pre, z, back, g, tot = cells_call(
        flow_field, cotangent, z.reshape(64, 128, C), arrived, skip_weight, ctx_weight,
        up_weight, down_weight, gy, gx, tx, big, spec_weight,
    )
    grad, spec, skip, ctx, up, down = last_call(
        picks, pre, z.reshape(64, 128, C), back, skip_weight, gy, gx, u, g, tot.reshape(TOT, C)
    )
    return layer, grad, spec, skip, ctx, up, down


def solution(mesh):
    return jax.shard_map(
        shards,
        mesh=mesh,
        in_specs=(
            P("px", "py", None),
            P("px", "py", None),
            P(None, "px", "py", None, None),
            P(),
            P(),
            P(),
            P(),
            P(),
            P(),
        ),
        out_specs=(
            P("px", "py", None),
            P("px", "py", None),
            P(None, "px", "py", None, None),
            P(),
            P(),
            P(),
            P(),
        ),
        check_vma=False,
    )
```
